32 devices in a mesh: view: 2 (over core), gauss: 16 (over z, y, x).
Axes of the slice: x: 2, y: 2, z: 4, core: 2. Of those that a mesh axis runs over, the one named last changes fastest.
Arguments:
- entry_grads: bfloat16 [2, 59, 81920], P('view', None, 'gauss'), may hold values from -4 to 4
- vis_ids: int32 [2, 81920], P('view', 'gauss'), may hold values from 0 to 5119
- feats: bfloat16 [256, 16, 5120], P(None, 'gauss', 'view'), may hold values from -6 to 6
- code_tab: float32 [256, 8], replicated, may hold values from -4 to 4
- subj_ids: int32 [16, 5120], P('gauss', 'view'), may hold values from 0 to 7
- bone_ids: int32 [4, 16, 5120], P(None, 'gauss', 'view'), may hold values from 0 to 23
- skin_w: float32 [4, 16, 5120], P(None, 'gauss', 'view'), may hold values from 0.05 to 0.5
- canon_pos: float32 [3, 16, 5120], P(None, 'gauss', 'view'), may hold values from -5 to 5
- bone_tf: float32 [12, 192], replicated, may hold values from -4 to 4
- w_first: bfloat16 [256, 256], replicated, may hold values from -0.375 to 0.375
- w_second: bfloat16 [256, 256], replicated, may hold values from -0.375 to 0.375
- w_third: bfloat16 [256, 256], replicated, may hold values from -0.375 to 0.375
- biases: float32 [3, 256], replicated, may hold values from -3 to 3
- w_head: bfloat16 [3, 256], replicated, may hold values from -0.375 to 0.375
Outputs:
- attr_grads: float32 [59, 16, 5120], P(None, 'gauss', 'view')
- feat_grads: bfloat16 [256, 16, 5120], P(None, 'gauss', 'view')
- skin_grads: float32 [4, 16, 5120], P(None, 'gauss', 'view')
- first_grad: float32 [256, 256], replicated
- second_grad: float32 [256, 256], replicated
- third_grad: float32 [256, 256], replicated
- bias_grads: float32 [3, 256], replicated
- head_grad: float32 [3, 256], replicated
- code_grad: float32 [256, 8], replicated
- bone_grad: float32 [12, 192], replicated
The draws below stay inside these ranges and needn't reach their ends.
All inputs are finite; a program needn't handle non-finite values.
Results may differ from the reference program's by a relative error of at most 0.024.
Values may be sent and summed in bfloat16 or wider, within the bound.
No kernel may reach another device: no remote copies, remote signals or barrier semaphores. Data moves between devices by JAX's collectives and lax.ppermute only.
A program may use at most 128 MiB of HBM per device.

```python
import math
import jax
import jax.numpy as jnp
from jax import lax

ATTRS = 59
WIDTH = 256
BONES = 24
INFLUENCE = 4
SUBJECTS = 8
VIEWS = 2
SHARDS = 16
GAUSS_PER_PART = 5120
ENTRIES = 81920
GAUSSIANS = 81920


def plant(drawn, rng, least, largest):
    dims = drawn.shape
    spot = [jax.random.randint(jax.random.fold_in(rng, axis), (), 0, dims[axis]) for axis in range(len(dims))]
    drawn = drawn.at[tuple(spot)].set(least)
    longest = dims.index(max(dims))
    spot[longest] = (spot[longest] + 1) % dims[longest]
    return drawn.at[tuple(spot)].set(largest)


def steps_of(key, shape, pieces, low, high):
    level = 1.0
    for dim, blocks in pieces:
        steps = jax.random.uniform(jax.random.fold_in(jax.random.fold_in(key, 6), dim), (blocks,), jnp.float32, low / len(pieces), high / len(pieces))
        level = level * jnp.repeat(jnp.exp(steps), shape[dim] // blocks).reshape((-1,) + (1,) * (len(shape) - 1 - dim))
    return level


def bell_draw(stream_key, shape, deviation, reach, split=(), held_as=jnp.bfloat16):
    loudness = steps_of(stream_key, shape, split, -0.22, 0.18) if split else 1.0
    result = jax.random.normal(stream_key, shape, jnp.float32) * deviation * loudness
    return jnp.minimum(jnp.maximum(result, -reach), reach).astype(held_as)


def setup_inputs(seed: int = 0) -> dict:
    arg_keys = jax.random.split(jax.random.key(seed), 15)
    entry_grads = bell_draw(arg_keys[0], (VIEWS, ATTRS, ENTRIES), 0.5, 4.0, ((0, 2), (2, 16)))
    vis_ids = plant(jax.random.randint(arg_keys[1], (VIEWS, ENTRIES), 0, GAUSS_PER_PART), jax.random.fold_in(arg_keys[1], 1), 0, GAUSS_PER_PART - 1).astype(jnp.int32)
    feats = bell_draw(arg_keys[2], (WIDTH, SHARDS, GAUSS_PER_PART), 1.0, 6.0, ((1, 16), (2, 2)))
    code_tab = bell_draw(arg_keys[3], (WIDTH, SUBJECTS), 0.5, 4.0, (), jnp.float32)
    subj_ids = plant(jax.random.randint(arg_keys[4], (SHARDS, GAUSS_PER_PART), 0, SUBJECTS), jax.random.fold_in(arg_keys[4], 1), 0, SUBJECTS - 1).astype(jnp.int32)
    bone_ids = plant(jax.random.randint(arg_keys[5], (INFLUENCE, SHARDS, GAUSS_PER_PART), 0, BONES), jax.random.fold_in(arg_keys[5], 1), 0, BONES - 1).astype(jnp.int32)
    skin_w = jnp.clip(0.05 + 0.45 * jax.random.uniform(arg_keys[6], (INFLUENCE, SHARDS, GAUSS_PER_PART), jnp.float32) ** steps_of(arg_keys[6], (INFLUENCE, SHARDS, GAUSS_PER_PART), ((1, 16), (2, 2)), -0.2, 0.2), 0.05, 0.5)
    canon_pos = bell_draw(arg_keys[7], (3, SHARDS, GAUSS_PER_PART), 1.0, 5.0, ((1, 16), (2, 2)), jnp.float32)
    bone_tf = bell_draw(arg_keys[8], (12, SUBJECTS * BONES), 0.6, 4.0, (), jnp.float32)
    w_first = bell_draw(arg_keys[9], (WIDTH, WIDTH), WIDTH ** -0.5, 0.375)
    w_second = bell_draw(arg_keys[10], (WIDTH, WIDTH), WIDTH ** -0.5, 0.375)
    w_third = bell_draw(arg_keys[11], (WIDTH, WIDTH), WIDTH ** -0.5, 0.375)
    biases = bell_draw(arg_keys[12], (3, WIDTH), 0.5, 3.0, (), jnp.float32)
    w_head = bell_draw(arg_keys[13], (3, WIDTH), WIDTH ** -0.5, 0.375)
    return dict(entry_grads=entry_grads, vis_ids=vis_ids, feats=feats, code_tab=code_tab, subj_ids=subj_ids, bone_ids=bone_ids, skin_w=skin_w, canon_pos=canon_pos, bone_tf=bone_tf, w_first=w_first, w_second=w_second, w_third=w_third, biases=biases, w_head=w_head)


def dsilu(value):
    sig = jax.nn.sigmoid(value)
    return sig * (1.0 + value * (1.0 - sig))

def reference(entry_grads, vis_ids, feats, code_tab, subj_ids, bone_ids, skin_w, canon_pos, bone_tf, w_first, w_second, w_third, biases, w_head):
    table_cols = SUBJECTS * BONES

    def one_shard(carry, block_index):
        first_col = (block_index * GAUSS_PER_PART).astype(jnp.int32)
        values = lax.dynamic_slice_in_dim(entry_grads, first_col, GAUSS_PER_PART, 2)
        indices = lax.dynamic_slice_in_dim(vis_ids, first_col, GAUSS_PER_PART, 1)
        summed = jnp.zeros((ATTRS, GAUSS_PER_PART), jnp.float32)
        for viewer in range(VIEWS):
            partial_value = jnp.zeros((ATTRS, GAUSS_PER_PART), jnp.float32).at[:, indices[viewer]].add(values[viewer].astype(jnp.float32))
            rounded = lax.optimization_barrier(partial_value.astype(jnp.bfloat16))
            summed = summed + rounded.astype(jnp.float32)
        features = lax.dynamic_index_in_dim(feats, block_index, 1, keepdims=False)
        subject = lax.dynamic_index_in_dim(subj_ids, block_index, 0, keepdims=False)
        chosen = lax.dynamic_index_in_dim(bone_ids, block_index, 1, keepdims=False)
        skinning_weight = lax.dynamic_index_in_dim(skin_w, block_index, 1, keepdims=False)
        canon = lax.dynamic_index_in_dim(canon_pos, block_index, 1, keepdims=False)
        inputs = (features.astype(jnp.float32) + jnp.take(code_tab, subject, axis=1)).astype(jnp.bfloat16)
        pre_one = jnp.dot(w_first, inputs, preferred_element_type=jnp.float32) + biases[0][:, None]
        act_one = jax.nn.silu(pre_one).astype(jnp.bfloat16)
        pre_two = jnp.dot(w_second, act_one, preferred_element_type=jnp.float32) + biases[1][:, None]
        act_two = jax.nn.silu(pre_two).astype(jnp.bfloat16)
        pre_three = jnp.dot(w_third, act_two, preferred_element_type=jnp.float32) + biases[2][:, None]
        act_three = jax.nn.silu(pre_three).astype(jnp.bfloat16)
        shifted_point = canon + jnp.dot(w_head, act_three, preferred_element_type=jnp.float32)
        homogeneous_point = jnp.concatenate([shifted_point, jnp.ones((1, GAUSS_PER_PART), jnp.float32)], axis=0)
        position_gradient = summed[:3]
        shift_acc = jnp.zeros((3, GAUSS_PER_PART), jnp.float32)
        bone_acc = jnp.zeros((12, table_cols), jnp.float32)
        skins = []
        for member_flag in range(INFLUENCE):
            column = (subject * BONES + chosen[member_flag]).astype(jnp.int32)
            blend_matrix = jnp.take(bone_tf, column, axis=1).reshape(3, 4, GAUSS_PER_PART)
            posed_point = lax.optimization_barrier(jnp.sum(blend_matrix * homogeneous_point[None], axis=1))
            skins.append(lax.optimization_barrier(jnp.sum(position_gradient * posed_point, axis=0)))
            shift_acc = shift_acc + skinning_weight[member_flag] * lax.optimization_barrier(jnp.sum(blend_matrix[:, :3] * position_gradient[:, None], axis=0))
            contribution = ((skinning_weight[member_flag] * position_gradient)[:, None] * homogeneous_point[None]).reshape(12, GAUSS_PER_PART)
            bone_acc = bone_acc + jax.ops.segment_sum(contribution.T, column, num_segments=table_cols).T
        shift_grad = shift_acc.astype(jnp.bfloat16)
        head = jnp.dot(shift_grad, act_three.T, preferred_element_type=jnp.float32)
        back_three = (jnp.dot(w_head.T, shift_grad, preferred_element_type=jnp.float32) * dsilu(pre_three)).astype(jnp.bfloat16)
        third = jnp.dot(back_three, act_two.T, preferred_element_type=jnp.float32)
        back_two = (jnp.dot(w_third.T, back_three, preferred_element_type=jnp.float32) * dsilu(pre_two)).astype(jnp.bfloat16)
        second = jnp.dot(back_two, act_one.T, preferred_element_type=jnp.float32)
        back_one = (jnp.dot(w_second.T, back_two, preferred_element_type=jnp.float32) * dsilu(pre_one)).astype(jnp.bfloat16)
        first = jnp.dot(back_one, inputs.T, preferred_element_type=jnp.float32)
        bias_rows = jnp.stack([lax.optimization_barrier(jnp.sum(back_one.astype(jnp.float32), axis=1)), lax.optimization_barrier(jnp.sum(back_two.astype(jnp.float32), axis=1)), lax.optimization_barrier(jnp.sum(back_three.astype(jnp.float32), axis=1))])
        input_grad = jnp.dot(w_first.T, back_one, preferred_element_type=jnp.float32)
        code = jax.ops.segment_sum(input_grad.T, subject.astype(jnp.int32), num_segments=SUBJECTS).T
        sums = (first, second, third, bias_rows, head, code, bone_acc)
        carry = tuple((old + new for old, new in zip(carry, sums)))
        return (carry, (summed, input_grad.astype(jnp.bfloat16), jnp.stack(skins)))
    start = (jnp.zeros((WIDTH, WIDTH), jnp.float32), jnp.zeros((WIDTH, WIDTH), jnp.float32), jnp.zeros((WIDTH, WIDTH), jnp.float32), jnp.zeros((3, WIDTH), jnp.float32), jnp.zeros((3, WIDTH), jnp.float32), jnp.zeros((WIDTH, SUBJECTS), jnp.float32), jnp.zeros((12, table_cols), jnp.float32))
    totals, stacked = lax.scan(one_shard, start, jnp.arange(SHARDS, dtype=jnp.int32))
    factor = 1.0 / math.sqrt(GAUSSIANS)
    first, second, third, bias_rows, head, code, bone_acc = [factor * value for value in totals]
    attr_grads = jnp.transpose(stacked[0], (1, 0, 2))
    feat_grads = jnp.transpose(stacked[1], (1, 0, 2))
    skin_grads = jnp.transpose(stacked[2], (1, 0, 2))
    return (attr_grads, feat_grads, skin_grads, first, second, third, bias_rows, head, code, bone_acc)
```

```python
import functools
import math

import jax
import jax.numpy as jnp
from jax import lax
from jax.experimental import pallas as pl
from jax.experimental.pallas import tpu as pltpu
from jax.sharding import PartitionSpec as P

F32 = jnp.float32
BF16 = jnp.bfloat16
AXES = ("view", "gauss")
LOW = 256
GROUP = 16
NT = (((1,), (1,)), ((), ()))
TN = (((0,), (0,)), ((), ()))
VMEM = pl.BlockSpec(memory_space=pltpu.VMEM)
SMEM = pl.BlockSpec(memory_space=pltpu.SMEM)


def params():
    return pltpu.CompilerParams(vmem_limit_bytes=48 * 1024 * 1024)


def mm(left, right, dims=(((1,), (0,)), ((), ()))):
    return lax.dot_general(left, right, dims, preferred_element_type=F32)


def divisor(total, choices):
    for choice in choices:
        if total % choice == 0:
            return choice
    return total


def scatter_kernel(first_row, rows, viewers, view_ref, grads_ref, ids_ref, out_ref, acc_ref):
    entries = ids_ref.shape[1]
    blocks = acc_ref.shape[0]
    groups = acc_ref.shape[1] // GROUP
    step = divisor(entries, (1024, 512, 256, 128))
    low_rows = lax.broadcasted_iota(jnp.int32, (LOW, step), 0).astype(F32).astype(BF16)
    one = jnp.ones((), BF16)
    zero = jnp.zeros((), BF16)

    acc_ref[...] = jnp.zeros_like(acc_ref)

    def chunk(index, carry):
        spot = pl.ds(pl.multiple_of(index * step, step), step)
        ids = ids_ref[0:1, spot]
        high = lax.shift_right_logical(ids, 8).astype(F32).astype(BF16)
        low = lax.bitwise_and(ids, LOW - 1).astype(F32).astype(BF16)
        hot = jnp.where(low_rows == low, one, zero)
        values = []
        for group in range(groups):
            begin = first_row + group * GROUP
            count = min(GROUP, first_row + rows - begin)
            piece = grads_ref[0, begin : begin + count, spot]
            if count < GROUP:
                piece = jnp.concatenate(
                    [piece.astype(F32), jnp.zeros((GROUP - count, step), F32)], axis=0
                ).astype(BF16)
            values.append(piece)
        high = jnp.broadcast_to(high, (GROUP, step))
        for block in range(blocks):
            inside = high == jnp.asarray(block, BF16)
            left = jnp.concatenate([jnp.where(inside, v, zero) for v in values], axis=0)
            acc_ref[block] += mm(left, hot, NT)
        return carry

    lax.fori_loop(0, entries // step, chunk, 0)
    per = blocks // viewers
    for block in range(blocks):
        slot = lax.rem(block // per - view_ref[0] + viewers, viewers)
        out_ref[slot, :, (block % per) * LOW : (block % per + 1) * LOW] = acc_ref[block].astype(BF16)


def scatter(view, entry_grads, vis_ids, first_row, rows, members, viewers):
    groups = -(-rows // GROUP)
    blocks = members * viewers // LOW
    return pl.pallas_call(
        functools.partial(scatter_kernel, first_row, rows, viewers),
        out_shape=jax.ShapeDtypeStruct((viewers, groups * GROUP, members), BF16),
        in_specs=[SMEM, VMEM, VMEM],
        out_specs=VMEM,
        scratch_shapes=[pltpu.VMEM((blocks, groups * GROUP, LOW), F32)],
        compiler_params=params(),
    )(view, entry_grads, vis_ids)


def network_kernel(
    factor,
    side_ref,
    pos_ref,
    feats_ref,
    code_ref,
    subj_ref,
    bone_ids_ref,
    skin_ref,
    canon_ref,
    table_ref,
    first_ref,
    second_ref,
    third_ref,
    bias_ref,
    head_ref,
    feat_out,
    skin_out,
    mine_out,
    theirs_out,
    head_s,
    bias_s,
    table_s,
    total_s,
    sums_s,
    hots_s,
    x_s,
    act_s,
    slope_s,
    back_s,
):
    width, members = feats_ref.shape
    subjects = code_ref.shape[0]
    table_cols = table_ref.shape[1]
    per_subject = table_cols // subjects
    influence = bone_ids_ref.shape[0]
    half = mine_out.shape[0]
    step = divisor(members, (512, 256, 128))

    head_s[...] = jnp.zeros_like(head_s)
    head_s[0:3, :] = head_ref[...].astype(F32)
    head_w = head_s[...].astype(BF16)
    bias_s[...] = jnp.zeros_like(bias_s)
    bias_s[0:3, :] = bias_ref[...]
    bias_cols = bias_s[...].T
    table = table_ref[...]
    table_hi = table.astype(BF16).astype(F32)
    table_s[...] = jnp.zeros_like(table_s)
    table_s[0:12, :] = table_hi
    table_s[16:28, :] = table - table_hi
    table_w = table_s[...].astype(BF16)
    code = code_ref[...]
    code_hi = code.astype(BF16).astype(F32)
    code_mid = (code - code_hi).astype(BF16).astype(F32)
    code_lo = code - code_hi - code_mid
    code_w = jnp.concatenate([code_hi, code_mid, code_lo], axis=0).T.astype(BF16)
    total_s[...] = jnp.zeros_like(total_s)
    sums_s[...] = jnp.zeros_like(sums_s)
    hot_rows = lax.broadcasted_iota(jnp.int32, (3 * subjects, step), 0) % subjects
    table_rows = lax.broadcasted_iota(jnp.int32, (table_cols, step), 0).astype(F32).astype(BF16)
    entry_rows = lax.broadcasted_iota(jnp.int32, (16, step), 0)
    one = jnp.ones((), BF16)
    zero = jnp.zeros((), BF16)

    def lane_sums(slot, value):
        total = value[:, 0:128]
        for lane in range(128, value.shape[1], 128):
            total = total + value[:, lane : lane + 128]
        sums_s[slot] += total

    def chunk(index, carry):
        spot = pl.ds(pl.multiple_of(index * step, step), step)
        subject = subj_ref[0:1, spot]
        hot = (hot_rows == subject).astype(F32).astype(BF16)
        x = (feats_ref[:, spot].astype(F32) + mm(code_w, hot)).astype(BF16)
        x_s[:, spot] = x
        hots_s[:, spot] = hot[0:16]
        act = x
        for layer, weight in enumerate((first_ref, second_ref, third_ref)):
            pre = mm(weight[...], act) + bias_cols[:, layer : layer + 1]
            sig = 0.5 * jnp.tanh(0.5 * pre) + 0.5
            value = pre * sig
            slope_s[layer, :, :] = sig + value * (1.0 - sig)
            act = value.astype(BF16)
            act_s[layer, :, spot] = act
        moved = mm(head_w, act)
        point = [canon_ref[axis, :, spot] + moved[axis : axis + 1] for axis in range(3)]
        grad = pos_ref[0, :, spot].astype(F32)
        for slot in range(1, pos_ref.shape[0]):
            grad = grad + pos_ref[slot, :, spot].astype(F32)
        quarter = entry_rows // 4
        place = entry_rows % 4
        grad_rows = jnp.where(
            quarter == 0,
            grad[0:1],
            jnp.where(quarter == 1, grad[1:2], jnp.where(quarter == 2, grad[2:3], 0.0)),
        )
        point_rows = jnp.where(
            place == 0, point[0], jnp.where(place == 1, point[1], jnp.where(place == 2, point[2], 1.0))
        )
        outer = grad_rows * point_rows
        blend = jnp.zeros((16, step), F32)
        bones = jnp.zeros((32, table_cols), F32)
        for member in range(influence):
            column = (subject * per_subject + bone_ids_ref[member, :, spot]).astype(F32).astype(BF16)
            onehot = jnp.where(table_rows == column, one, zero)
            both = mm(table_w, onehot)
            matrix = both[0:16] + both[16:32]
            skin_out[member, :, spot] = jnp.sum(outer * matrix, axis=0, keepdims=True)
            weight = skin_ref[member, :, spot]
            blend = blend + weight * matrix
            share = weight * outer
            share_hi = share.astype(BF16).astype(F32)
            parts = jnp.concatenate([share_hi, share - share_hi], axis=0).astype(BF16)
            bones = bones + mm(parts, onehot, NT)
        total_s[2 * half - 16 : 2 * half, 0:table_cols] += bones[0:16] + bones[16:32]
        pulled = blend * grad_rows
        shift = pulled[0:4] + pulled[4:8] + pulled[8:12]
        shift = jnp.where(entry_rows[0:4] < 3, shift, 0.0)
        shift = jnp.concatenate([shift, jnp.zeros((12, step), F32)], axis=0).astype(BF16)
        total_s[half - 16 : half, :] += mm(shift, act, NT)
        back = mm(head_w, shift, TN) * slope_s[2, :, :]
        lane_sums(2, back)
        back = back.astype(BF16)
        back_s[2, :, spot] = back
        back = mm(third_ref[...], back, TN) * slope_s[1, :, :]
        lane_sums(1, back)
        back = back.astype(BF16)
        back_s[1, :, spot] = back
        back = mm(second_ref[...], back, TN) * slope_s[0, :, :]
        back = back.astype(BF16)
        back_s[0, :, spot] = back
        feat_out[:, spot] = mm(first_ref[...], back, TN).astype(BF16)
        return carry

    lax.fori_loop(0, members // step, chunk, 0)
    total_s[0:width, :] = mm(back_s[2], act_s[1], NT)
    second = mm(back_s[1], act_s[0], NT)
    total_s[width : half - 16, :] = second[0 : width // 2]
    total_s[half : half + width // 2, :] = second[width // 2 :]
    total_s[half + width // 2 : 2 * half - 16, :] = mm(back_s[0], x_s[...], NT)
    by_subject = mm(back_s[0], hots_s[...], NT)[:, 0:subjects]
    by_hi = by_subject.astype(BF16).astype(F32)
    by_mid = (by_subject - by_hi).astype(BF16).astype(F32)
    by_lo = by_subject - by_hi - by_mid
    code_total = (
        mm(first_ref[...], by_hi.astype(BF16), TN)
        + mm(first_ref[...], by_mid.astype(BF16), TN)
        + mm(first_ref[...], by_lo.astype(BF16), TN)
    )
    bias_one = jnp.sum(by_subject, axis=1, keepdims=True)
    bias_two = jnp.sum(sums_s[1], axis=1, keepdims=True)
    bias_three = jnp.sum(sums_s[2], axis=1, keepdims=True)
    tail = jnp.concatenate(
        [code_total, bias_one, bias_two, bias_three, jnp.zeros((width, 128 - subjects - 3), F32)], axis=1
    ).T
    total_s[half - 16 + 3 : half - 16 + 6, :] = tail[subjects : subjects + 3]
    total_s[half - 8 : half, :] = tail[0:subjects]
    side = side_ref[0]
    mine_out[...] = (total_s[pl.ds(pl.multiple_of(side * half, 16), half), :] * factor).astype(BF16)
    theirs_out[...] = (total_s[pl.ds(pl.multiple_of((1 - side) * half, 16), half), :] * factor).astype(BF16)


def network(side, position, feats, code, subj, bone_ids, skin, canon, table, w1, w2, w3, bias, head, factor):
    width, members = feats.shape
    half = width + width // 2 + 16
    influence = bone_ids.shape[0]
    table_cols = table.shape[1]
    step = divisor(members, (512, 256, 128))
    return pl.pallas_call(
        functools.partial(network_kernel, factor),
        out_shape=(
            jax.ShapeDtypeStruct((width, members), BF16),
            jax.ShapeDtypeStruct((influence, 1, members), F32),
            jax.ShapeDtypeStruct((half, width), BF16),
            jax.ShapeDtypeStruct((half, width), BF16),
        ),
        in_specs=[SMEM] + [VMEM] * 13,
        out_specs=(VMEM,) * 4,
        scratch_shapes=[
            pltpu.VMEM((16, width), F32),
            pltpu.VMEM((8, width), F32),
            pltpu.VMEM((32, table_cols), F32),
            pltpu.VMEM((2 * half, width), F32),
            pltpu.VMEM((3, width, 128), F32),
            pltpu.VMEM((16, members), BF16),
            pltpu.VMEM((width, members), BF16),
            pltpu.VMEM((3, width, members), BF16),
            pltpu.VMEM((3, width, step), F32),
            pltpu.VMEM((3, width, members), BF16),
        ],
        compiler_params=params(),
    )(side, position, feats, code, subj, bone_ids, skin, canon, table, w1, w2, w3, bias, head)


def finish_kernel(side_ref, mine_ref, theirs_ref, first_out, second_out, third_out, bias_out, head_out, code_out, bone_out):
    width = first_out.shape[0]
    half = mine_ref.shape[0]
    subjects = code_out.shape[0]
    table_cols = bone_out.shape[1]

    def write(top, bottom):
        third_out[...] = top[0:width, :].astype(F32)
        second_out[0 : width // 2, :] = top[width : half - 16, :].astype(F32)
        second_out[width // 2 :, :] = bottom[0 : width // 2, :].astype(F32)
        first_out[...] = bottom[width // 2 : half - 16, :].astype(F32)
        small = top[half - 16 : half, :].astype(F32)
        head_out[...] = small[0:3]
        bias_out[...] = small[3:6]
        code_out[...] = small[8 : 8 + subjects]
        bone_out[...] = bottom[half - 16 : half, :].astype(F32)[0:12, 0:table_cols]

    @pl.when(side_ref[0] == 0)
    def _():
        write(mine_ref, theirs_ref)

    @pl.when(side_ref[0] != 0)
    def _():
        write(theirs_ref, mine_ref)


def finish(side, mine, theirs, width, subjects, table_cols):
    square = jax.ShapeDtypeStruct((width, width), F32)
    rows = jax.ShapeDtypeStruct((3, width), F32)
    return pl.pallas_call(
        finish_kernel,
        out_shape=(
            square,
            square,
            square,
            rows,
            rows,
            jax.ShapeDtypeStruct((subjects, width), F32),
            jax.ShapeDtypeStruct((12, table_cols), F32),
        ),
        in_specs=[SMEM, VMEM, VMEM],
        out_specs=(VMEM,) * 7,
        compiler_params=params(),
    )(side, mine, theirs)


def add(left, right):
    return (left.astype(F32) + right.astype(F32)).astype(BF16)


def swap(value, mask, count):
    return lax.ppermute(value, AXES, [(place, place ^ mask) for place in range(count)])


def sum_over_devices(mine, theirs, viewers, shards):
    count = viewers * shards
    pair = shards
    mine = add(mine, swap(theirs, pair, count))
    masks = []
    mask = 1
    while mask < count:
        if mask != pair:
            masks.append(mask)
        mask *= 2
    shift = len(masks) // 2
    rows = mine.shape[0]
    cut = rows // 32 * 16
    parts = [mine[:cut], mine[cut:]]
    orders = [masks, masks[shift:] + masks[:shift]]
    for stage in range(len(masks)):
        got = [swap(part, order[stage], count) for part, order in zip(parts, orders)]
        parts = [add(part, other) for part, other in zip(parts, got)]
    mine = jnp.concatenate(parts, axis=0)
    return mine, swap(mine, pair, count)


def to_owner(parts, viewers):
    got = [parts[0]]
    for away in range(1, viewers):
        perm = [(place, (place + away) % viewers) for place in range(viewers)]
        got.append(lax.ppermute(parts[away], "view", perm))
    return jnp.stack(got)


def body(
    entry_grads,
    vis_ids,
    feats,
    code_tab,
    subj_ids,
    bone_ids,
    skin_w,
    canon_pos,
    bone_tf,
    w_first,
    w_second,
    w_third,
    biases,
    w_head,
):
    width, _, members = feats.shape
    viewers = lax.axis_size("view")
    shards = lax.axis_size("gauss")
    attrs = entry_grads.shape[1]
    factor = 1.0 / math.sqrt(members * viewers * shards)
    view = lax.axis_index("view").astype(jnp.int32).reshape(1)
    side = view % 2
    position = scatter(view, entry_grads, vis_ids, 0, GROUP, members, viewers)
    position = to_owner(position, viewers)
    others = scatter(view, entry_grads, vis_ids, GROUP, attrs - GROUP, members, viewers)
    others = to_owner(others, viewers)
    feat_grads, skin_grads, mine, theirs = network(
        side,
        position,
        feats[:, 0],
        code_tab.T,
        subj_ids,
        bone_ids,
        skin_w,
        canon_pos,
        bone_tf,
        w_first,
        w_second,
        w_third,
        biases,
        w_head,
        factor,
    )
    mine, theirs = sum_over_devices(mine, theirs, viewers, shards)
    first, second, third, bias, head, code, bone = finish(
        side, mine, theirs, width, code_tab.shape[1], bone_tf.shape[1]
    )
    attr = jnp.concatenate(
        [jnp.sum(position.astype(F32), axis=0), jnp.sum(others.astype(F32), axis=0)[: attrs - GROUP]], axis=0
    )
    return (
        attr[:, None, :],
        feat_grads[:, None, :],
        skin_grads,
        first,
        second,
        third,
        bias,
        head,
        code.T,
        bone,
    )


def solution(mesh):
    placed = (
        P("view", None, "gauss"),
        P("view", "gauss"),
        P(None, "gauss", "view"),
        P(),
        P("gauss", "view"),
        P(None, "gauss", "view"),
        P(None, "gauss", "view"),
        P(None, "gauss", "view"),
        P(),
        P(),
        P(),
        P(),
        P(),
        P(),
    )
    return jax.shard_map(
        body,
        mesh=mesh,
        in_specs=placed,
        out_specs=(
            P(None, "gauss", "view"),
            P(None, "gauss", "view"),
            P(None, "gauss", "view"),
            P(),
            P(),
            P(),
            P(),
            P(),
            P(),
            P(),
        ),
        check_vma=False,
    )
```

```python
import functools
import math

import jax
import jax.numpy as jnp
from jax import lax
from jax.experimental import pallas as pl
from jax.experimental.pallas import tpu as pltpu
from jax.sharding import PartitionSpec as P

F32 = jnp.float32
BF16 = jnp.bfloat16
AXES = ("view", "gauss")
LOW = 256
GROUP = 16
NT = (((1,), (1,)), ((), ()))
TN = (((0,), (0,)), ((), ()))
VMEM = pl.BlockSpec(memory_space=pltpu.VMEM)
SMEM = pl.BlockSpec(memory_space=pltpu.SMEM)


def params():
    return pltpu.CompilerParams(vmem_limit_bytes=48 * 1024 * 1024)


def mm(left, right, dims=(((1,), (0,)), ((), ()))):
    return lax.dot_general(left, right, dims, preferred_element_type=F32)


def divisor(total, choices):
    for choice in choices:
        if total % choice == 0:
            return choice
    return total


def scatter_kernel(first_row, rows, viewers, view_ref, grads_ref, ids_ref, out_ref, acc_ref, left_ref):
    entries = ids_ref.shape[1]
    step = left_ref.shape[1]
    height = out_ref.shape[1]
    blocks = acc_ref.shape[0] // height
    groups = height // GROUP
    low_rows = lax.broadcasted_iota(jnp.int32, (LOW, step), 0).astype(F32).astype(BF16)
    one = jnp.ones((), BF16)
    zero = jnp.zeros((), BF16)

    def chunk(index, carry):
        spot = pl.ds(pl.multiple_of(index * step, step), step)
        ids = ids_ref[0:1, spot]
        high = lax.shift_right_logical(ids, 8).astype(F32).astype(BF16)
        low = lax.bitwise_and(ids, LOW - 1).astype(F32).astype(BF16)
        hot = jnp.where(low_rows == low, one, zero)
        high = jnp.broadcast_to(high, (GROUP, step))
        for group in range(groups):
            begin = first_row + group * GROUP
            count = min(GROUP, first_row + rows - begin)
            piece = grads_ref[0, begin : begin + count, spot]
            if count < GROUP:
                piece = jnp.concatenate(
                    [piece.astype(F32), jnp.zeros((GROUP - count, step), F32)], axis=0
                ).astype(BF16)
            for block in range(blocks):
                place = block * height + group * GROUP
                left_ref[place : place + GROUP, :] = jnp.where(high == jnp.asarray(block, BF16), piece, zero)
        product = mm(left_ref[...], hot, NT)

        @pl.when(index == 0)
        def _():
            acc_ref[...] = product

        @pl.when(index != 0)
        def _():
            acc_ref[...] += product

        return carry

    lax.fori_loop(0, entries // step, chunk, 0)
    per = blocks // viewers
    for block in range(blocks):
        slot = lax.rem(block // per - view_ref[0] + viewers, viewers)
        out_ref[slot, :, (block % per) * LOW : (block % per + 1) * LOW] = acc_ref[
            block * height : (block + 1) * height, :
        ].astype(BF16)


def scatter(view, entry_grads, vis_ids, first_row, rows, members, viewers):
    height = -(-rows // GROUP) * GROUP
    blocks = members * viewers // LOW
    step = divisor(vis_ids.shape[1], (2560, 2048, 1024, 512, 256, 128))
    return pl.pallas_call(
        functools.partial(scatter_kernel, first_row, rows, viewers),
        out_shape=jax.ShapeDtypeStruct((viewers, height, members), BF16),
        in_specs=[SMEM, VMEM, VMEM],
        out_specs=VMEM,
        scratch_shapes=[pltpu.VMEM((blocks * height, LOW), F32), pltpu.VMEM((blocks * height, step), BF16)],
        compiler_params=params(),
    )(view, entry_grads, vis_ids)


def network_kernel(
    factor,
    side_ref,
    pos_ref,
    feats_ref,
    code_ref,
    subj_ref,
    bone_ids_ref,
    skin_ref,
    canon_ref,
    table_ref,
    first_ref,
    second_ref,
    third_ref,
    bias_ref,
    head_ref,
    feat_out,
    skin_out,
    mine_out,
    theirs_out,
    head_s,
    bias_s,
    table_s,
    total_s,
    sums_s,
    hots_s,
    x_s,
    act_s,
    slope_s,
    back_s,
):
    width, members = feats_ref.shape
    subjects = code_ref.shape[0]
    table_cols = table_ref.shape[1]
    per_subject = table_cols // subjects
    influence = bone_ids_ref.shape[0]
    half = mine_out.shape[0]
    step = divisor(members, (512, 256, 128))

    head_s[...] = jnp.zeros_like(head_s)
    head_s[0:3, :] = head_ref[...].astype(F32)
    head_w = head_s[...].astype(BF16)
    bias_s[...] = jnp.zeros_like(bias_s)
    bias_s[0:3, :] = bias_ref[...]
    bias_cols = bias_s[...].T
    table = table_ref[...]
    table_hi = table.astype(BF16).astype(F32)
    table_s[...] = jnp.zeros_like(table_s)
    table_s[0:12, :] = table_hi
    table_s[16:28, :] = table - table_hi
    table_w = table_s[...].astype(BF16)
    code = code_ref[...]
    code_hi = code.astype(BF16).astype(F32)
    code_mid = (code - code_hi).astype(BF16).astype(F32)
    code_lo = code - code_hi - code_mid
    code_w = jnp.concatenate([code_hi, code_mid, code_lo], axis=0).T.astype(BF16)
    total_s[...] = jnp.zeros_like(total_s)
    sums_s[...] = jnp.zeros_like(sums_s)
    hot_rows = lax.broadcasted_iota(jnp.int32, (3 * subjects, step), 0) % subjects
    table_rows = lax.broadcasted_iota(jnp.int32, (table_cols, step), 0).astype(F32).astype(BF16)
    entry_rows = lax.broadcasted_iota(jnp.int32, (16, step), 0)
    one = jnp.ones((), BF16)
    zero = jnp.zeros((), BF16)

    def lane_sums(slot, value):
        total = value[:, 0:128]
        for lane in range(128, value.shape[1], 128):
            total = total + value[:, lane : lane + 128]
        sums_s[slot] += total

    def chunk(index, carry):
        spot = pl.ds(pl.multiple_of(index * step, step), step)
        subject = subj_ref[0:1, spot]
        hot = (hot_rows == subject).astype(F32).astype(BF16)
        x = (feats_ref[:, spot].astype(F32) + mm(code_w, hot)).astype(BF16)
        x_s[:, spot] = x
        hots_s[:, spot] = hot[0:16]
        act = x
        for layer, weight in enumerate((first_ref, second_ref, third_ref)):
            pre = mm(weight[...], act) + bias_cols[:, layer : layer + 1]
            sig = 0.5 * jnp.tanh(0.5 * pre) + 0.5
            value = pre * sig
            slope_s[layer, :, :] = sig + value * (1.0 - sig)
            act = value.astype(BF16)
            act_s[layer, :, spot] = act
        moved = mm(head_w, act)
        point = [canon_ref[axis, :, spot] + moved[axis : axis + 1] for axis in range(3)]
        grad = pos_ref[0, :, spot].astype(F32)
        for slot in range(1, pos_ref.shape[0]):
            grad = grad + pos_ref[slot, :, spot].astype(F32)
        quarter = entry_rows // 4
        place = entry_rows % 4
        grad_rows = jnp.where(
            quarter == 0,
            grad[0:1],
            jnp.where(quarter == 1, grad[1:2], jnp.where(quarter == 2, grad[2:3], 0.0)),
        )
        point_rows = jnp.where(
            place == 0, point[0], jnp.where(place == 1, point[1], jnp.where(place == 2, point[2], 1.0))
        )
        outer = grad_rows * point_rows
        blend = jnp.zeros((16, step), F32)
        bones = jnp.zeros((32, table_cols), F32)
        for member in range(influence):
            column = (subject * per_subject + bone_ids_ref[member, :, spot]).astype(F32).astype(BF16)
            onehot = jnp.where(table_rows == column, one, zero)
            both = mm(table_w, onehot)
            matrix = both[0:16] + both[16:32]
            skin_out[member, :, spot] = jnp.sum(outer * matrix, axis=0, keepdims=True)
            weight = skin_ref[member, :, spot]
            blend = blend + weight * matrix
            share = weight * outer
            share_hi = share.astype(BF16).astype(F32)
            parts = jnp.concatenate([share_hi, share - share_hi], axis=0).astype(BF16)
            bones = bones + mm(parts, onehot, NT)
        total_s[2 * half - 16 : 2 * half, 0:table_cols] += bones[0:16] + bones[16:32]
        pulled = blend * grad_rows
        shift = pulled[0:4] + pulled[4:8] + pulled[8:12]
        shift = jnp.where(entry_rows[0:4] < 3, shift, 0.0)
        shift = jnp.concatenate([shift, jnp.zeros((12, step), F32)], axis=0).astype(BF16)
        total_s[half - 16 : half, :] += mm(shift, act, NT)
        back = mm(head_w, shift, TN) * slope_s[2, :, :]
        lane_sums(2, back)
        back = back.astype(BF16)
        back_s[2, :, spot] = back
        back = mm(third_ref[...], back, TN) * slope_s[1, :, :]
        lane_sums(1, back)
        back = back.astype(BF16)
        back_s[1, :, spot] = back
        back = mm(second_ref[...], back, TN) * slope_s[0, :, :]
        back = back.astype(BF16)
        back_s[0, :, spot] = back
        feat_out[:, spot] = mm(first_ref[...], back, TN).astype(BF16)
        return carry

    lax.fori_loop(0, members // step, chunk, 0)
    total_s[0:width, :] = mm(back_s[2], act_s[1], NT)
    second = mm(back_s[1], act_s[0], NT)
    total_s[width : half - 16, :] = second[0 : width // 2]
    total_s[half : half + width // 2, :] = second[width // 2 :]
    total_s[half + width // 2 : 2 * half - 16, :] = mm(back_s[0], x_s[...], NT)
    by_subject = mm(back_s[0], hots_s[...], NT)[:, 0:subjects]
    by_hi = by_subject.astype(BF16).astype(F32)
    by_mid = (by_subject - by_hi).astype(BF16).astype(F32)
    by_lo = by_subject - by_hi - by_mid
    code_total = (
        mm(first_ref[...], by_hi.astype(BF16), TN)
        + mm(first_ref[...], by_mid.astype(BF16), TN)
        + mm(first_ref[...], by_lo.astype(BF16), TN)
    )
    bias_one = jnp.sum(by_subject, axis=1, keepdims=True)
    bias_two = jnp.sum(sums_s[1], axis=1, keepdims=True)
    bias_three = jnp.sum(sums_s[2], axis=1, keepdims=True)
    tail = jnp.concatenate(
        [code_total, bias_one, bias_two, bias_three, jnp.zeros((width, 128 - subjects - 3), F32)], axis=1
    ).T
    total_s[half - 16 + 3 : half - 16 + 6, :] = tail[subjects : subjects + 3]
    total_s[half - 8 : half, :] = tail[0:subjects]
    side = side_ref[0]
    mine_out[...] = (total_s[pl.ds(pl.multiple_of(side * half, 16), half), :] * factor).astype(BF16)
    theirs_out[...] = (total_s[pl.ds(pl.multiple_of((1 - side) * half, 16), half), :] * factor).astype(BF16)


def network(side, position, feats, code, subj, bone_ids, skin, canon, table, w1, w2, w3, bias, head, factor):
    width, members = feats.shape
    half = width + width // 2 + 16
    influence = bone_ids.shape[0]
    table_cols = table.shape[1]
    step = divisor(members, (512, 256, 128))
    return pl.pallas_call(
        functools.partial(network_kernel, factor),
        out_shape=(
            jax.ShapeDtypeStruct((width, members), BF16),
            jax.ShapeDtypeStruct((influence, 1, members), F32),
            jax.ShapeDtypeStruct((half, width), BF16),
            jax.ShapeDtypeStruct((half, width), BF16),
        ),
        in_specs=[SMEM] + [VMEM] * 13,
        out_specs=(VMEM,) * 4,
        scratch_shapes=[
            pltpu.VMEM((16, width), F32),
            pltpu.VMEM((8, width), F32),
            pltpu.VMEM((32, table_cols), F32),
            pltpu.VMEM((2 * half, width), F32),
            pltpu.VMEM((3, width, 128), F32),
            pltpu.VMEM((16, members), BF16),
            pltpu.VMEM((width, members), BF16),
            pltpu.VMEM((3, width, members), BF16),
            pltpu.VMEM((3, width, step), F32),
            pltpu.VMEM((3, width, members), BF16),
        ],
        compiler_params=params(),
    )(side, position, feats, code, subj, bone_ids, skin, canon, table, w1, w2, w3, bias, head)


def finish_kernel(side_ref, mine_ref, theirs_ref, first_out, second_out, third_out, bias_out, head_out, code_out, bone_out):
    width = first_out.shape[0]
    half = mine_ref.shape[0]
    subjects = code_out.shape[0]
    table_cols = bone_out.shape[1]

    def write(top, bottom):
        third_out[...] = top[0:width, :].astype(F32)
        second_out[0 : width // 2, :] = top[width : half - 16, :].astype(F32)
        second_out[width // 2 :, :] = bottom[0 : width // 2, :].astype(F32)
        first_out[...] = bottom[width // 2 : half - 16, :].astype(F32)
        small = top[half - 16 : half, :].astype(F32)
        head_out[...] = small[0:3]
        bias_out[...] = small[3:6]
        code_out[...] = small[8 : 8 + subjects]
        bone_out[...] = bottom[half - 16 : half, :].astype(F32)[0:12, 0:table_cols]

    @pl.when(side_ref[0] == 0)
    def _():
        write(mine_ref, theirs_ref)

    @pl.when(side_ref[0] != 0)
    def _():
        write(theirs_ref, mine_ref)


def finish(side, mine, theirs, width, subjects, table_cols):
    square = jax.ShapeDtypeStruct((width, width), F32)
    rows = jax.ShapeDtypeStruct((3, width), F32)
    return pl.pallas_call(
        finish_kernel,
        out_shape=(
            square,
            square,
            square,
            rows,
            rows,
            jax.ShapeDtypeStruct((subjects, width), F32),
            jax.ShapeDtypeStruct((12, table_cols), F32),
        ),
        in_specs=[SMEM, VMEM, VMEM],
        out_specs=(VMEM,) * 7,
        compiler_params=params(),
    )(side, mine, theirs)


def add(left, right):
    return (left.astype(F32) + right.astype(F32)).astype(BF16)


def swap(value, mask, count):
    return lax.ppermute(value, AXES, [(place, place ^ mask) for place in range(count)])


def sum_over_devices(mine, theirs, viewers, shards):
    count = viewers * shards
    pair = shards
    mine = add(mine, swap(theirs, pair, count))
    masks = []
    mask = 1
    while mask < count:
        if mask != pair:
            masks.append(mask)
        mask *= 2
    shift = len(masks) // 2
    rows = mine.shape[0]
    cut = rows // 32 * 16
    parts = [mine[:cut], mine[cut:]]
    orders = [masks, masks[shift:] + masks[:shift]]
    for stage in range(len(masks)):
        got = [swap(part, order[stage], count) for part, order in zip(parts, orders)]
        parts = [add(part, other) for part, other in zip(parts, got)]
    mine = jnp.concatenate(parts, axis=0)
    return mine, swap(mine, pair, count)


def to_owner(parts, viewers):
    got = [parts[0]]
    for away in range(1, viewers):
        perm = [(place, (place + away) % viewers) for place in range(viewers)]
        got.append(lax.ppermute(parts[away], "view", perm))
    return jnp.stack(got)


def body(
    entry_grads,
    vis_ids,
    feats,
    code_tab,
    subj_ids,
    bone_ids,
    skin_w,
    canon_pos,
    bone_tf,
    w_first,
    w_second,
    w_third,
    biases,
    w_head,
):
    width, _, members = feats.shape
    viewers = lax.axis_size("view")
    shards = lax.axis_size("gauss")
    attrs = entry_grads.shape[1]
    factor = 1.0 / math.sqrt(members * viewers * shards)
    view = lax.axis_index("view").astype(jnp.int32).reshape(1)
    side = view % 2
    position = scatter(view, entry_grads, vis_ids, 0, GROUP, members, viewers)
    position = to_owner(position, viewers)
    others = scatter(view, entry_grads, vis_ids, GROUP, attrs - GROUP, members, viewers)
    others = to_owner(others, viewers)
    feat_grads, skin_grads, mine, theirs = network(
        side,
        position,
        feats[:, 0],
        code_tab.T,
        subj_ids,
        bone_ids,
        skin_w,
        canon_pos,
        bone_tf,
        w_first,
        w_second,
        w_third,
        biases,
        w_head,
        factor,
    )
    mine, theirs = sum_over_devices(mine, theirs, viewers, shards)
    first, second, third, bias, head, code, bone = finish(
        side, mine, theirs, width, code_tab.shape[1], bone_tf.shape[1]
    )
    attr = jnp.concatenate(
        [jnp.sum(position.astype(F32), axis=0), jnp.sum(others.astype(F32), axis=0)[: attrs - GROUP]], axis=0
    )
    return (
        attr[:, None, :],
        feat_grads[:, None, :],
        skin_grads,
        first,
        second,
        third,
        bias,
        head,
        code.T,
        bone,
    )


def solution(mesh):
    placed = (
        P("view", None, "gauss"),
        P("view", "gauss"),
        P(None, "gauss", "view"),
        P(),
        P("gauss", "view"),
        P(None, "gauss", "view"),
        P(None, "gauss", "view"),
        P(None, "gauss", "view"),
        P(),
        P(),
        P(),
        P(),
        P(),
        P(),
    )
    return jax.shard_map(
        body,
        mesh=mesh,
        in_specs=placed,
        out_specs=(
            P(None, "gauss", "view"),
            P(None, "gauss", "view"),
            P(None, "gauss", "view"),
            P(),
            P(),
            P(),
            P(),
            P(),
            P(),
            P(),
        ),
        check_vma=False,
    )
```

```python
import functools
import math

import jax
import jax.numpy as jnp
from jax import lax
from jax.experimental import pallas as pl
from jax.experimental.pallas import tpu as pltpu
from jax.sharding import PartitionSpec as P

F32 = jnp.float32
BF16 = jnp.bfloat16
AXES = ("view", "gauss")
LOW = 256
GROUP = 16
NT = (((1,), (1,)), ((), ()))
TN = (((0,), (0,)), ((), ()))
HBM = pl.BlockSpec(memory_space=pltpu.HBM)
VMEM = pl.BlockSpec(memory_space=pltpu.VMEM)
SMEM = pl.BlockSpec(memory_space=pltpu.SMEM)


def params(mebibytes):
    return pltpu.CompilerParams(vmem_limit_bytes=mebibytes * 1024 * 1024)


def mm(left, right, dims=(((1,), (0,)), ((), ()))):
    return lax.dot_general(left, right, dims, preferred_element_type=F32)


def divisor(total, choices):
    for choice in choices:
        if total % choice == 0:
            return choice
    return total


def scatter_kernel(first_row, rows, viewers, view_ref, grads_ref, ids_ref, out_ref, acc_ref, left_ref):
    entries = ids_ref.shape[1]
    step = left_ref.shape[1]
    height = out_ref.shape[1]
    blocks = acc_ref.shape[0] // height
    groups = height // GROUP
    low_rows = lax.broadcasted_iota(jnp.int32, (LOW, step), 0).astype(F32).astype(BF16)
    one = jnp.ones((), BF16)
    zero = jnp.zeros((), BF16)

    def chunk(index, carry):
        spot = pl.ds(pl.multiple_of(index * step, step), step)
        ids = ids_ref[0:1, spot]
        high = lax.shift_right_logical(ids, 8).astype(F32).astype(BF16)
        low = lax.bitwise_and(ids, LOW - 1).astype(F32).astype(BF16)
        hot = jnp.where(low_rows == low, one, zero)
        high = jnp.broadcast_to(high, (GROUP, step))
        for group in range(groups):
            begin = first_row + group * GROUP
            count = min(GROUP, first_row + rows - begin)
            piece = grads_ref[0, begin : begin + count, spot]
            if count < GROUP:
                piece = jnp.concatenate(
                    [piece.astype(F32), jnp.zeros((GROUP - count, step), F32)], axis=0
                ).astype(BF16)
            for block in range(blocks):
                place = block * height + group * GROUP
                left_ref[place : place + GROUP, :] = jnp.where(high == jnp.asarray(block, BF16), piece, zero)
        product = mm(left_ref[...], hot, NT)

        @pl.when(index == 0)
        def _():
            acc_ref[...] = product

        @pl.when(index != 0)
        def _():
            acc_ref[...] += product

        return carry

    lax.fori_loop(0, entries // step, chunk, 0)
    per = blocks // viewers
    for block in range(blocks):
        slot = lax.rem(block // per - view_ref[0] + viewers, viewers)
        out_ref[slot, :, (block % per) * LOW : (block % per + 1) * LOW] = acc_ref[
            block * height : (block + 1) * height, :
        ].astype(BF16)


def scatter(view, entry_grads, vis_ids, first_row, rows, members, viewers):
    height = -(-rows // GROUP) * GROUP
    blocks = members * viewers // LOW
    step = divisor(vis_ids.shape[1], (2560, 2048, 1024, 512, 256, 128))
    return pl.pallas_call(
        functools.partial(scatter_kernel, first_row, rows, viewers),
        out_shape=jax.ShapeDtypeStruct((viewers, height, members), BF16),
        in_specs=[SMEM, VMEM, VMEM],
        out_specs=VMEM,
        scratch_shapes=[pltpu.VMEM((blocks * height, LOW), F32), pltpu.VMEM((blocks * height, step), BF16)],
        compiler_params=params(16),
    )(view, entry_grads, vis_ids)


def entry_kernel(viewers, count, view_ref, *refs):
    sources, out_ref, targets = refs[:count], refs[count], refs[count + 1 : 2 * count + 1]
    acc_ref, left_ref, rows_ref, sems = refs[2 * count + 1 :]
    copies = [
        pltpu.make_async_copy(source, target, sems.at[index])
        for index, (source, target) in enumerate(zip(sources, targets))
    ]
    early = pltpu.make_async_copy(sources[1].at[:, 0:GROUP, :], rows_ref, sems.at[count])
    copies[0].start()
    early.start()
    for copy in copies[1:]:
        copy.start()
    copies[0].wait()
    early.wait()
    scatter_kernel(0, GROUP, viewers, view_ref, rows_ref, targets[0], out_ref, acc_ref, left_ref)
    for copy in copies[1:]:
        copy.wait()


def entry(view, arrays, members, viewers):
    blocks = members * viewers // LOW
    step = divisor(arrays[0].shape[1], (2560, 2048, 1024, 512, 256, 128))
    count = len(arrays)
    results = pl.pallas_call(
        functools.partial(entry_kernel, viewers, count),
        out_shape=(
            jax.ShapeDtypeStruct((viewers, GROUP, members), BF16),
            *(jax.ShapeDtypeStruct(value.shape, value.dtype) for value in arrays),
        ),
        in_specs=[SMEM] + [HBM] * count,
        out_specs=(VMEM,) * (count + 1),
        scratch_shapes=[
            pltpu.VMEM((blocks * GROUP, LOW), F32),
            pltpu.VMEM((blocks * GROUP, step), BF16),
            pltpu.VMEM((1, GROUP, arrays[0].shape[1]), BF16),
            pltpu.SemaphoreType.DMA((count + 1,)),
        ],
        compiler_params=params(16),
    )(view, *(pltpu.with_memory_space_constraint(value, pltpu.HBM) for value in arrays))
    return results[0], results[1:]


def two_parts(value):
    top = value.astype(BF16)
    return top, value - top.astype(F32)


def forward_kernel(
    feats_ref,
    code_ref,
    subj_ref,
    bone_ids_ref,
    skin_ref,
    canon_ref,
    table_ref,
    first_ref,
    second_ref,
    third_ref,
    bias_ref,
    head_ref,
    inputs_out,
    act_one_out,
    act_two_out,
    act_three_out,
    slope_one_out,
    slope_two_out,
    slope_three_out,
    point_out,
    matrix_out,
    blend_out,
    bone_out,
    head_s,
    bias_s,
    table_s,
):
    width, members = feats_ref.shape
    subjects = code_ref.shape[0]
    table_cols = table_ref.shape[1]
    per_subject = table_cols // subjects
    influence = bone_ids_ref.shape[0]
    padded = bone_out.shape[0] // 2
    pieces = table_s.shape[1] // 128

    head_s[...] = jnp.zeros_like(head_s)
    head_s[0:3, :] = head_ref[...].astype(F32)
    head_w = head_s[...].astype(BF16)
    bias_s[...] = jnp.zeros_like(bias_s)
    bias_s[0:3, :] = bias_ref[...]
    bias_cols = bias_s[...].T
    table_s[...] = jnp.zeros_like(table_s)
    table_s[0:12, 0:table_cols] = table_ref[...]
    code = code_ref[...]
    code_hi, code_rest = two_parts(code)
    code_mid, code_lo = two_parts(code_rest)
    code_w = jnp.concatenate([code_hi.astype(F32), code_mid.astype(F32), code_lo], axis=0).T.astype(BF16)

    subject = subj_ref[0:1, :]
    hot_rows = lax.broadcasted_iota(jnp.int32, (3 * subjects, members), 0) % subjects
    hot = (hot_rows == subject).astype(F32).astype(BF16)
    x = (feats_ref[...].astype(F32) + mm(code_w, hot)).astype(BF16)
    inputs_out[0:width, :] = x
    inputs_out[width : width + 16, :] = hot[0:16]
    act = x
    layers = (
        (first_ref, act_one_out, slope_one_out),
        (second_ref, act_two_out, slope_two_out),
        (third_ref, act_three_out, slope_three_out),
    )
    for layer, (weight, act_out, slope_out) in enumerate(layers):
        pre = mm(weight[...], act) + bias_cols[:, layer : layer + 1]
        sig = 0.5 * jnp.tanh(0.5 * pre) + 0.5
        value = pre * sig
        slope_out[...] = sig + value * (1.0 - sig)
        act = value.astype(BF16)
        act_out[...] = act
    moved = mm(head_w, act)
    for axis in range(3):
        point_out[axis : axis + 1, :] = canon_ref[axis] + moved[axis : axis + 1]
    point_out[3:4, :] = jnp.ones((1, members), F32)

    bone_rows = lax.broadcasted_iota(jnp.int32, (padded, members), 0)
    spread = jnp.zeros((padded, members), F32)
    for member in range(influence):
        chosen = bone_ids_ref[member]
        spread = spread + jnp.where(bone_rows == chosen, skin_ref[member], 0.0)
    spread_hi, spread_lo = two_parts(spread)
    bone_out[0:padded, :] = spread_hi
    bone_out[padded : 2 * padded, :] = spread_lo.astype(BF16)

    for tile in range(members // 128):
        lanes = slice(tile * 128, (tile + 1) * 128)
        base = subj_ref[0:1, lanes] * per_subject
        blend = [jnp.zeros((8, 128), F32), jnp.zeros((8, 128), F32)]
        for member in range(influence):
            column = jnp.broadcast_to(base + bone_ids_ref[member, :, lanes], (8, 128))
            within = lax.bitwise_and(column, 127)
            weight = skin_ref[member, :, lanes]
            for part in range(2):
                rows = slice(part * 8, part * 8 + 8)
                matrix = jnp.take_along_axis(table_s[rows, 0:128], within, axis=1, mode="promise_in_bounds")
                for piece in range(1, pieces):
                    other = jnp.take_along_axis(
                        table_s[rows, piece * 128 : (piece + 1) * 128], within, axis=1, mode="promise_in_bounds"
                    )
                    matrix = jnp.where(column >= piece * 128, other, matrix)
                matrix_out[member, rows, lanes] = matrix
                blend[part] = blend[part] + weight * matrix
        blend_out[0:8, lanes] = blend[0]
        blend_out[8:16, lanes] = blend[1]


def forward(feats, code, subj, bone_ids, skin, canon, table, w1, w2, w3, bias, head):
    width, members = feats.shape
    influence = bone_ids.shape[0]
    subjects = code.shape[0]
    table_cols = table.shape[1]
    padded = -(-(table_cols // subjects) // 16) * 16
    act = jax.ShapeDtypeStruct((width, members), BF16)
    slope = jax.ShapeDtypeStruct((width, members), F32)
    return pl.pallas_call(
        forward_kernel,
        out_shape=(
            jax.ShapeDtypeStruct((width + 16, members), BF16),
            act,
            act,
            act,
            slope,
            slope,
            slope,
            jax.ShapeDtypeStruct((4, members), F32),
            jax.ShapeDtypeStruct((influence, 16, members), F32),
            jax.ShapeDtypeStruct((16, members), F32),
            jax.ShapeDtypeStruct((2 * padded, members), BF16),
        ),
        in_specs=[VMEM] * 12,
        out_specs=(VMEM,) * 11,
        scratch_shapes=[
            pltpu.VMEM((16, width), F32),
            pltpu.VMEM((8, width), F32),
            pltpu.VMEM((16, -(-table_cols // 128) * 128), F32),
        ],
        compiler_params=params(16),
    )(feats, code, subj, bone_ids, skin, canon, table, w1, w2, w3, bias, head)


def split_halves(side, total_s, mine_out, theirs_out, factor):
    half = mine_out.shape[0]
    mine_out[...] = (total_s[pl.ds(pl.multiple_of(side * half, 16), half), :] * factor).astype(BF16)
    theirs_out[...] = (total_s[pl.ds(pl.multiple_of((1 - side) * half, 16), half), :] * factor).astype(BF16)


def lane_sums(value):
    total = value[:, 0:128]
    for lane in range(128, value.shape[1], 128):
        total = total + value[:, lane : lane + 128]
    return jnp.sum(total.T, axis=0, keepdims=True)


def upper_kernel(factor, subjects, per_subject, got, *refs):
    (side_ref, pos_ref), refs = refs[:2], refs[2:]
    got_refs, refs = refs[:got], refs[got:]
    (
        point_ref,
        blend_ref,
        bone_ref,
        subj_ref,
        act_one_ref,
        act_two_ref,
        act_three_ref,
        slope_two_ref,
        slope_three_ref,
        third_ref,
        head_ref,
        outer_out,
        back_out,
        rest_out,
        mine_out,
        theirs_out,
        total_s,
        head_s,
        masked_s,
    ) = refs
    width, members = act_one_ref.shape
    lead = width // 2
    padded = bone_ref.shape[0] // 2
    half = mine_out.shape[0]

    head_s[...] = jnp.zeros_like(head_s)
    head_s[0:3, :] = head_ref[...].astype(F32)
    head_w = head_s[...].astype(BF16)
    grad = pos_ref[0].astype(F32)
    for ref in got_refs:
        grad = grad + ref[...].astype(F32)
    rows = lax.broadcasted_iota(jnp.int32, (16, members), 0)
    quarter = rows // 4
    place = rows % 4
    grad_rows = jnp.where(
        quarter == 0,
        grad[0:1],
        jnp.where(quarter == 1, grad[1:2], jnp.where(quarter == 2, grad[2:3], 0.0)),
    )
    point = point_ref[...]
    point_rows = jnp.where(
        place == 0, point[0:1], jnp.where(place == 1, point[1:2], jnp.where(place == 2, point[2:3], point[3:4]))
    )
    outer = grad_rows * point_rows
    outer_out[...] = outer
    pulled = blend_ref[...] * grad_rows
    shift = pulled[0:4] + pulled[4:8] + pulled[8:12]
    shift = jnp.where(rows[0:4] < 3, shift, 0.0)
    shift = jnp.concatenate([shift, jnp.zeros((12, members), F32)], axis=0).astype(BF16)
    back = mm(head_w, shift, TN) * slope_three_ref[...]
    bias_three = lane_sums(back)
    back = back.astype(BF16)
    total_s[0:width, :] = mm(back, act_two_ref[...], NT)
    small = half + half - 32
    total_s[small : small + 3, :] = mm(shift, act_three_ref[...], NT)[0:3]
    back = mm(third_ref[...], back, TN) * slope_two_ref[...]
    total_s[small + 3 : small + 4, :] = lane_sums(back)
    total_s[small + 4 : small + 5, :] = bias_three
    total_s[small + 5 : small + 16, :] = jnp.zeros((11, width), F32)
    back = back.astype(BF16)
    back_out[...] = back
    second = mm(back, act_one_ref[...], NT)
    total_s[width : width + lead, :] = second[0:lead]
    rest_out[...] = second[lead:width]

    outer_hi, outer_lo = two_parts(outer)
    outer_lo = outer_lo.astype(BF16)
    subject = jnp.broadcast_to(subj_ref[...].astype(F32).astype(BF16), (16, members))
    zero = jnp.zeros((), BF16)
    for s in range(subjects):
        inside = subject == jnp.asarray(s, BF16)
        masked_s[32 * s : 32 * s + 16, :] = jnp.where(inside, outer_hi, zero)
        masked_s[32 * s + 16 : 32 * s + 32, :] = jnp.where(inside, outer_lo, zero)
    product = mm(masked_s[...], bone_ref[...], NT)
    total_s[small + 16 : small + 32, :] = jnp.zeros((16, width), F32)
    for s in range(subjects):
        both = product[32 * s : 32 * s + 16] + product[32 * s + 16 : 32 * s + 32]
        columns = slice(s * per_subject, (s + 1) * per_subject)
        total_s[small + 16 : small + 32, columns] = both[:, 0:per_subject] + both[:, padded : padded + per_subject]
    split_halves(side_ref[0], total_s, mine_out, theirs_out, factor)


def upper(side, pos, got, forwarded, subj, w3, head, factor, subjects, per_subject):
    _, act_one, act_two, act_three, _, slope_two, slope_three, point, _, blend, bone = forwarded
    width, members = act_one.shape
    half = (width + width // 2 + 32) // 2
    part = jax.ShapeDtypeStruct((half, width), BF16)
    return pl.pallas_call(
        functools.partial(upper_kernel, factor, subjects, per_subject, len(got)),
        out_shape=(
            jax.ShapeDtypeStruct((16, members), F32),
            jax.ShapeDtypeStruct((width, members), BF16),
            jax.ShapeDtypeStruct((width // 2, width), F32),
            part,
            part,
        ),
        in_specs=[SMEM] + [VMEM] * (12 + len(got)),
        out_specs=(VMEM,) * 5,
        scratch_shapes=[
            pltpu.VMEM((2 * half, width), F32),
            pltpu.VMEM((16, width), F32),
            pltpu.VMEM((32 * subjects, members), BF16),
        ],
        compiler_params=params(16),
    )(
        side,
        pos,
        *got,
        point,
        blend,
        bone,
        subj,
        act_one,
        act_two,
        act_three,
        slope_two,
        slope_three,
        w3,
        head,
    )


def lower_kernel(
    factor,
    subjects,
    side_ref,
    back_ref,
    rest_ref,
    inputs_ref,
    slope_ref,
    second_ref,
    first_ref,
    back_out,
    mine_out,
    theirs_out,
    total_s,
):
    width = back_out.shape[0]
    half = mine_out.shape[0]
    lead = width // 2
    back = (mm(second_ref[...], back_ref[...], TN) * slope_ref[...]).astype(BF16)
    back_out[...] = back
    product = mm(inputs_ref[...], back, NT)
    by_subject = product[width : width + subjects]
    by_hi, by_rest = two_parts(by_subject)
    by_mid, by_lo = two_parts(by_rest)
    by_parts = jnp.concatenate([by_hi.astype(F32), by_mid.astype(F32), by_lo], axis=0).astype(BF16)
    code = mm(by_parts, first_ref[...])
    total_s[0:width, :] = product[0:width].T
    total_s[width : width + lead, :] = rest_ref[...]
    small = width + lead
    total_s[small : small + subjects, :] = (
        code[0:subjects] + code[subjects : 2 * subjects] + code[2 * subjects : 3 * subjects]
    )
    total_s[small + subjects : small + 16, :] = jnp.broadcast_to(
        jnp.sum(by_subject, axis=0, keepdims=True), (16 - subjects, width)
    )
    total_s[small + 16 : small + 32, :] = jnp.zeros((16, width), F32)
    split_halves(side_ref[0], total_s, mine_out, theirs_out, factor)


def lower(side, back, rest, inputs, slope, w2, w1, factor, subjects):
    width, members = back.shape
    half = (width + width // 2 + 32) // 2
    part = jax.ShapeDtypeStruct((half, width), BF16)
    return pl.pallas_call(
        functools.partial(lower_kernel, factor, subjects),
        out_shape=(jax.ShapeDtypeStruct((width, members), BF16), part, part),
        in_specs=[SMEM] + [VMEM] * 6,
        out_specs=(VMEM,) * 3,
        scratch_shapes=[pltpu.VMEM((2 * half, width), F32)],
        compiler_params=params(16),
    )(side, back, rest, inputs, slope, w2, w1)


def gaussian_kernel(back_ref, first_ref, outer_ref, matrix_ref, feat_out, skin_out):
    feat_out[...] = mm(first_ref[...], back_ref[...], TN).astype(BF16)
    outer = outer_ref[...]
    for member in range(matrix_ref.shape[0]):
        skin_out[member] = jnp.sum(outer * matrix_ref[member], axis=0, keepdims=True)


def gaussian_grads(back, w1, outer, matrix):
    width, members = back.shape
    influence = matrix.shape[0]
    return pl.pallas_call(
        gaussian_kernel,
        out_shape=(
            jax.ShapeDtypeStruct((width, members), BF16),
            jax.ShapeDtypeStruct((influence, 1, members), F32),
        ),
        in_specs=[VMEM] * 4,
        out_specs=(VMEM,) * 2,
        compiler_params=params(16),
    )(back, w1, outer, matrix)


def finish_kernel(
    side_ref,
    upper_mine,
    upper_theirs,
    lower_mine,
    lower_theirs,
    first_out,
    second_out,
    third_out,
    bias_out,
    head_out,
    code_out,
    bone_out,
):
    width = third_out.shape[0]
    half = upper_mine.shape[0]
    lead = width // 2
    table_cols = bone_out.shape[1]
    subjects = code_out.shape[0]

    def write(up, low):
        def rows(pair, begin, end):
            pieces = []
            if begin < half:
                pieces.append(pair[0][begin : min(end, half), :].astype(F32))
            if end > half:
                pieces.append(pair[1][max(begin, half) - half : end - half, :].astype(F32))
            return pieces

        def store(out, pair, begin, end, place=0):
            for piece in rows(pair, begin, end):
                out[place : place + piece.shape[0], :] = piece
                place += piece.shape[0]

        small = width + lead
        store(third_out, up, 0, width)
        store(second_out, up, width, small)
        store(second_out, low, small - lead, small, lead)
        store(first_out, low, 0, width)
        (values,) = rows(up, small, small + 16)
        head_out[...] = values[0:3]
        bias_out[1:3, :] = values[3:5]
        (values,) = rows(up, small + 16, small + 32)
        bone_out[...] = values[0:12, 0:table_cols]
        (values,) = rows(low, small, small + 16)
        code_out[...] = values[0:subjects]
        bias_out[0:1, :] = values[subjects : subjects + 1]

    @pl.when(side_ref[0] == 0)
    def _():
        write((upper_mine, upper_theirs), (lower_mine, lower_theirs))

    @pl.when(side_ref[0] != 0)
    def _():
        write((upper_theirs, upper_mine), (lower_theirs, lower_mine))


def finish(side, upper_both, lower_both, subjects, table_cols):
    width = upper_both[0].shape[1]
    square = jax.ShapeDtypeStruct((width, width), F32)
    rows = jax.ShapeDtypeStruct((3, width), F32)
    return pl.pallas_call(
        finish_kernel,
        out_shape=(
            square,
            square,
            square,
            rows,
            rows,
            jax.ShapeDtypeStruct((subjects, width), F32),
            jax.ShapeDtypeStruct((12, table_cols), F32),
        ),
        in_specs=[SMEM] + [VMEM] * 4,
        out_specs=(VMEM,) * 7,
        compiler_params=params(16),
    )(side, *upper_both, *lower_both)


def attr_kernel(count, *refs):
    out_ref = refs[-1]
    attrs = out_ref.shape[0]
    row = 0
    for start in (0, count):
        total = refs[start][0].astype(F32)
        for ref in refs[start + 1 : start + count]:
            total = total + ref[...].astype(F32)
        for place in range(min(total.shape[0], attrs - row)):
            out_ref[row + place] = total[place : place + 1]
        row += total.shape[0]


def attr_sum(position, position_got, others, others_got, attrs):
    members = position.shape[2]
    count = 1 + len(position_got)
    return pl.pallas_call(
        functools.partial(attr_kernel, count),
        out_shape=jax.ShapeDtypeStruct((attrs, 1, members), F32),
        in_specs=[VMEM] * (2 * count),
        out_specs=VMEM,
        compiler_params=params(16),
    )(position, *position_got, others, *others_got)


def add(left, right):
    return (left.astype(F32) + right.astype(F32)).astype(BF16)


def swap(value, mask, count):
    return lax.ppermute(value, AXES, [(place, place ^ mask) for place in range(count)])


def tied(values, others):
    held = lax.optimization_barrier((tuple(values), tuple(others)))
    return list(held[0]), list(held[1])


def sum_over_devices(halves, viewers, shards, between):
    count = viewers * shards
    pair = shards
    masks = [1 << bit for bit in range(count.bit_length() - 1) if 1 << bit != pair]
    orders = [[masks[0], *masks[2:], masks[1]], [masks[1], masks[0], *masks[2:]]]
    parts = [add(mine, swap(theirs, pair, count)) for mine, theirs in halves]
    for stage in range(len(masks)):
        got = [swap(part, order[stage], count) for part, order in zip(parts, orders)]
        for work in between.get(stage, ()):
            got[0] = work(parts[0], got[0])
        parts = [add(part, other) for part, other in zip(parts, got)]
    return [(part, swap(part, pair, count)) for part in parts]


class Work:
    def __init__(self, call, *operands):
        self.call = call
        self.operands = operands
        self.results = None

    def __call__(self, after, before):
        operands, _ = tied(self.operands, [after])
        results = self.call(*operands)
        self.results, held = tied(results, [before])
        return held[0]


def received(parts, viewers):
    got = []
    for away in range(1, viewers):
        perm = [(place, (place + away) % viewers) for place in range(viewers)]
        got.append(lax.ppermute(parts[away], "view", perm))
    return got


def body(
    entry_grads,
    vis_ids,
    feats,
    code_tab,
    subj_ids,
    bone_ids,
    skin_w,
    canon_pos,
    bone_tf,
    w_first,
    w_second,
    w_third,
    biases,
    w_head,
):
    members = feats.shape[2]
    viewers = lax.axis_size("view")
    shards = lax.axis_size("gauss")
    attrs = entry_grads.shape[1]
    subjects = code_tab.shape[1]
    table_cols = bone_tf.shape[1]
    factor = 1.0 / math.sqrt(members * viewers * shards)
    view = lax.axis_index("view").astype(jnp.int32).reshape(1)
    side = lax.bitwise_and(view, 1)
    position, arrays = entry(
        view,
        (
            vis_ids,
            entry_grads,
            feats[:, 0],
            code_tab.T,
            subj_ids,
            bone_ids,
            skin_w,
            canon_pos,
            bone_tf,
            w_first,
            w_second,
            w_third,
            biases,
            w_head,
        ),
        members,
        viewers,
    )
    vis_ids, entry_grads, *arrays = arrays
    subj_ids, (w_first, w_second, w_third), w_head = arrays[2], arrays[7:10], arrays[11]
    position_got = received(position, viewers)
    forwarded = forward(*arrays)
    outer, back_two, second_rest, *upper_halves = upper(
        side, position, position_got, forwarded, subj_ids, w_third, w_head, factor, subjects, table_cols // subjects
    )
    back_one, *lower_halves = lower(
        side, back_two, second_rest, forwarded[0], forwarded[4], w_second, w_first, factor, subjects
    )

    def scatter_rows(row):
        def call(grads, ids):
            return [scatter(view, grads, ids, row, min(GROUP, attrs - row), members, viewers)]

        return Work(call, entry_grads, vis_ids)

    works = [scatter_rows(row) for row in range(GROUP, attrs, GROUP)]
    per_gaussian = Work(gaussian_grads, back_one, w_first, outer, forwarded[8])

    def exchange(_):
        others = jnp.concatenate([work.results[0] for work in works], axis=1)
        others_got = received(others, viewers)
        return [attr_sum(position, position_got, others, others_got, attrs)]

    last = Work(exchange, view)
    between = {0: [works[0]], 1: [works[1]], 2: [works[2], per_gaussian], 3: [last]}
    upper_both, lower_both = sum_over_devices([upper_halves, lower_halves], viewers, shards, between)
    attr = last.results[0]
    feat_grads, skin_grads = per_gaussian.results
    first, second, third, bias, head, code, bone = finish(side, upper_both, lower_both, subjects, table_cols)
    return (
        attr,
        feat_grads[:, None, :],
        skin_grads,
        first,
        second,
        third,
        bias,
        head,
        code.T,
        bone,
    )


def solution(mesh):
    placed = (
        P("view", None, "gauss"),
        P("view", "gauss"),
        P(None, "gauss", "view"),
        P(),
        P("gauss", "view"),
        P(None, "gauss", "view"),
        P(None, "gauss", "view"),
        P(None, "gauss", "view"),
        P(),
        P(),
        P(),
        P(),
        P(),
        P(),
    )
    return jax.shard_map(
        body,
        mesh=mesh,
        in_specs=placed,
        out_specs=(
            P(None, "gauss", "view"),
            P(None, "gauss", "view"),
            P(None, "gauss", "view"),
            P(),
            P(),
            P(),
            P(),
            P(),
            P(),
            P(),
        ),
        check_vma=False,
    )
```

```python
import functools
import math

import jax
import jax.numpy as jnp
from jax import lax
from jax.experimental import pallas as pl
from jax.experimental.pallas import tpu as pltpu
from jax.sharding import PartitionSpec as P

F32 = jnp.float32
BF16 = jnp.bfloat16
AXES = ("view", "gauss")
LOW = 256
GROUP = 16
FAN = 4
NT = (((1,), (1,)), ((), ()))
TN = (((0,), (0,)), ((), ()))
HBM = pl.BlockSpec(memory_space=pltpu.HBM)
VMEM = pl.BlockSpec(memory_space=pltpu.VMEM)
SMEM = pl.BlockSpec(memory_space=pltpu.SMEM)


def params(mebibytes):
    return pltpu.CompilerParams(vmem_limit_bytes=mebibytes * 1024 * 1024)


def mm(left, right, dims=(((1,), (0,)), ((), ()))):
    return lax.dot_general(left, right, dims, preferred_element_type=F32)


def divisor(total, choices):
    for choice in choices:
        if total % choice == 0:
            return choice
    return total


def scatter_kernel(first_row, rows, viewers, view_ref, grads_ref, ids_ref, out_ref, acc_ref, left_ref):
    entries = ids_ref.shape[1]
    step = left_ref.shape[1]
    height = out_ref.shape[1]
    blocks = acc_ref.shape[0] // height
    groups = height // GROUP
    low_rows = lax.broadcasted_iota(jnp.int32, (LOW, step), 0).astype(F32).astype(BF16)
    one = jnp.ones((), BF16)
    zero = jnp.zeros((), BF16)

    def chunk(index, carry):
        spot = pl.ds(pl.multiple_of(index * step, step), step)
        ids = ids_ref[0:1, spot]
        high = lax.shift_right_logical(ids, 8).astype(F32).astype(BF16)
        low = lax.bitwise_and(ids, LOW - 1).astype(F32).astype(BF16)
        hot = jnp.where(low_rows == low, one, zero)
        high = jnp.broadcast_to(high, (GROUP, step))
        for group in range(groups):
            begin = first_row + group * GROUP
            count = min(GROUP, first_row + rows - begin)
            piece = grads_ref[0, begin : begin + count, spot]
            if count < GROUP:
                piece = jnp.concatenate(
                    [piece.astype(F32), jnp.zeros((GROUP - count, step), F32)], axis=0
                ).astype(BF16)
            for block in range(blocks):
                place = block * height + group * GROUP
                left_ref[place : place + GROUP, :] = jnp.where(high == jnp.asarray(block, BF16), piece, zero)
        product = mm(left_ref[...], hot, NT)

        @pl.when(index == 0)
        def _():
            acc_ref[...] = product

        @pl.when(index != 0)
        def _():
            acc_ref[...] += product

        return carry

    lax.fori_loop(0, entries // step, chunk, 0)
    per = blocks // viewers
    for block in range(blocks):
        slot = lax.rem(block // per - view_ref[0] + viewers, viewers)
        out_ref[slot, :, (block % per) * LOW : (block % per + 1) * LOW] = acc_ref[
            block * height : (block + 1) * height, :
        ].astype(BF16)


def scatter(view, entry_grads, vis_ids, first_row, rows, members, viewers):
    height = -(-rows // GROUP) * GROUP
    blocks = members * viewers // LOW
    step = divisor(vis_ids.shape[1], (2560, 2048, 1024, 512, 256, 128))
    return pl.pallas_call(
        functools.partial(scatter_kernel, first_row, rows, viewers),
        out_shape=jax.ShapeDtypeStruct((viewers, height, members), BF16),
        in_specs=[SMEM, VMEM, VMEM],
        out_specs=VMEM,
        scratch_shapes=[pltpu.VMEM((blocks * height, LOW), F32), pltpu.VMEM((blocks * height, step), BF16)],
        compiler_params=params(16),
    )(view, entry_grads, vis_ids)


def entry_kernel(viewers, count, view_ref, *refs):
    sources, out_ref, targets = refs[:count], refs[count], refs[count + 1 : 2 * count + 1]
    acc_ref, left_ref, rows_ref, sems = refs[2 * count + 1 :]
    copies = [
        pltpu.make_async_copy(source, target, sems.at[index])
        for index, (source, target) in enumerate(zip(sources, targets))
    ]
    early = pltpu.make_async_copy(sources[1].at[:, 0:GROUP, :], rows_ref, sems.at[count])
    copies[0].start()
    early.start()
    for copy in copies[1:]:
        copy.start()
    copies[0].wait()
    early.wait()
    scatter_kernel(0, GROUP, viewers, view_ref, rows_ref, targets[0], out_ref, acc_ref, left_ref)
    for copy in copies[1:]:
        copy.wait()


def entry(view, arrays, members, viewers):
    blocks = members * viewers // LOW
    step = divisor(arrays[0].shape[1], (2560, 2048, 1024, 512, 256, 128))
    count = len(arrays)
    results = pl.pallas_call(
        functools.partial(entry_kernel, viewers, count),
        out_shape=(
            jax.ShapeDtypeStruct((viewers, GROUP, members), BF16),
            *(jax.ShapeDtypeStruct(value.shape, value.dtype) for value in arrays),
        ),
        in_specs=[SMEM] + [HBM] * count,
        out_specs=(VMEM,) * (count + 1),
        scratch_shapes=[
            pltpu.VMEM((blocks * GROUP, LOW), F32),
            pltpu.VMEM((blocks * GROUP, step), BF16),
            pltpu.VMEM((1, GROUP, arrays[0].shape[1]), BF16),
            pltpu.SemaphoreType.DMA((count + 1,)),
        ],
        compiler_params=params(16),
    )(view, *(pltpu.with_memory_space_constraint(value, pltpu.HBM) for value in arrays))
    return results[0], results[1:]


def two_parts(value):
    top = value.astype(BF16)
    return top, value - top.astype(F32)


def forward_kernel(
    feats_ref,
    code_ref,
    subj_ref,
    bone_ids_ref,
    skin_ref,
    canon_ref,
    table_ref,
    first_ref,
    second_ref,
    third_ref,
    bias_ref,
    head_ref,
    inputs_out,
    act_one_out,
    act_two_out,
    act_three_out,
    slope_one_out,
    slope_two_out,
    slope_three_out,
    point_out,
    matrix_out,
    blend_out,
    bone_out,
    head_s,
    bias_s,
    table_s,
):
    width, members = feats_ref.shape
    subjects = code_ref.shape[0]
    table_cols = table_ref.shape[1]
    per_subject = table_cols // subjects
    influence = bone_ids_ref.shape[0]
    padded = bone_out.shape[0] // 2
    pieces = table_s.shape[1] // 128

    head_s[...] = jnp.zeros_like(head_s)
    head_s[0:3, :] = head_ref[...].astype(F32)
    head_w = head_s[...].astype(BF16)
    bias_s[...] = jnp.zeros_like(bias_s)
    bias_s[0:3, :] = bias_ref[...]
    bias_cols = bias_s[...].T
    table_s[...] = jnp.zeros_like(table_s)
    table_s[0:12, 0:table_cols] = table_ref[...]
    code = code_ref[...]
    code_hi, code_rest = two_parts(code)
    code_mid, code_lo = two_parts(code_rest)
    code_w = jnp.concatenate([code_hi.astype(F32), code_mid.astype(F32), code_lo], axis=0).T.astype(BF16)

    subject = subj_ref[0:1, :]
    hot_rows = lax.broadcasted_iota(jnp.int32, (3 * subjects, members), 0) % subjects
    hot = (hot_rows == subject).astype(F32).astype(BF16)
    x = (feats_ref[...].astype(F32) + mm(code_w, hot)).astype(BF16)
    inputs_out[0:width, :] = x
    inputs_out[width : width + 16, :] = hot[0:16]
    act = x
    layers = (
        (first_ref, act_one_out, slope_one_out),
        (second_ref, act_two_out, slope_two_out),
        (third_ref, act_three_out, slope_three_out),
    )
    for layer, (weight, act_out, slope_out) in enumerate(layers):
        pre = mm(weight[...], act) + bias_cols[:, layer : layer + 1]
        sig = 0.5 * jnp.tanh(0.5 * pre) + 0.5
        value = pre * sig
        slope_out[...] = sig + value * (1.0 - sig)
        act = value.astype(BF16)
        act_out[...] = act
    moved = mm(head_w, act)
    for axis in range(3):
        point_out[axis : axis + 1, :] = canon_ref[axis] + moved[axis : axis + 1]
    point_out[3:4, :] = jnp.ones((1, members), F32)

    bone_rows = lax.broadcasted_iota(jnp.int32, (padded, members), 0)
    spread = jnp.zeros((padded, members), F32)
    for member in range(influence):
        chosen = bone_ids_ref[member]
        spread = spread + jnp.where(bone_rows == chosen, skin_ref[member], 0.0)
    spread_hi, spread_lo = two_parts(spread)
    bone_out[0:padded, :] = spread_hi
    bone_out[padded : 2 * padded, :] = spread_lo.astype(BF16)

    for tile in range(members // 128):
        lanes = slice(tile * 128, (tile + 1) * 128)
        base = subj_ref[0:1, lanes] * per_subject
        blend = [jnp.zeros((8, 128), F32), jnp.zeros((8, 128), F32)]
        for member in range(influence):
            column = jnp.broadcast_to(base + bone_ids_ref[member, :, lanes], (8, 128))
            within = lax.bitwise_and(column, 127)
            weight = skin_ref[member, :, lanes]
            for part in range(2):
                rows = slice(part * 8, part * 8 + 8)
                matrix = jnp.take_along_axis(table_s[rows, 0:128], within, axis=1, mode="promise_in_bounds")
                for piece in range(1, pieces):
                    other = jnp.take_along_axis(
                        table_s[rows, piece * 128 : (piece + 1) * 128], within, axis=1, mode="promise_in_bounds"
                    )
                    matrix = jnp.where(column >= piece * 128, other, matrix)
                matrix_out[member, rows, lanes] = matrix
                blend[part] = blend[part] + weight * matrix
        blend_out[0:8, lanes] = blend[0]
        blend_out[8:16, lanes] = blend[1]


def forward(feats, code, subj, bone_ids, skin, canon, table, w1, w2, w3, bias, head):
    width, members = feats.shape
    influence = bone_ids.shape[0]
    subjects = code.shape[0]
    table_cols = table.shape[1]
    padded = -(-(table_cols // subjects) // 16) * 16
    act = jax.ShapeDtypeStruct((width, members), BF16)
    slope = jax.ShapeDtypeStruct((width, members), F32)
    return pl.pallas_call(
        forward_kernel,
        out_shape=(
            jax.ShapeDtypeStruct((width + 16, members), BF16),
            act,
            act,
            act,
            slope,
            slope,
            slope,
            jax.ShapeDtypeStruct((4, members), F32),
            jax.ShapeDtypeStruct((influence, 16, members), F32),
            jax.ShapeDtypeStruct((16, members), F32),
            jax.ShapeDtypeStruct((2 * padded, members), BF16),
        ),
        in_specs=[VMEM] * 12,
        out_specs=(VMEM,) * 11,
        scratch_shapes=[
            pltpu.VMEM((16, width), F32),
            pltpu.VMEM((8, width), F32),
            pltpu.VMEM((16, -(-table_cols // 128) * 128), F32),
        ],
        compiler_params=params(16),
    )(feats, code, subj, bone_ids, skin, canon, table, w1, w2, w3, bias, head)


def block_rows(width):
    return -(-(3 * width + 48) // (2 * FAN * 16)) * 16


def split_blocks(side, quarter, total_s, mine_out, theirs_out, factor):
    rows = mine_out.shape[1]
    for core, out in ((side, mine_out), (1 - side, theirs_out)):
        for slot in range(FAN):
            place = (core * FAN + lax.bitwise_xor(quarter, slot)) * rows
            out[slot] = (total_s[pl.ds(pl.multiple_of(place, 16), rows), :] * factor).astype(BF16)


def lane_sums(value):
    total = value[:, 0:128]
    for lane in range(128, value.shape[1], 128):
        total = total + value[:, lane : lane + 128]
    return jnp.sum(total.T, axis=0, keepdims=True)


def backward_kernel(factor, subjects, per_subject, got, *refs):
    (side_ref, quarter_ref, pos_ref), refs = refs[:3], refs[3:]
    got_refs, refs = refs[:got], refs[got:]
    (
        point_ref,
        blend_ref,
        bone_ref,
        subj_ref,
        inputs_ref,
        act_one_ref,
        act_two_ref,
        act_three_ref,
        slope_one_ref,
        slope_two_ref,
        slope_three_ref,
        first_ref,
        second_ref,
        third_ref,
        head_ref,
        outer_out,
        back_out,
        mine_out,
        theirs_out,
        total_s,
        head_s,
        masked_s,
    ) = refs
    width, members = act_one_ref.shape
    padded = bone_ref.shape[0] // 2
    small = 3 * width

    head_s[...] = jnp.zeros_like(head_s)
    head_s[0:3, :] = head_ref[...].astype(F32)
    head_w = head_s[...].astype(BF16)
    total_s[small:, :] = jnp.zeros((total_s.shape[0] - small, width), F32)
    grad = pos_ref[0].astype(F32)
    for ref in got_refs:
        grad = grad + ref[...].astype(F32)
    rows = lax.broadcasted_iota(jnp.int32, (16, members), 0)
    quarter = rows // 4
    place = rows % 4
    grad_rows = jnp.where(
        quarter == 0,
        grad[0:1],
        jnp.where(quarter == 1, grad[1:2], jnp.where(quarter == 2, grad[2:3], 0.0)),
    )
    point = point_ref[...]
    point_rows = jnp.where(
        place == 0, point[0:1], jnp.where(place == 1, point[1:2], jnp.where(place == 2, point[2:3], point[3:4]))
    )
    outer = grad_rows * point_rows
    outer_out[...] = outer
    pulled = blend_ref[...] * grad_rows
    shift = pulled[0:4] + pulled[4:8] + pulled[8:12]
    shift = jnp.where(rows[0:4] < 3, shift, 0.0)
    shift = jnp.concatenate([shift, jnp.zeros((12, members), F32)], axis=0).astype(BF16)

    back = mm(head_w, shift, TN) * slope_three_ref[...]
    total_s[small + 5 : small + 6, :] = lane_sums(back)
    back = back.astype(BF16)
    total_s[0:width, :] = mm(back, act_two_ref[...], NT)
    total_s[small : small + 3, :] = mm(shift, act_three_ref[...], NT)[0:3]
    back = mm(third_ref[...], back, TN) * slope_two_ref[...]
    total_s[small + 4 : small + 5, :] = lane_sums(back)
    back = back.astype(BF16)
    total_s[width : 2 * width, :] = mm(back, act_one_ref[...], NT)
    back = (mm(second_ref[...], back, TN) * slope_one_ref[...]).astype(BF16)
    back_out[...] = back
    product = mm(inputs_ref[...], back, NT)
    total_s[2 * width : 3 * width, :] = product[0:width].T
    by_subject = product[width : width + subjects]
    total_s[small + 3 : small + 4, :] = jnp.sum(by_subject, axis=0, keepdims=True)
    by_hi, by_rest = two_parts(by_subject)
    by_mid, by_lo = two_parts(by_rest)
    by_parts = jnp.concatenate([by_hi.astype(F32), by_mid.astype(F32), by_lo], axis=0).astype(BF16)
    code = mm(by_parts, first_ref[...])
    total_s[small + 32 : small + 32 + subjects, :] = (
        code[0:subjects] + code[subjects : 2 * subjects] + code[2 * subjects : 3 * subjects]
    )

    outer_hi, outer_lo = two_parts(outer)
    outer_lo = outer_lo.astype(BF16)
    subject = jnp.broadcast_to(subj_ref[...].astype(F32).astype(BF16), (16, members))
    zero = jnp.zeros((), BF16)
    for s in range(subjects):
        inside = subject == jnp.asarray(s, BF16)
        masked_s[32 * s : 32 * s + 16, :] = jnp.where(inside, outer_hi, zero)
        masked_s[32 * s + 16 : 32 * s + 32, :] = jnp.where(inside, outer_lo, zero)
    product = mm(masked_s[...], bone_ref[...], NT)
    for s in range(subjects):
        both = product[32 * s : 32 * s + 16] + product[32 * s + 16 : 32 * s + 32]
        columns = slice(s * per_subject, (s + 1) * per_subject)
        total_s[small + 16 : small + 32, columns] = both[:, 0:per_subject] + both[:, padded : padded + per_subject]
    split_blocks(side_ref[0], quarter_ref[0], total_s, mine_out, theirs_out, factor)


def backward(side, quarter, pos, got, forwarded, subj, weights, head, factor, subjects, per_subject):
    inputs, act_one, act_two, act_three, *slopes, point, _, blend, bone = forwarded
    width, members = act_one.shape
    rows = block_rows(width)
    part = jax.ShapeDtypeStruct((FAN, rows, width), BF16)
    return pl.pallas_call(
        functools.partial(backward_kernel, factor, subjects, per_subject, len(got)),
        out_shape=(
            jax.ShapeDtypeStruct((16, members), F32),
            jax.ShapeDtypeStruct((width, members), BF16),
            part,
            part,
        ),
        in_specs=[SMEM] * 2 + [VMEM] * (16 + len(got)),
        out_specs=(VMEM,) * 4,
        scratch_shapes=[
            pltpu.VMEM((2 * FAN * rows, width), F32),
            pltpu.VMEM((16, width), F32),
            pltpu.VMEM((32 * subjects, members), BF16),
        ],
        compiler_params=params(24),
    )(
        side,
        quarter,
        pos,
        *got,
        point,
        blend,
        bone,
        subj,
        inputs,
        act_one,
        act_two,
        act_three,
        *slopes,
        *weights,
        head,
    )


def gaussian_kernel(back_ref, first_ref, outer_ref, matrix_ref, feat_out, skin_out):
    feat_out[...] = mm(first_ref[...], back_ref[...], TN).astype(BF16)
    outer = outer_ref[...]
    for member in range(matrix_ref.shape[0]):
        skin_out[member] = jnp.sum(outer * matrix_ref[member], axis=0, keepdims=True)


def gaussian_grads(back, w1, outer, matrix):
    width, members = back.shape
    influence = matrix.shape[0]
    return pl.pallas_call(
        gaussian_kernel,
        out_shape=(
            jax.ShapeDtypeStruct((width, members), BF16),
            jax.ShapeDtypeStruct((influence, 1, members), F32),
        ),
        in_specs=[VMEM] * 4,
        out_specs=(VMEM,) * 2,
        compiler_params=params(16),
    )(back, w1, outer, matrix)


def finish_kernel(side_ref, quarter_ref, *refs):
    mine_refs, refs = refs[:FAN], refs[FAN:]
    theirs_ref, first_out, second_out, third_out, bias_out, head_out, code_out, bone_out, total_s = refs
    width = third_out.shape[0]
    table_cols = bone_out.shape[1]
    subjects = code_out.shape[0]
    rows = mine_refs[0].shape[0]
    side = side_ref[0]
    for slot in range(FAN):
        place = lax.bitwise_xor(quarter_ref[0], slot)
        mine = pl.multiple_of((side * FAN + place) * rows, 16)
        theirs = pl.multiple_of(((1 - side) * FAN + place) * rows, 16)
        total_s[pl.ds(mine, rows), :] = mine_refs[slot][...].astype(F32)
        total_s[pl.ds(theirs, rows), :] = theirs_ref[slot * rows : (slot + 1) * rows, :].astype(F32)
    third_out[...] = total_s[0:width, :]
    second_out[...] = total_s[width : 2 * width, :]
    first_out[...] = total_s[2 * width : 3 * width, :]
    small = total_s[3 * width : 3 * width + 48, :]
    head_out[...] = small[0:3]
    bias_out[...] = small[3:6]
    bone_out[...] = small[16:28, 0:table_cols]
    code_out[...] = small[32 : 32 + subjects]


def finish(side, quarter, mine, theirs, subjects, table_cols):
    rows, width = mine[0].shape
    square = jax.ShapeDtypeStruct((width, width), F32)
    lines = jax.ShapeDtypeStruct((3, width), F32)
    return pl.pallas_call(
        finish_kernel,
        out_shape=(
            square,
            square,
            square,
            lines,
            lines,
            jax.ShapeDtypeStruct((subjects, width), F32),
            jax.ShapeDtypeStruct((12, table_cols), F32),
        ),
        in_specs=[SMEM] * 2 + [VMEM] * (FAN + 1),
        out_specs=(VMEM,) * 7,
        scratch_shapes=[pltpu.VMEM((2 * FAN * rows, width), F32)],
        compiler_params=params(16),
    )(side, quarter, *mine, theirs)


def attr_kernel(count, *refs):
    out_ref = refs[-1]
    attrs = out_ref.shape[0]
    row = 0
    for start in (0, count):
        total = refs[start][0].astype(F32)
        for ref in refs[start + 1 : start + count]:
            total = total + ref[...].astype(F32)
        for place in range(min(total.shape[0], attrs - row)):
            out_ref[row + place] = total[place : place + 1]
        row += total.shape[0]


def attr_sum(position, position_got, others, others_got, attrs):
    members = position.shape[2]
    count = 1 + len(position_got)
    return pl.pallas_call(
        functools.partial(attr_kernel, count),
        out_shape=jax.ShapeDtypeStruct((attrs, 1, members), F32),
        in_specs=[VMEM] * (2 * count),
        out_specs=VMEM,
        compiler_params=params(16),
    )(position, *position_got, others, *others_got)


def add(left, right):
    return (left.astype(F32) + right.astype(F32)).astype(BF16)


def swap(value, mask, count):
    return lax.ppermute(value, AXES, [(place, place ^ mask) for place in range(count)])


def tied(values, others):
    held = lax.optimization_barrier((tuple(values), tuple(others)))
    return list(held[0]), list(held[1])


def sum_over_devices(mine, theirs, viewers, shards, between):
    count = viewers * shards
    pair = shards
    rows, width = mine.shape[1:]
    masks = [1 << bit for bit in range(count.bit_length() - 1) if 1 << bit >= FAN and 1 << bit != pair]

    def work(stage, after, got):
        for item in between.get(stage, ()):
            got[0] = item(after, got[0])
        return got

    arrived = swap(theirs, pair, count)
    blocks = [add(mine[slot], arrived[slot]) for slot in range(FAN)]
    got = [swap(blocks[slot], slot, count) for slot in range(1, FAN)]
    got = work("scatter", blocks[0], got)
    total = sum((value.astype(F32) for value in got), blocks[0].astype(F32)).astype(BF16)
    for stage, mask in enumerate(masks):
        got = work(stage, total, [swap(total, mask, count)])
        total = add(total, got[0])
    got = [swap(total, slot, count) for slot in range(1, FAN)]
    got = work("gather", total, got)
    mine = [total, *got]
    theirs = swap(jnp.concatenate(mine, axis=0), pair, count)
    return mine, theirs


class Work:
    def __init__(self, call, *operands):
        self.call = call
        self.operands = operands
        self.results = None

    def __call__(self, after, before):
        operands, _ = tied(self.operands, [after])
        results = self.call(*operands)
        self.results, held = tied(results, [before])
        return held[0]


def received(parts, viewers):
    got = []
    for away in range(1, viewers):
        perm = [(place, (place + away) % viewers) for place in range(viewers)]
        got.append(lax.ppermute(parts[away], "view", perm))
    return got


def body(
    entry_grads,
    vis_ids,
    feats,
    code_tab,
    subj_ids,
    bone_ids,
    skin_w,
    canon_pos,
    bone_tf,
    w_first,
    w_second,
    w_third,
    biases,
    w_head,
):
    members = feats.shape[2]
    viewers = lax.axis_size("view")
    shards = lax.axis_size("gauss")
    attrs = entry_grads.shape[1]
    subjects = code_tab.shape[1]
    table_cols = bone_tf.shape[1]
    factor = 1.0 / math.sqrt(members * viewers * shards)
    view = lax.axis_index("view").astype(jnp.int32).reshape(1)
    side = lax.bitwise_and(view, 1)
    quarter = lax.bitwise_and(lax.axis_index("gauss").astype(jnp.int32).reshape(1), FAN - 1)
    position, arrays = entry(
        view,
        (
            vis_ids,
            entry_grads,
            feats[:, 0],
            code_tab.T,
            subj_ids,
            bone_ids,
            skin_w,
            canon_pos,
            bone_tf,
            w_first,
            w_second,
            w_third,
            biases,
            w_head,
        ),
        members,
        viewers,
    )
    vis_ids, entry_grads, *arrays = arrays
    subj_ids, weights, w_head = arrays[2], arrays[7:10], arrays[11]
    position_got = received(position, viewers)
    forwarded = forward(*arrays)
    outer, back_one, mine, theirs = backward(
        side,
        quarter,
        position,
        position_got,
        forwarded,
        subj_ids,
        weights,
        w_head,
        factor,
        subjects,
        table_cols // subjects,
    )

    def scatter_rows(row):
        def call(grads, ids):
            return [scatter(view, grads, ids, row, min(GROUP, attrs - row), members, viewers)]

        return Work(call, entry_grads, vis_ids)

    works = [scatter_rows(row) for row in range(GROUP, attrs, GROUP)]
    per_gaussian = Work(gaussian_grads, back_one, weights[0], outer, forwarded[8])

    def attributes(_):
        others = jnp.concatenate([work.results[0] for work in works], axis=1)
        others_got = received(others, viewers)
        return [attr_sum(position, position_got, others, others_got, attrs)]

    last = Work(attributes, view)
    between = {"scatter": works[:2], 0: works[2:], 1: [per_gaussian], "gather": [last]}
    mine, theirs = sum_over_devices(mine, theirs, viewers, shards, between)
    attr = last.results[0]
    feat_grads, skin_grads = per_gaussian.results
    first, second, third, bias, head, code, bone = finish(side, quarter, mine, theirs, subjects, table_cols)
    return (
        attr,
        feat_grads[:, None, :],
        skin_grads,
        first,
        second,
        third,
        bias,
        head,
        code.T,
        bone,
    )


def solution(mesh):
    placed = (
        P("view", None, "gauss"),
        P("view", "gauss"),
        P(None, "gauss", "view"),
        P(),
        P("gauss", "view"),
        P(None, "gauss", "view"),
        P(None, "gauss", "view"),
        P(None, "gauss", "view"),
        P(),
        P(),
        P(),
        P(),
        P(),
        P(),
    )
    return jax.shard_map(
        body,
        mesh=mesh,
        in_specs=placed,
        out_specs=(
            P(None, "gauss", "view"),
            P(None, "gauss", "view"),
            P(None, "gauss", "view"),
            P(),
            P(),
            P(),
            P(),
            P(),
            P(),
            P(),
        ),
        check_vma=False,
    )
```

```python
import functools
import math

import jax
import jax.numpy as jnp
from jax import lax
from jax.experimental import pallas as pl
from jax.experimental.pallas import tpu as pltpu
from jax.sharding import PartitionSpec as P

F32 = jnp.float32
BF16 = jnp.bfloat16
AXES = ("view", "gauss")
LOW = 256
GROUP = 16
FAN = 4
NT = (((1,), (1,)), ((), ()))
TN = (((0,), (0,)), ((), ()))
HBM = pl.BlockSpec(memory_space=pltpu.HBM)
VMEM = pl.BlockSpec(memory_space=pltpu.VMEM)
SMEM = pl.BlockSpec(memory_space=pltpu.SMEM)


def params(mebibytes):
    return pltpu.CompilerParams(vmem_limit_bytes=mebibytes * 1024 * 1024)


def mm(left, right, dims=(((1,), (0,)), ((), ()))):
    return lax.dot_general(left, right, dims, preferred_element_type=F32)


def divisor(total, choices):
    for choice in choices:
        if total % choice == 0:
            return choice
    return total


def scatter_kernel(first_row, rows, viewers, view_ref, grads_ref, ids_ref, out_ref, acc_ref, left_ref):
    entries = ids_ref.shape[1]
    step = left_ref.shape[1]
    height = out_ref.shape[1]
    blocks = acc_ref.shape[0] // height
    groups = height // GROUP
    low_rows = lax.broadcasted_iota(jnp.int32, (LOW, step), 0).astype(F32).astype(BF16)
    one = jnp.ones((), BF16)
    zero = jnp.zeros((), BF16)

    def chunk(index, carry):
        spot = pl.ds(pl.multiple_of(index * step, step), step)
        ids = ids_ref[0:1, spot]
        high = lax.shift_right_logical(ids, 8).astype(F32).astype(BF16)
        low = lax.bitwise_and(ids, LOW - 1).astype(F32).astype(BF16)
        hot = jnp.where(low_rows == low, one, zero)
        high = jnp.broadcast_to(high, (GROUP, step))
        for group in range(groups):
            begin = first_row + group * GROUP
            count = min(GROUP, first_row + rows - begin)
            piece = grads_ref[0, begin : begin + count, spot]
            if count < GROUP:
                piece = jnp.concatenate(
                    [piece.astype(F32), jnp.zeros((GROUP - count, step), F32)], axis=0
                ).astype(BF16)
            for block in range(blocks):
                place = block * height + group * GROUP
                left_ref[place : place + GROUP, :] = jnp.where(high == jnp.asarray(block, BF16), piece, zero)
        product = mm(left_ref[...], hot, NT)

        @pl.when(index == 0)
        def _():
            acc_ref[...] = product

        @pl.when(index != 0)
        def _():
            acc_ref[...] += product

        return carry

    lax.fori_loop(0, entries // step, chunk, 0)
    per = blocks // viewers
    for block in range(blocks):
        slot = lax.rem(block // per - view_ref[0] + viewers, viewers)
        out_ref[slot, :, (block % per) * LOW : (block % per + 1) * LOW] = acc_ref[
            block * height : (block + 1) * height, :
        ].astype(BF16)


def scatter(view, entry_grads, vis_ids, first_row, rows, members, viewers):
    height = -(-rows // GROUP) * GROUP
    blocks = members * viewers // LOW
    step = divisor(vis_ids.shape[1], (2560, 2048, 1024, 512, 256, 128))
    return pl.pallas_call(
        functools.partial(scatter_kernel, first_row, rows, viewers),
        out_shape=jax.ShapeDtypeStruct((viewers, height, members), BF16),
        in_specs=[SMEM, VMEM, VMEM],
        out_specs=VMEM,
        scratch_shapes=[pltpu.VMEM((blocks * height, LOW), F32), pltpu.VMEM((blocks * height, step), BF16)],
        compiler_params=params(16),
    )(view, entry_grads, vis_ids)


def entry_kernel(viewers, count, view_ref, *refs):
    sources, out_ref, targets = refs[:count], refs[count], refs[count + 1 : 2 * count + 1]
    acc_ref, left_ref, rows_ref, sems = refs[2 * count + 1 :]
    copies = [
        pltpu.make_async_copy(source, target, sems.at[index])
        for index, (source, target) in enumerate(zip(sources, targets))
    ]
    early = pltpu.make_async_copy(sources[1].at[:, 0:GROUP, :], rows_ref, sems.at[count])
    copies[0].start()
    early.start()
    for copy in copies[1:]:
        copy.start()
    copies[0].wait()
    early.wait()
    scatter_kernel(0, GROUP, viewers, view_ref, rows_ref, targets[0], out_ref, acc_ref, left_ref)
    for copy in copies[1:]:
        copy.wait()


def entry(view, arrays, members, viewers):
    blocks = members * viewers // LOW
    step = divisor(arrays[0].shape[1], (2560, 2048, 1024, 512, 256, 128))
    count = len(arrays)
    results = pl.pallas_call(
        functools.partial(entry_kernel, viewers, count),
        out_shape=(
            jax.ShapeDtypeStruct((viewers, GROUP, members), BF16),
            *(jax.ShapeDtypeStruct(value.shape, value.dtype) for value in arrays),
        ),
        in_specs=[SMEM] + [HBM] * count,
        out_specs=(VMEM,) * (count + 1),
        scratch_shapes=[
            pltpu.VMEM((blocks * GROUP, LOW), F32),
            pltpu.VMEM((blocks * GROUP, step), BF16),
            pltpu.VMEM((1, GROUP, arrays[0].shape[1]), BF16),
            pltpu.SemaphoreType.DMA((count + 1,)),
        ],
        compiler_params=params(16),
    )(view, *(pltpu.with_memory_space_constraint(value, pltpu.HBM) for value in arrays))
    return results[0], results[1:]


def two_parts(value):
    top = value.astype(BF16)
    return top, value - top.astype(F32)


def forward_kernel(
    feats_ref,
    code_ref,
    subj_ref,
    bone_ids_ref,
    skin_ref,
    canon_ref,
    table_ref,
    first_ref,
    second_ref,
    third_ref,
    bias_ref,
    head_ref,
    inputs_out,
    act_one_out,
    act_two_out,
    act_three_out,
    slope_one_out,
    slope_two_out,
    slope_three_out,
    point_out,
    matrix_out,
    blend_out,
    bone_out,
    head_s,
    bias_s,
    table_s,
):
    width, members = feats_ref.shape
    subjects = code_ref.shape[0]
    table_cols = table_ref.shape[1]
    per_subject = table_cols // subjects
    influence = bone_ids_ref.shape[0]
    padded = bone_out.shape[0]
    pieces = table_s.shape[1] // 128

    head_s[...] = jnp.zeros_like(head_s)
    head_s[0:3, :] = head_ref[...].astype(F32)
    head_w = head_s[...].astype(BF16)
    bias_s[...] = jnp.zeros_like(bias_s)
    bias_s[0:3, :] = bias_ref[...]
    bias_cols = bias_s[...].T
    table_s[...] = jnp.zeros_like(table_s)
    table_s[0:12, 0:table_cols] = table_ref[...]
    code = code_ref[...]
    code_hi, code_rest = two_parts(code)
    code_mid, code_lo = two_parts(code_rest)
    code_w = jnp.concatenate([code_hi.astype(F32), code_mid.astype(F32), code_lo], axis=0).T.astype(BF16)

    subject = subj_ref[0:1, :]
    hot_rows = lax.broadcasted_iota(jnp.int32, (3 * subjects, members), 0) % subjects
    hot = (hot_rows == subject).astype(F32).astype(BF16)
    x = (feats_ref[...].astype(F32) + mm(code_w, hot)).astype(BF16)
    inputs_out[0:width, :] = x
    inputs_out[width : width + 16, :] = hot[0:16]
    layers = (
        (first_ref, act_one_out, slope_one_out),
        (second_ref, act_two_out, slope_two_out),
        (third_ref, act_three_out, slope_three_out),
    )
    half = jnp.asarray(0.5, BF16)
    source = inputs_out
    for layer, (weight, act_out, slope_out) in enumerate(layers):
        halved = weight[...] * half
        bias = 0.5 * bias_cols[:, layer : layer + 1]
        for lane in range(0, members, LOW):
            tile = slice(lane, lane + LOW)
            pre = mm(halved, source[0:width, tile]) + bias
            turn = jnp.tanh(pre)
            more = 1.0 + turn
            value = pre * more
            act_out[:, tile] = value.astype(BF16)
            slope_out[:, tile] = more + value * (1.0 - turn)
        source = act_out
    act = act_three_out[...]
    moved = mm(head_w, act)
    for axis in range(3):
        point_out[axis : axis + 1, :] = canon_ref[axis] + moved[axis : axis + 1]
    point_out[3:4, :] = jnp.ones((1, members), F32)

    bone_rows = lax.broadcasted_iota(jnp.int32, (padded, members), 0)
    spread = jnp.zeros((padded, members), F32)
    for member in range(influence):
        chosen = bone_ids_ref[member]
        spread = spread + jnp.where(bone_rows == chosen, skin_ref[member], 0.0)
    bone_out[...] = spread.astype(BF16)

    for tile in range(members // 128):
        lanes = slice(tile * 128, (tile + 1) * 128)
        base = subj_ref[0:1, lanes] * per_subject
        blend = [jnp.zeros((8, 128), F32), jnp.zeros((8, 128), F32)]
        for member in range(influence):
            column = jnp.broadcast_to(base + bone_ids_ref[member, :, lanes], (8, 128))
            within = lax.bitwise_and(column, 127)
            weight = skin_ref[member, :, lanes]
            for part in range(2):
                rows = slice(part * 8, part * 8 + 8)
                matrix = jnp.take_along_axis(table_s[rows, 0:128], within, axis=1, mode="promise_in_bounds")
                for piece in range(1, pieces):
                    other = jnp.take_along_axis(
                        table_s[rows, piece * 128 : (piece + 1) * 128], within, axis=1, mode="promise_in_bounds"
                    )
                    matrix = jnp.where(column >= piece * 128, other, matrix)
                matrix_out[member, rows, lanes] = matrix
                blend[part] = blend[part] + weight * matrix
        blend_out[0:8, lanes] = blend[0]
        blend_out[8:16, lanes] = blend[1]


def forward(feats, code, subj, bone_ids, skin, canon, table, w1, w2, w3, bias, head):
    width, members = feats.shape
    influence = bone_ids.shape[0]
    subjects = code.shape[0]
    table_cols = table.shape[1]
    padded = -(-(table_cols // subjects) // 16) * 16
    act = jax.ShapeDtypeStruct((width, members), BF16)
    slope = jax.ShapeDtypeStruct((width, members), F32)
    return pl.pallas_call(
        forward_kernel,
        out_shape=(
            jax.ShapeDtypeStruct((width + 16, members), BF16),
            act,
            act,
            act,
            slope,
            slope,
            slope,
            jax.ShapeDtypeStruct((4, members), F32),
            jax.ShapeDtypeStruct((influence, 16, members), F32),
            jax.ShapeDtypeStruct((16, members), F32),
            jax.ShapeDtypeStruct((padded, members), BF16),
        ),
        in_specs=[VMEM] * 12,
        out_specs=(VMEM,) * 11,
        scratch_shapes=[
            pltpu.VMEM((16, width), F32),
            pltpu.VMEM((8, width), F32),
            pltpu.VMEM((16, -(-table_cols // 128) * 128), F32),
        ],
        compiler_params=params(16),
    )(feats, code, subj, bone_ids, skin, canon, table, w1, w2, w3, bias, head)


def block_rows(width):
    return -(-(3 * width + 48) // (2 * FAN * 16)) * 16


def split_blocks(side, quarter, total_s, mine_out, theirs_out, factor):
    rows = mine_out.shape[1]
    for core, out in ((side, mine_out), (1 - side, theirs_out)):
        for slot in range(FAN):
            place = (core * FAN + lax.bitwise_xor(quarter, slot)) * rows
            out[slot] = (total_s[pl.ds(pl.multiple_of(place, 16), rows), :] * factor).astype(BF16)


def lane_sums(value):
    total = value[:, 0:128]
    for lane in range(128, value.shape[1], 128):
        total = total + value[:, lane : lane + 128]
    return jnp.sum(total.T, axis=0, keepdims=True)


def backward_kernel(factor, subjects, per_subject, got, *refs):
    (side_ref, quarter_ref, pos_ref), refs = refs[:3], refs[3:]
    got_refs, refs = refs[:got], refs[got:]
    (
        point_ref,
        blend_ref,
        bone_ref,
        subj_ref,
        inputs_ref,
        act_one_ref,
        act_two_ref,
        act_three_ref,
        slope_one_ref,
        slope_two_ref,
        slope_three_ref,
        first_ref,
        second_ref,
        third_ref,
        head_ref,
        outer_out,
        back_out,
        mine_out,
        theirs_out,
        total_s,
        head_s,
        masked_s,
    ) = refs
    width, members = act_one_ref.shape
    small = 3 * width

    head_s[...] = jnp.zeros_like(head_s)
    head_s[0:3, :] = head_ref[...].astype(F32)
    head_w = head_s[...].astype(BF16)
    total_s[small:, :] = jnp.zeros((total_s.shape[0] - small, width), F32)
    grad = pos_ref[0].astype(F32)
    for ref in got_refs:
        grad = grad + ref[...].astype(F32)
    rows = lax.broadcasted_iota(jnp.int32, (16, members), 0)
    quarter = rows // 4
    place = rows % 4
    grad_rows = jnp.where(
        quarter == 0,
        grad[0:1],
        jnp.where(quarter == 1, grad[1:2], jnp.where(quarter == 2, grad[2:3], 0.0)),
    )
    point = point_ref[...]
    point_rows = jnp.where(
        place == 0, point[0:1], jnp.where(place == 1, point[1:2], jnp.where(place == 2, point[2:3], point[3:4]))
    )
    outer = grad_rows * point_rows
    outer_out[...] = outer
    pulled = blend_ref[...] * grad_rows
    shift = pulled[0:4] + pulled[4:8] + pulled[8:12]
    shift = jnp.where(rows[0:4] < 3, shift, 0.0)
    shift = jnp.concatenate([shift, jnp.zeros((12, members), F32)], axis=0).astype(BF16)

    outer = outer.astype(BF16)
    subject = jnp.broadcast_to(subj_ref[...].astype(F32).astype(BF16), (16, members))
    zero = jnp.zeros((), BF16)
    for s in range(subjects):
        masked_s[16 * s : 16 * s + 16, :] = jnp.where(subject == jnp.asarray(s, BF16), outer, zero)
    product = mm(masked_s[...], bone_ref[...], NT)
    for s in range(subjects):
        columns = slice(s * per_subject, (s + 1) * per_subject)
        total_s[small + 16 : small + 32, columns] = product[16 * s : 16 * s + 16, 0:per_subject]

    half = jnp.asarray(0.5, BF16)
    back = mm(head_w * half, shift, TN) * slope_three_ref[...]
    total_s[small + 5 : small + 6, :] = lane_sums(back)
    back = back.astype(BF16)
    total_s[0:width, :] = mm(back, act_two_ref[...], NT)
    total_s[small : small + 3, :] = mm(shift, act_three_ref[...], NT)[0:3]
    back = mm(third_ref[...] * half, back, TN) * slope_two_ref[...]
    total_s[small + 4 : small + 5, :] = lane_sums(back)
    back = back.astype(BF16)
    total_s[width : 2 * width, :] = mm(back, act_one_ref[...], NT)
    back = (mm(second_ref[...] * half, back, TN) * slope_one_ref[...]).astype(BF16)
    back_out[...] = back
    product = mm(inputs_ref[...], back, NT)
    total_s[2 * width : 3 * width, :] = product[0:width].T
    by_subject = product[width : width + subjects]
    total_s[small + 3 : small + 4, :] = jnp.sum(by_subject, axis=0, keepdims=True)
    by_hi, by_rest = two_parts(by_subject)
    by_mid, by_lo = two_parts(by_rest)
    by_parts = jnp.concatenate([by_hi.astype(F32), by_mid.astype(F32), by_lo], axis=0).astype(BF16)
    code = mm(by_parts, first_ref[...])
    total_s[small + 32 : small + 32 + subjects, :] = (
        code[0:subjects] + code[subjects : 2 * subjects] + code[2 * subjects : 3 * subjects]
    )

    split_blocks(side_ref[0], quarter_ref[0], total_s, mine_out, theirs_out, factor)


def backward(side, quarter, pos, got, forwarded, subj, weights, head, factor, subjects, per_subject):
    inputs, act_one, act_two, act_three, *slopes, point, _, blend, bone = forwarded
    width, members = act_one.shape
    rows = block_rows(width)
    part = jax.ShapeDtypeStruct((FAN, rows, width), BF16)
    return pl.pallas_call(
        functools.partial(backward_kernel, factor, subjects, per_subject, len(got)),
        out_shape=(
            jax.ShapeDtypeStruct((16, members), F32),
            jax.ShapeDtypeStruct((width, members), BF16),
            part,
            part,
        ),
        in_specs=[SMEM] * 2 + [VMEM] * (16 + len(got)),
        out_specs=(VMEM,) * 4,
        scratch_shapes=[
            pltpu.VMEM((2 * FAN * rows, width), F32),
            pltpu.VMEM((16, width), F32),
            pltpu.VMEM((16 * subjects, members), BF16),
        ],
        compiler_params=params(24),
    )(
        side,
        quarter,
        pos,
        *got,
        point,
        blend,
        bone,
        subj,
        inputs,
        act_one,
        act_two,
        act_three,
        *slopes,
        *weights,
        head,
    )


def gaussian_kernel(back_ref, first_ref, outer_ref, matrix_ref, feat_out, skin_out):
    feat_out[...] = mm(first_ref[...], back_ref[...], TN).astype(BF16)
    outer = outer_ref[...]
    for member in range(matrix_ref.shape[0]):
        skin_out[member] = jnp.sum(outer * matrix_ref[member], axis=0, keepdims=True)


def gaussian_grads(back, w1, outer, matrix):
    width, members = back.shape
    influence = matrix.shape[0]
    return pl.pallas_call(
        gaussian_kernel,
        out_shape=(
            jax.ShapeDtypeStruct((width, members), BF16),
            jax.ShapeDtypeStruct((influence, 1, members), F32),
        ),
        in_specs=[VMEM] * 4,
        out_specs=(VMEM,) * 2,
        compiler_params=params(16),
    )(back, w1, outer, matrix)


def finish_kernel(side_ref, quarter_ref, *refs):
    mine_refs, refs = refs[:FAN], refs[FAN:]
    theirs_ref, first_out, second_out, third_out, bias_out, head_out, code_out, bone_out, total_s = refs
    width = third_out.shape[0]
    table_cols = bone_out.shape[1]
    subjects = code_out.shape[0]
    rows = mine_refs[0].shape[0]
    side = side_ref[0]
    for slot in range(FAN):
        place = lax.bitwise_xor(quarter_ref[0], slot)
        mine = pl.multiple_of((side * FAN + place) * rows, 16)
        theirs = pl.multiple_of(((1 - side) * FAN + place) * rows, 16)
        total_s[pl.ds(mine, rows), :] = mine_refs[slot][...].astype(F32)
        total_s[pl.ds(theirs, rows), :] = theirs_ref[slot * rows : (slot + 1) * rows, :].astype(F32)
    third_out[...] = total_s[0:width, :]
    second_out[...] = total_s[width : 2 * width, :]
    first_out[...] = total_s[2 * width : 3 * width, :]
    small = total_s[3 * width : 3 * width + 48, :]
    head_out[...] = small[0:3]
    bias_out[...] = small[3:6]
    bone_out[...] = small[16:28, 0:table_cols]
    code_out[...] = small[32 : 32 + subjects]


def finish(side, quarter, mine, theirs, subjects, table_cols):
    rows, width = mine[0].shape
    square = jax.ShapeDtypeStruct((width, width), F32)
    lines = jax.ShapeDtypeStruct((3, width), F32)
    return pl.pallas_call(
        finish_kernel,
        out_shape=(
            square,
            square,
            square,
            lines,
            lines,
            jax.ShapeDtypeStruct((subjects, width), F32),
            jax.ShapeDtypeStruct((12, table_cols), F32),
        ),
        in_specs=[SMEM] * 2 + [VMEM] * (FAN + 1),
        out_specs=(VMEM,) * 7,
        scratch_shapes=[pltpu.VMEM((2 * FAN * rows, width), F32)],
        compiler_params=params(16),
    )(side, quarter, *mine, theirs)


def attr_kernel(count, *refs):
    out_ref = refs[-1]
    attrs = out_ref.shape[0]
    row = 0
    for start in (0, count):
        total = refs[start][0].astype(F32)
        for ref in refs[start + 1 : start + count]:
            total = total + ref[...].astype(F32)
        for place in range(min(total.shape[0], attrs - row)):
            out_ref[row + place] = total[place : place + 1]
        row += total.shape[0]


def attr_sum(position, position_got, others, others_got, attrs):
    members = position.shape[2]
    count = 1 + len(position_got)
    return pl.pallas_call(
        functools.partial(attr_kernel, count),
        out_shape=jax.ShapeDtypeStruct((attrs, 1, members), F32),
        in_specs=[VMEM] * (2 * count),
        out_specs=VMEM,
        compiler_params=params(16),
    )(position, *position_got, others, *others_got)


def add(left, right):
    return (left.astype(F32) + right.astype(F32)).astype(BF16)


def swap(value, mask, count):
    return lax.ppermute(value, AXES, [(place, place ^ mask) for place in range(count)])


def tied(values, others):
    held = lax.optimization_barrier((tuple(values), tuple(others)))
    return list(held[0]), list(held[1])


def sum_over_devices(mine, theirs, viewers, shards, between):
    count = viewers * shards
    pair = shards
    rows, width = mine.shape[1:]
    masks = [1 << bit for bit in range(count.bit_length() - 1) if 1 << bit >= FAN and 1 << bit != pair]

    def work(stage, after, got):
        for item in between.get(stage, ()):
            got[0] = item(after, got[0])
        return got

    arrived = swap(theirs, pair, count)
    blocks = [add(mine[slot], arrived[slot]) for slot in range(FAN)]
    got = [swap(blocks[slot], slot, count) for slot in range(1, FAN)]
    got = work("scatter", blocks[0], got)
    total = sum((value.astype(F32) for value in got), blocks[0].astype(F32)).astype(BF16)
    for stage, mask in enumerate(masks):
        got = work(stage, total, [swap(total, mask, count)])
        total = add(total, got[0])
    got = [swap(total, slot, count) for slot in range(1, FAN)]
    got = work("gather", total, got)
    mine = [total, *got]
    theirs = swap(jnp.concatenate(mine, axis=0), pair, count)
    return mine, theirs


class Work:
    def __init__(self, call, *operands):
        self.call = call
        self.operands = operands
        self.results = None

    def __call__(self, after, before):
        operands, _ = tied(self.operands, [after])
        results = self.call(*operands)
        self.results, held = tied(results, [before])
        return held[0]


def received(parts, viewers):
    got = []
    for away in range(1, viewers):
        perm = [(place, (place + away) % viewers) for place in range(viewers)]
        got.append(lax.ppermute(parts[away], "view", perm))
    return got


def body(
    entry_grads,
    vis_ids,
    feats,
    code_tab,
    subj_ids,
    bone_ids,
    skin_w,
    canon_pos,
    bone_tf,
    w_first,
    w_second,
    w_third,
    biases,
    w_head,
):
    members = feats.shape[2]
    viewers = lax.axis_size("view")
    shards = lax.axis_size("gauss")
    attrs = entry_grads.shape[1]
    subjects = code_tab.shape[1]
    table_cols = bone_tf.shape[1]
    factor = 1.0 / math.sqrt(members * viewers * shards)
    view = lax.axis_index("view").astype(jnp.int32).reshape(1)
    side = lax.bitwise_and(view, 1)
    quarter = lax.bitwise_and(lax.axis_index("gauss").astype(jnp.int32).reshape(1), FAN - 1)
    position, arrays = entry(
        view,
        (
            vis_ids,
            entry_grads,
            feats[:, 0],
            code_tab.T,
            subj_ids,
            bone_ids,
            skin_w,
            canon_pos,
            bone_tf,
            w_first,
            w_second,
            w_third,
            biases,
            w_head,
        ),
        members,
        viewers,
    )
    vis_ids, entry_grads, *arrays = arrays
    subj_ids, weights, w_head = arrays[2], arrays[7:10], arrays[11]
    position_got = received(position, viewers)
    forwarded = forward(*arrays)
    outer, back_one, mine, theirs = backward(
        side,
        quarter,
        position,
        position_got,
        forwarded,
        subj_ids,
        weights,
        w_head,
        factor,
        subjects,
        table_cols // subjects,
    )

    def scatter_rows(row):
        def call(grads, ids):
            return [scatter(view, grads, ids, row, min(GROUP, attrs - row), members, viewers)]

        return Work(call, entry_grads, vis_ids)

    works = [scatter_rows(row) for row in range(GROUP, attrs, GROUP)]
    per_gaussian = Work(gaussian_grads, back_one, weights[0], outer, forwarded[8])

    def attributes(_):
        others = jnp.concatenate([work.results[0] for work in works], axis=1)
        others_got = received(others, viewers)
        return [attr_sum(position, position_got, others, others_got, attrs)]

    last = Work(attributes, view)
    between = {"scatter": works[:2], 0: works[2:], 1: [per_gaussian], "gather": [last]}
    mine, theirs = sum_over_devices(mine, theirs, viewers, shards, between)
    attr = last.results[0]
    feat_grads, skin_grads = per_gaussian.results
    first, second, third, bias, head, code, bone = finish(side, quarter, mine, theirs, subjects, table_cols)
    return (
        attr,
        feat_grads[:, None, :],
        skin_grads,
        first,
        second,
        third,
        bias,
        head,
        code.T,
        bone,
    )


def solution(mesh):
    placed = (
        P("view", None, "gauss"),
        P("view", "gauss"),
        P(None, "gauss", "view"),
        P(),
        P("gauss", "view"),
        P(None, "gauss", "view"),
        P(None, "gauss", "view"),
        P(None, "gauss", "view"),
        P(),
        P(),
        P(),
        P(),
        P(),
        P(),
    )
    return jax.shard_map(
        body,
        mesh=mesh,
        in_specs=placed,
        out_specs=(
            P(None, "gauss", "view"),
            P(None, "gauss", "view"),
            P(None, "gauss", "view"),
            P(),
            P(),
            P(),
            P(),
            P(),
            P(),
            P(),
        ),
        check_vma=False,
    )
```

```python
import functools
import math

import jax
import jax.numpy as jnp
from jax import lax
from jax.experimental import pallas as pl
from jax.experimental.pallas import tpu as pltpu
from jax.sharding import PartitionSpec as P

F32 = jnp.float32
BF16 = jnp.bfloat16
AXES = ("view", "gauss")
LOW = 256
GROUP = 16
BAND = 32
SMALL = 8
FAN = 4
NT = (((1,), (1,)), ((), ()))
TN = (((0,), (0,)), ((), ()))
HBM = pl.BlockSpec(memory_space=pltpu.HBM)
VMEM = pl.BlockSpec(memory_space=pltpu.VMEM)
SMEM = pl.BlockSpec(memory_space=pltpu.SMEM)


def params(mebibytes):
    return pltpu.CompilerParams(vmem_limit_bytes=mebibytes * 1024 * 1024)


def mm(left, right, dims=(((1,), (0,)), ((), ()))):
    return lax.dot_general(left, right, dims, preferred_element_type=F32)


def divisor(total, choices):
    for choice in choices:
        if total % choice == 0:
            return choice
    return total


def entry_step(entries, rows):
    fitting = [step for step in (2560, 1280, 1024, 512, 256, 128) if rows * step * 2 <= 8 << 20]
    return divisor(entries, fitting)


def scatter_kernel(first_row, rows, viewers, view_ref, grads_ref, ids_ref, out_ref, acc_ref, left_ref):
    entries = ids_ref.shape[1]
    step = left_ref.shape[1]
    height = out_ref.shape[1]
    blocks = acc_ref.shape[0] // height
    groups = height // GROUP
    low_rows = lax.broadcasted_iota(jnp.int32, (LOW, step), 0).astype(F32).astype(BF16)
    one = jnp.ones((), BF16)
    zero = jnp.zeros((), BF16)

    def chunk(index, carry):
        spot = pl.ds(pl.multiple_of(index * step, step), step)
        ids = ids_ref[0:1, spot]
        high = lax.shift_right_logical(ids, 8).astype(F32).astype(BF16)
        low = lax.bitwise_and(ids, LOW - 1).astype(F32).astype(BF16)
        hot = jnp.where(low_rows == low, one, zero)
        high = jnp.broadcast_to(high, (GROUP, step))
        for group in range(groups):
            begin = first_row + group * GROUP
            count = min(GROUP, first_row + rows - begin)
            piece = grads_ref[0, begin : begin + count, spot]
            if count < GROUP:
                piece = jnp.concatenate(
                    [piece.astype(F32), jnp.zeros((GROUP - count, step), F32)], axis=0
                ).astype(BF16)
            for block in range(blocks):
                place = block * height + group * GROUP
                left_ref[place : place + GROUP, :] = jnp.where(high == jnp.asarray(block, BF16), piece, zero)
        product = mm(left_ref[...], hot, NT)

        @pl.when(index == 0)
        def _():
            acc_ref[...] = product

        @pl.when(index != 0)
        def _():
            acc_ref[...] += product

        return carry

    lax.fori_loop(0, entries // step, chunk, 0)
    per = blocks // viewers
    for block in range(blocks):
        slot = lax.rem(block // per - view_ref[0] + viewers, viewers)
        out_ref[slot, :, (block % per) * LOW : (block % per + 1) * LOW] = acc_ref[
            block * height : (block + 1) * height, :
        ].astype(BF16)


def scatter(view, entry_grads, vis_ids, first_row, rows, members, viewers):
    height = -(-rows // GROUP) * GROUP
    blocks = members * viewers // LOW
    step = entry_step(vis_ids.shape[1], blocks * height)
    return pl.pallas_call(
        functools.partial(scatter_kernel, first_row, rows, viewers),
        out_shape=jax.ShapeDtypeStruct((viewers, height, members), BF16),
        in_specs=[SMEM, VMEM, VMEM],
        out_specs=VMEM,
        scratch_shapes=[pltpu.VMEM((blocks * height, LOW), F32), pltpu.VMEM((blocks * height, step), BF16)],
        compiler_params=params(16),
    )(view, entry_grads, vis_ids)


def position_kernel(viewers, view_ref, grads_ref, ids_ref, out_ref, acc_ref, left_ref, rows_ref):
    entries = ids_ref.shape[1]
    step = left_ref.shape[1]
    height = left_ref.shape[0] // 3
    blocks = out_ref.shape[2] * viewers // 128
    per = blocks // viewers
    high_rows = lax.broadcasted_iota(jnp.int32, (height, step), 0).astype(F32).astype(BF16)
    low_rows = lax.broadcasted_iota(jnp.int32, (128, step), 0).astype(F32).astype(BF16)
    one = jnp.ones((), BF16)
    zero = jnp.zeros((), BF16)

    def chunk(index, carry):
        spot = pl.ds(pl.multiple_of(index * step, step), step)
        ids = ids_ref[0:1, spot]
        high = lax.shift_right_logical(ids, 7).astype(F32).astype(BF16)
        low = lax.bitwise_and(ids, 127).astype(F32).astype(BF16)
        hot = jnp.where(low_rows == low, one, zero)
        inside = high_rows == high
        values = grads_ref[0, :, spot].astype(F32)
        for axis in range(3):
            value = jnp.broadcast_to(values[axis : axis + 1], (height, step)).astype(BF16)
            left_ref[axis * height : (axis + 1) * height, :] = jnp.where(inside, value, zero)
        product = mm(left_ref[...], hot, NT)

        @pl.when(index == 0)
        def _():
            acc_ref[...] = product

        @pl.when(index != 0)
        def _():
            acc_ref[...] += product

        return carry

    lax.fori_loop(0, entries // step, chunk, 0)
    rows_ref[...] = jnp.zeros_like(rows_ref)
    for block in range(blocks):
        slot = lax.rem(block // per - view_ref[0] + viewers, viewers)
        lanes = slice(block % per * 128, (block % per + 1) * 128)
        for axis in range(3):
            place = axis * height + block
            rows_ref[slot, axis : axis + 1, lanes] = acc_ref[place : place + 1, :]
    out_ref[...] = rows_ref[...].astype(BF16)


def entry_kernel(viewers, count, view_ref, *refs):
    sources, out_ref, targets = refs[:count], refs[count], refs[count + 1 : 2 * count + 1]
    acc_ref, left_ref, rows_ref, grads_ref, sems = refs[2 * count + 1 :]
    copies = [
        pltpu.make_async_copy(source, target, sems.at[index])
        for index, (source, target) in enumerate(zip(sources, targets))
    ]
    early = pltpu.make_async_copy(sources[1].at[:, 0:GROUP, :], grads_ref, sems.at[count])
    copies[0].start()
    early.start()
    for copy in copies[1:]:
        copy.start()
    copies[0].wait()
    early.wait()
    position_kernel(viewers, view_ref, grads_ref, targets[0], out_ref, acc_ref, left_ref, rows_ref)
    for copy in copies[1:]:
        copy.wait()


def entry(view, arrays, members, viewers):
    height = -(-(members * viewers // 128) // 16) * 16
    step = entry_step(arrays[0].shape[1], 3 * height)
    count = len(arrays)
    results = pl.pallas_call(
        functools.partial(entry_kernel, viewers, count),
        out_shape=(
            jax.ShapeDtypeStruct((viewers, GROUP, members), BF16),
            *(jax.ShapeDtypeStruct(value.shape, value.dtype) for value in arrays),
        ),
        in_specs=[SMEM] + [HBM] * count,
        out_specs=(VMEM,) * (count + 1),
        scratch_shapes=[
            pltpu.VMEM((3 * height, 128), F32),
            pltpu.VMEM((3 * height, step), BF16),
            pltpu.VMEM((viewers, GROUP, members), F32),
            pltpu.VMEM((1, GROUP, arrays[0].shape[1]), BF16),
            pltpu.SemaphoreType.DMA((count + 1,)),
        ],
        compiler_params=params(16),
    )(view, *(pltpu.with_memory_space_constraint(value, pltpu.HBM) for value in arrays))
    return results[0], results[1:]


def two_parts(value):
    top = value.astype(BF16)
    return top, value - top.astype(F32)


def forward_kernel(
    feats_ref,
    code_ref,
    subj_ref,
    bone_ids_ref,
    skin_ref,
    canon_ref,
    table_ref,
    first_ref,
    second_ref,
    third_ref,
    bias_ref,
    head_ref,
    inputs_out,
    act_one_out,
    act_two_out,
    act_three_out,
    slope_one_out,
    slope_two_out,
    slope_three_out,
    point_out,
    matrix_out,
    blend_out,
    bone_out,
    head_s,
    bias_s,
    table_s,
):
    width, members = feats_ref.shape
    subjects = code_ref.shape[0]
    table_cols = table_ref.shape[1]
    per_subject = table_cols // subjects
    influence = bone_ids_ref.shape[0]
    padded = bone_out.shape[0]
    pieces = table_s.shape[1] // 128

    head_s[...] = jnp.zeros_like(head_s)
    head_s[0:3, :] = head_ref[...].astype(F32)
    head_w = head_s[...].astype(BF16)
    bias_s[...] = jnp.zeros_like(bias_s)
    bias_s[0:3, :] = bias_ref[...]
    bias_cols = bias_s[...].T
    table_s[...] = jnp.zeros_like(table_s)
    table_s[0:12, 0:table_cols] = table_ref[...]
    code = code_ref[...]
    code_hi, code_rest = two_parts(code)
    code_mid, code_lo = two_parts(code_rest)
    code_w = jnp.concatenate([code_hi.astype(F32), code_mid.astype(F32), code_lo], axis=0).T.astype(BF16)

    subject = subj_ref[0:1, :]
    hot_rows = lax.broadcasted_iota(jnp.int32, (3 * subjects, members), 0) % subjects
    hot = (hot_rows == subject).astype(F32).astype(BF16)
    x = (feats_ref[...].astype(F32) + mm(code_w, hot)).astype(BF16)
    inputs_out[0:width, :] = x
    inputs_out[width : width + 16, :] = hot[0:16]
    layers = (
        (first_ref, act_one_out, slope_one_out),
        (second_ref, act_two_out, slope_two_out),
        (third_ref, act_three_out, slope_three_out),
    )
    half = jnp.asarray(0.5, BF16)
    source = inputs_out
    for layer, (weight, act_out, slope_out) in enumerate(layers):
        halved = weight[...] * half
        bias = 0.5 * bias_cols[:, layer : layer + 1]
        for lane in range(0, members, LOW):
            tile = slice(lane, lane + LOW)
            pre = mm(halved, source[0:width, tile]) + bias
            turn = jnp.tanh(pre)
            more = 1.0 + turn
            value = pre * more
            act_out[:, tile] = value.astype(BF16)
            slope_out[:, tile] = more + value * (1.0 - turn)
        source = act_out
    act = act_three_out[...]
    moved = mm(head_w, act)
    for axis in range(3):
        point_out[axis : axis + 1, :] = canon_ref[axis] + moved[axis : axis + 1]
    point_out[3:4, :] = jnp.ones((1, members), F32)

    bone_rows = lax.broadcasted_iota(jnp.int32, (padded, members), 0)
    spread = jnp.zeros((padded, members), F32)
    for member in range(influence):
        chosen = bone_ids_ref[member]
        spread = spread + jnp.where(bone_rows == chosen, skin_ref[member], 0.0)
    bone_out[...] = spread.astype(BF16)

    for tile in range(members // 128):
        lanes = slice(tile * 128, (tile + 1) * 128)
        base = subj_ref[0:1, lanes] * per_subject
        blend = [jnp.zeros((8, 128), F32), jnp.zeros((8, 128), F32)]
        for member in range(influence):
            column = jnp.broadcast_to(base + bone_ids_ref[member, :, lanes], (8, 128))
            within = lax.bitwise_and(column, 127)
            weight = skin_ref[member, :, lanes]
            for part in range(2):
                rows = slice(part * 8, part * 8 + 8)
                matrix = jnp.take_along_axis(table_s[rows, 0:128], within, axis=1, mode="promise_in_bounds")
                for piece in range(1, pieces):
                    other = jnp.take_along_axis(
                        table_s[rows, piece * 128 : (piece + 1) * 128], within, axis=1, mode="promise_in_bounds"
                    )
                    matrix = jnp.where(column >= piece * 128, other, matrix)
                matrix_out[member, rows, lanes] = matrix
                blend[part] = blend[part] + weight * matrix
        blend_out[0:8, lanes] = blend[0]
        blend_out[8:16, lanes] = blend[1]


def forward(feats, code, subj, bone_ids, skin, canon, table, w1, w2, w3, bias, head):
    width, members = feats.shape
    influence = bone_ids.shape[0]
    subjects = code.shape[0]
    table_cols = table.shape[1]
    padded = -(-(table_cols // subjects) // 16) * 16
    act = jax.ShapeDtypeStruct((width, members), BF16)
    slope = jax.ShapeDtypeStruct((width, members), F32)
    return pl.pallas_call(
        forward_kernel,
        out_shape=(
            jax.ShapeDtypeStruct((width + 16, members), BF16),
            act,
            act,
            act,
            slope,
            slope,
            slope,
            jax.ShapeDtypeStruct((4, members), F32),
            jax.ShapeDtypeStruct((influence, 16, members), F32),
            jax.ShapeDtypeStruct((16, members), F32),
            jax.ShapeDtypeStruct((padded, members), BF16),
        ),
        in_specs=[VMEM] * 12,
        out_specs=(VMEM,) * 11,
        scratch_shapes=[
            pltpu.VMEM((16, width), F32),
            pltpu.VMEM((8, width), F32),
            pltpu.VMEM((16, -(-table_cols // 128) * 128), F32),
        ],
        compiler_params=params(16),
    )(feats, code, subj, bone_ids, skin, canon, table, w1, w2, w3, bias, head)


def block_pieces(width):
    piece = width // (2 * FAN)
    return piece, 3 * piece + SMALL


def split_blocks(side, quarter, total_s, mine_out, theirs_out, factor):
    width = mine_out.shape[2]
    piece, rows = block_pieces(width)
    for core, out in ((side, mine_out), (1 - side, theirs_out)):
        for slot in range(FAN):
            place = core * FAN + lax.bitwise_xor(quarter, slot)
            for square in range(3):
                spot = pl.ds(pl.multiple_of(square * width + place * piece, 16), piece)
                out[slot, square * piece : (square + 1) * piece, :] = (total_s[spot, :] * factor).astype(BF16)
            spot = pl.ds(pl.multiple_of(3 * width + place * SMALL, SMALL), SMALL)
            out[slot, 3 * piece : rows, :] = (total_s[spot, :] * factor).astype(BF16)


def lane_sums(value):
    total = value[:, 0:128]
    for lane in range(128, value.shape[1], 128):
        total = total + value[:, lane : lane + 128]
    return jnp.sum(total.T, axis=0, keepdims=True)


def backward_kernel(factor, subjects, per_subject, got, *refs):
    (side_ref, quarter_ref, pos_ref), refs = refs[:3], refs[3:]
    got_refs, refs = refs[:got], refs[got:]
    (
        point_ref,
        blend_ref,
        bone_ref,
        subj_ref,
        inputs_ref,
        act_one_ref,
        act_two_ref,
        act_three_ref,
        slope_one_ref,
        slope_two_ref,
        slope_three_ref,
        first_ref,
        second_ref,
        third_ref,
        head_ref,
        outer_out,
        back_out,
        mine_out,
        theirs_out,
        total_s,
        head_s,
        masked_s,
    ) = refs
    width, members = act_one_ref.shape
    small = 3 * width

    head_s[...] = jnp.zeros_like(head_s)
    head_s[0:3, :] = head_ref[...].astype(F32)
    head_w = head_s[...].astype(BF16)
    total_s[small:, :] = jnp.zeros((total_s.shape[0] - small, width), F32)
    grad = pos_ref[0].astype(F32)
    for ref in got_refs:
        grad = grad + ref[...].astype(F32)
    rows = lax.broadcasted_iota(jnp.int32, (16, members), 0)
    quarter = rows // 4
    place = rows % 4
    grad_rows = jnp.where(
        quarter == 0,
        grad[0:1],
        jnp.where(quarter == 1, grad[1:2], jnp.where(quarter == 2, grad[2:3], 0.0)),
    )
    point = point_ref[...]
    point_rows = jnp.where(
        place == 0, point[0:1], jnp.where(place == 1, point[1:2], jnp.where(place == 2, point[2:3], point[3:4]))
    )
    outer = grad_rows * point_rows
    outer_out[...] = outer
    pulled = blend_ref[...] * grad_rows
    shift = pulled[0:4] + pulled[4:8] + pulled[8:12]
    shift = jnp.where(rows[0:4] < 3, shift, 0.0)
    shift = jnp.concatenate([shift, jnp.zeros((12, members), F32)], axis=0).astype(BF16)

    outer = outer.astype(BF16)
    subject = jnp.broadcast_to(subj_ref[...].astype(F32).astype(BF16), (16, members))
    zero = jnp.zeros((), BF16)
    for s in range(subjects):
        masked_s[16 * s : 16 * s + 16, :] = jnp.where(subject == jnp.asarray(s, BF16), outer, zero)
    product = mm(masked_s[...], bone_ref[...], NT)
    for s in range(subjects):
        columns = slice(s * per_subject, (s + 1) * per_subject)
        total_s[small + 8 : small + 24, columns] = product[16 * s : 16 * s + 16, 0:per_subject]

    half = jnp.asarray(0.5, BF16)
    back = mm(head_w * half, shift, TN) * slope_three_ref[...]
    total_s[small + 5 : small + 6, :] = lane_sums(back)
    back = back.astype(BF16)
    total_s[0:width, :] = mm(back, act_two_ref[...], NT)
    total_s[small : small + 3, :] = mm(shift, act_three_ref[...], NT)[0:3]
    back = mm(third_ref[...] * half, back, TN) * slope_two_ref[...]
    total_s[small + 4 : small + 5, :] = lane_sums(back)
    back = back.astype(BF16)
    total_s[width : 2 * width, :] = mm(back, act_one_ref[...], NT)
    back = (mm(second_ref[...] * half, back, TN) * slope_one_ref[...]).astype(BF16)
    back_out[...] = back
    product = mm(inputs_ref[...], back, NT)
    total_s[2 * width : 3 * width, :] = product[0:width].T
    by_subject = product[width : width + subjects]
    total_s[small + 3 : small + 4, :] = jnp.sum(by_subject, axis=0, keepdims=True)
    by_hi, by_rest = two_parts(by_subject)
    by_mid, by_lo = two_parts(by_rest)
    by_parts = jnp.concatenate([by_hi.astype(F32), by_mid.astype(F32), by_lo], axis=0).astype(BF16)
    code = mm(by_parts, first_ref[...])
    total_s[small + 24 : small + 24 + subjects, :] = (
        code[0:subjects] + code[subjects : 2 * subjects] + code[2 * subjects : 3 * subjects]
    )

    split_blocks(side_ref[0], quarter_ref[0], total_s, mine_out, theirs_out, factor)


def backward(side, quarter, pos, got, forwarded, subj, weights, head, factor, subjects, per_subject):
    inputs, act_one, act_two, act_three, *slopes, point, _, blend, bone = forwarded
    width, members = act_one.shape
    piece, rows = block_pieces(width)
    part = jax.ShapeDtypeStruct((FAN, rows, width), BF16)
    return pl.pallas_call(
        functools.partial(backward_kernel, factor, subjects, per_subject, len(got)),
        out_shape=(
            jax.ShapeDtypeStruct((16, members), F32),
            jax.ShapeDtypeStruct((width, members), BF16),
            part,
            part,
        ),
        in_specs=[SMEM] * 2 + [VMEM] * (16 + len(got)),
        out_specs=(VMEM,) * 4,
        scratch_shapes=[
            pltpu.VMEM((3 * width + 2 * FAN * SMALL, width), F32),
            pltpu.VMEM((16, width), F32),
            pltpu.VMEM((16 * subjects, members), BF16),
        ],
        compiler_params=params(24),
    )(
        side,
        quarter,
        pos,
        *got,
        point,
        blend,
        bone,
        subj,
        inputs,
        act_one,
        act_two,
        act_three,
        *slopes,
        *weights,
        head,
    )


def gaussian_kernel(back_ref, first_ref, outer_ref, matrix_ref, feat_out, skin_out):
    feat_out[...] = mm(first_ref[...], back_ref[...], TN).astype(BF16)
    outer = outer_ref[...]
    for member in range(matrix_ref.shape[0]):
        skin_out[member] = jnp.sum(outer * matrix_ref[member], axis=0, keepdims=True)


def gaussian_grads(back, w1, outer, matrix):
    width, members = back.shape
    influence = matrix.shape[0]
    return pl.pallas_call(
        gaussian_kernel,
        out_shape=(
            jax.ShapeDtypeStruct((width, members), BF16),
            jax.ShapeDtypeStruct((influence, 1, members), F32),
        ),
        in_specs=[VMEM] * 4,
        out_specs=(VMEM,) * 2,
        compiler_params=params(16),
    )(back, w1, outer, matrix)


def finish_kernel(side_ref, quarter_ref, *refs):
    mine_refs, refs = refs[:FAN], refs[FAN:]
    theirs_ref, *square_outs, bias_out, head_out, code_out, bone_out, small_s = refs
    piece, rows = block_pieces(theirs_ref.shape[1])
    for core in range(2):
        owner = side_ref[0] if core == 0 else 1 - side_ref[0]
        for slot in range(FAN):
            block = mine_refs[slot] if core == 0 else theirs_ref.at[slot * rows : (slot + 1) * rows]
            place = owner * FAN + lax.bitwise_xor(quarter_ref[0], slot)
            spot = pl.ds(pl.multiple_of(place * piece, piece), piece)
            for square, out in enumerate(square_outs):
                out[spot, :] = block[square * piece : (square + 1) * piece, :].astype(F32)
            spot = pl.ds(pl.multiple_of(place * SMALL, SMALL), SMALL)
            small_s[spot, :] = block[3 * piece : rows, :].astype(F32)
    small = small_s[...]
    head_out[...] = small[0:3]
    bias_out[...] = small[3:6]
    bone_out[...] = small[8:20, 0 : bone_out.shape[1]]
    code_out[...] = small[24 : 24 + code_out.shape[0]]


def finish(side, quarter, mine, theirs, subjects, table_cols):
    width = mine[0].shape[1]
    square = jax.ShapeDtypeStruct((width, width), F32)
    lines = jax.ShapeDtypeStruct((3, width), F32)
    third, second, first, *small = pl.pallas_call(
        finish_kernel,
        out_shape=(
            square,
            square,
            square,
            lines,
            lines,
            jax.ShapeDtypeStruct((subjects, width), F32),
            jax.ShapeDtypeStruct((12, table_cols), F32),
        ),
        in_specs=[SMEM] * 2 + [VMEM] * (FAN + 1),
        out_specs=(VMEM,) * 7,
        scratch_shapes=[pltpu.VMEM((2 * FAN * SMALL, width), F32)],
        compiler_params=params(16),
    )(side, quarter, *mine, theirs)
    return first, second, third, *small


def attr_kernel(groups, *refs):
    out_ref = refs[-1]
    count = (len(refs) - 1) // groups
    row = 0
    for start in range(0, groups * count, count):
        total = refs[start][0].astype(F32)
        for ref in refs[start + 1 : start + count]:
            total = total + ref[...].astype(F32)
        for place in range(min(total.shape[0], out_ref.shape[0] - row)):
            out_ref[row + place] = total[place : place + 1]
        row += total.shape[0]


def attr_sum(groups, attrs):
    members = groups[0][0].shape[2]
    operands = [value for group in groups for value in group]
    return pl.pallas_call(
        functools.partial(attr_kernel, len(groups)),
        out_shape=jax.ShapeDtypeStruct((attrs, 1, members), F32),
        in_specs=[VMEM] * len(operands),
        out_specs=VMEM,
        compiler_params=params(16),
    )(*operands)


def add(left, right):
    return (left.astype(F32) + right.astype(F32)).astype(BF16)


def swap(value, mask, count):
    return lax.ppermute(value, AXES, [(place, place ^ mask) for place in range(count)])


def tied(values, others):
    held = lax.optimization_barrier((tuple(values), tuple(others)))
    return list(held[0]), list(held[1])


def sum_over_devices(mine, theirs, viewers, shards, between):
    count = viewers * shards
    pair = shards
    rows, width = mine.shape[1:]
    masks = [1 << bit for bit in range(count.bit_length() - 1) if 1 << bit >= FAN and 1 << bit != pair]

    def work(stage, after, got):
        for item in between.get(stage, ()):
            got[0] = item(after, got[0])
        return got

    arrived = swap(theirs, pair, count)
    blocks = [add(mine[slot], arrived[slot]) for slot in range(FAN)]
    got = [swap(blocks[slot], slot, count) for slot in range(1, FAN)]
    got = work("scatter", blocks[0], got)
    total = sum((value.astype(F32) for value in got), blocks[0].astype(F32)).astype(BF16)
    for stage, mask in enumerate(masks):
        got = work(stage, total, [swap(total, mask, count)])
        total = add(total, got[0])
    got = [swap(total, slot, count) for slot in range(1, FAN)]
    got = work("gather", total, got)
    mine = [total, *got]
    theirs = swap(jnp.concatenate(mine, axis=0), pair, count)
    return mine, theirs


class Work:
    def __init__(self, call, *operands):
        self.call = call
        self.operands = operands
        self.results = None

    def __call__(self, after, before):
        operands, _ = tied(self.operands, [after])
        results = self.call(*operands)
        self.results, held = tied(results, [before])
        return held[0]


def received(parts, viewers):
    got = []
    for away in range(1, viewers):
        perm = [(place, (place + away) % viewers) for place in range(viewers)]
        got.append(lax.ppermute(parts[away], "view", perm))
    return got


def body(
    entry_grads,
    vis_ids,
    feats,
    code_tab,
    subj_ids,
    bone_ids,
    skin_w,
    canon_pos,
    bone_tf,
    w_first,
    w_second,
    w_third,
    biases,
    w_head,
):
    members = feats.shape[2]
    viewers = lax.axis_size("view")
    shards = lax.axis_size("gauss")
    attrs = entry_grads.shape[1]
    subjects = code_tab.shape[1]
    table_cols = bone_tf.shape[1]
    factor = 1.0 / math.sqrt(members * viewers * shards)
    view = lax.axis_index("view").astype(jnp.int32).reshape(1)
    side = lax.bitwise_and(view, 1)
    quarter = lax.bitwise_and(lax.axis_index("gauss").astype(jnp.int32).reshape(1), FAN - 1)
    position, arrays = entry(
        view,
        (
            vis_ids,
            entry_grads,
            feats[:, 0],
            code_tab.T,
            subj_ids,
            bone_ids,
            skin_w,
            canon_pos,
            bone_tf,
            w_first,
            w_second,
            w_third,
            biases,
            w_head,
        ),
        members,
        viewers,
    )
    vis_ids, entry_grads, *arrays = arrays
    subj_ids, weights, w_head = arrays[2], arrays[7:10], arrays[11]
    position_got = received(position, viewers)
    forwarded = forward(*arrays)
    outer, back_one, mine, theirs = backward(
        side,
        quarter,
        position,
        position_got,
        forwarded,
        subj_ids,
        weights,
        w_head,
        factor,
        subjects,
        table_cols // subjects,
    )

    def scatter_rows(row):
        def call(grads, ids):
            return [scatter(view, grads, ids, row, min(BAND, attrs - row), members, viewers)]

        return Work(call, entry_grads, vis_ids)

    works = [scatter_rows(row) for row in range(0, attrs, BAND)]
    per_gaussian = Work(gaussian_grads, back_one, weights[0], outer, forwarded[8])

    def attributes(_):
        sums = [work.results[0] for work in works]
        return [attr_sum([[value, *received(value, viewers)] for value in sums], attrs)]

    last = Work(attributes, view)
    between = {"scatter": works[:1], 0: works[1:], 1: [per_gaussian], "gather": [last]}
    mine, theirs = sum_over_devices(mine, theirs, viewers, shards, between)
    attr = last.results[0]
    feat_grads, skin_grads = per_gaussian.results
    first, second, third, bias, head, code, bone = finish(side, quarter, mine, theirs, subjects, table_cols)
    return (
        attr,
        feat_grads[:, None, :],
        skin_grads,
        first,
        second,
        third,
        bias,
        head,
        code.T,
        bone,
    )


def solution(mesh):
    placed = (
        P("view", None, "gauss"),
        P("view", "gauss"),
        P(None, "gauss", "view"),
        P(),
        P("gauss", "view"),
        P(None, "gauss", "view"),
        P(None, "gauss", "view"),
        P(None, "gauss", "view"),
        P(),
        P(),
        P(),
        P(),
        P(),
        P(),
    )
    return jax.shard_map(
        body,
        mesh=mesh,
        in_specs=placed,
        out_specs=(
            P(None, "gauss", "view"),
            P(None, "gauss", "view"),
            P(None, "gauss", "view"),
            P(),
            P(),
            P(),
            P(),
            P(),
            P(),
            P(),
        ),
        check_vma=False,
    )
```

```python
import functools
import math

import jax
import jax.numpy as jnp
from jax import lax
from jax.experimental import pallas as pl
from jax.experimental.pallas import tpu as pltpu
from jax.sharding import PartitionSpec as P

F32 = jnp.float32
BF16 = jnp.bfloat16
AXES = ("view", "gauss")
LOW = 256
GROUP = 16
BAND = 32
SMALL = 8
FAN = 4
NT = (((1,), (1,)), ((), ()))
TN = (((0,), (0,)), ((), ()))
HBM = pl.BlockSpec(memory_space=pltpu.HBM)
VMEM = pl.BlockSpec(memory_space=pltpu.VMEM)
SMEM = pl.BlockSpec(memory_space=pltpu.SMEM)


def params(mebibytes):
    return pltpu.CompilerParams(vmem_limit_bytes=mebibytes * 1024 * 1024)


def mm(left, right, dims=(((1,), (0,)), ((), ()))):
    return lax.dot_general(left, right, dims, preferred_element_type=F32)


def divisor(total, choices):
    for choice in choices:
        if total % choice == 0:
            return choice
    return total


def entry_step(entries, rows):
    fitting = [step for step in (2560, 1280, 1024, 512, 256, 128) if rows * step * 2 <= 8 << 20]
    return divisor(entries, fitting)


def scatter_kernel(first_row, rows, viewers, view_ref, grads_ref, ids_ref, out_ref, acc_ref, left_ref):
    entries = ids_ref.shape[1]
    step = left_ref.shape[1]
    height = out_ref.shape[1]
    blocks = acc_ref.shape[0] // height
    groups = height // GROUP
    low_rows = lax.broadcasted_iota(jnp.int32, (LOW, step), 0).astype(F32).astype(BF16)
    one = jnp.ones((), BF16)
    zero = jnp.zeros((), BF16)

    def chunk(index, carry):
        spot = pl.ds(pl.multiple_of(index * step, step), step)
        ids = ids_ref[0:1, spot]
        high = lax.shift_right_logical(ids, 8).astype(F32).astype(BF16)
        low = lax.bitwise_and(ids, LOW - 1).astype(F32).astype(BF16)
        hot = jnp.where(low_rows == low, one, zero)
        high = jnp.broadcast_to(high, (GROUP, step))
        for group in range(groups):
            begin = first_row + group * GROUP
            count = min(GROUP, first_row + rows - begin)
            piece = grads_ref[0, begin : begin + count, spot]
            if count < GROUP:
                piece = jnp.concatenate(
                    [piece.astype(F32), jnp.zeros((GROUP - count, step), F32)], axis=0
                ).astype(BF16)
            for block in range(blocks):
                place = block * height + group * GROUP
                left_ref[place : place + GROUP, :] = jnp.where(high == jnp.asarray(block, BF16), piece, zero)
        product = mm(left_ref[...], hot, NT)

        @pl.when(index == 0)
        def _():
            acc_ref[...] = product

        @pl.when(index != 0)
        def _():
            acc_ref[...] += product

        return carry

    lax.fori_loop(0, entries // step, chunk, 0)
    per = blocks // viewers
    for block in range(blocks):
        slot = lax.rem(block // per - view_ref[0] + viewers, viewers)
        out_ref[slot, :, (block % per) * LOW : (block % per + 1) * LOW] = acc_ref[
            block * height : (block + 1) * height, :
        ].astype(BF16)


def scatter(view, entry_grads, vis_ids, first_row, rows, members, viewers):
    height = -(-rows // GROUP) * GROUP
    blocks = members * viewers // LOW
    step = entry_step(vis_ids.shape[1], blocks * height)
    return pl.pallas_call(
        functools.partial(scatter_kernel, first_row, rows, viewers),
        out_shape=jax.ShapeDtypeStruct((viewers, height, members), BF16),
        in_specs=[SMEM, VMEM, VMEM],
        out_specs=VMEM,
        scratch_shapes=[pltpu.VMEM((blocks * height, LOW), F32), pltpu.VMEM((blocks * height, step), BF16)],
        compiler_params=params(16),
    )(view, entry_grads, vis_ids)


def position_kernel(viewers, view_ref, grads_ref, ids_ref, out_ref, acc_ref, left_ref, rows_ref):
    entries = ids_ref.shape[1]
    step = left_ref.shape[1]
    height = left_ref.shape[0] // 3
    blocks = out_ref.shape[2] * viewers // 128
    per = blocks // viewers
    high_rows = lax.broadcasted_iota(jnp.int32, (height, step), 0).astype(F32).astype(BF16)
    low_rows = lax.broadcasted_iota(jnp.int32, (128, step), 0).astype(F32).astype(BF16)
    one = jnp.ones((), BF16)
    zero = jnp.zeros((), BF16)

    def chunk(index, carry):
        spot = pl.ds(pl.multiple_of(index * step, step), step)
        ids = ids_ref[0:1, spot]
        high = lax.shift_right_logical(ids, 7).astype(F32).astype(BF16)
        low = lax.bitwise_and(ids, 127).astype(F32).astype(BF16)
        hot = jnp.where(low_rows == low, one, zero)
        inside = high_rows == high
        values = grads_ref[0, :, spot].astype(F32)
        for axis in range(3):
            value = jnp.broadcast_to(values[axis : axis + 1], (height, step)).astype(BF16)
            left_ref[axis * height : (axis + 1) * height, :] = jnp.where(inside, value, zero)
        product = mm(left_ref[...], hot, NT)

        @pl.when(index == 0)
        def _():
            acc_ref[...] = product

        @pl.when(index != 0)
        def _():
            acc_ref[...] += product

        return carry

    lax.fori_loop(0, entries // step, chunk, 0)
    rows_ref[...] = jnp.zeros_like(rows_ref)
    for block in range(blocks):
        slot = lax.rem(block // per - view_ref[0] + viewers, viewers)
        lanes = slice(block % per * 128, (block % per + 1) * 128)
        for axis in range(3):
            place = axis * height + block
            rows_ref[slot, axis : axis + 1, lanes] = acc_ref[place : place + 1, :]
    out_ref[...] = rows_ref[...].astype(BF16)


def entry_kernel(viewers, count, view_ref, *refs):
    sources, out_ref, targets = refs[:count], refs[count], refs[count + 1 : 2 * count + 1]
    acc_ref, left_ref, rows_ref, grads_ref, sems = refs[2 * count + 1 :]
    copies = [
        pltpu.make_async_copy(source, target, sems.at[index])
        for index, (source, target) in enumerate(zip(sources, targets))
    ]
    early = pltpu.make_async_copy(sources[1].at[:, 0:GROUP, :], grads_ref, sems.at[count])
    copies[0].start()
    early.start()
    for copy in copies[1:]:
        copy.start()
    copies[0].wait()
    early.wait()
    position_kernel(viewers, view_ref, grads_ref, targets[0], out_ref, acc_ref, left_ref, rows_ref)
    for copy in copies[1:]:
        copy.wait()


def entry(view, arrays, members, viewers):
    height = -(-(members * viewers // 128) // 16) * 16
    step = entry_step(arrays[0].shape[1], 3 * height)
    count = len(arrays)
    results = pl.pallas_call(
        functools.partial(entry_kernel, viewers, count),
        out_shape=(
            jax.ShapeDtypeStruct((viewers, GROUP, members), BF16),
            *(jax.ShapeDtypeStruct(value.shape, value.dtype) for value in arrays),
        ),
        in_specs=[SMEM] + [HBM] * count,
        out_specs=(VMEM,) * (count + 1),
        scratch_shapes=[
            pltpu.VMEM((3 * height, 128), F32),
            pltpu.VMEM((3 * height, step), BF16),
            pltpu.VMEM((viewers, GROUP, members), F32),
            pltpu.VMEM((1, GROUP, arrays[0].shape[1]), BF16),
            pltpu.SemaphoreType.DMA((count + 1,)),
        ],
        compiler_params=params(16),
    )(view, *(pltpu.with_memory_space_constraint(value, pltpu.HBM) for value in arrays))
    return results[0], results[1:]


def two_parts(value):
    top = value.astype(BF16)
    return top, value - top.astype(F32)


def forward_kernel(
    feats_ref,
    code_ref,
    subj_ref,
    bone_ids_ref,
    skin_ref,
    canon_ref,
    table_ref,
    first_ref,
    second_ref,
    third_ref,
    bias_ref,
    head_ref,
    inputs_out,
    act_one_out,
    act_two_out,
    act_three_out,
    slope_one_out,
    slope_two_out,
    slope_three_out,
    point_out,
    matrix_out,
    blend_out,
    bone_out,
    head_s,
    bias_s,
    table_s,
):
    width, members = feats_ref.shape
    subjects = code_ref.shape[0]
    table_cols = table_ref.shape[1]
    per_subject = table_cols // subjects
    influence = bone_ids_ref.shape[0]
    padded = bone_out.shape[0]
    pieces = table_s.shape[1] // 128

    head_s[...] = jnp.zeros_like(head_s)
    head_s[0:3, :] = head_ref[...].astype(F32)
    head_w = head_s[...].astype(BF16)
    bias_s[...] = jnp.zeros_like(bias_s)
    bias_s[0:3, :] = bias_ref[...]
    bias_cols = bias_s[...].T
    table_s[...] = jnp.zeros_like(table_s)
    table_s[0:12, 0:table_cols] = table_ref[...]
    code = code_ref[...]
    code_hi, code_rest = two_parts(code)
    code_mid, code_lo = two_parts(code_rest)
    code_w = jnp.concatenate([code_hi.astype(F32), code_mid.astype(F32), code_lo], axis=0).T.astype(BF16)

    subject = subj_ref[0:1, :]
    hot = (lax.broadcasted_iota(jnp.int32, (subjects, members), 0) == subject).astype(F32)
    hot = jnp.concatenate([hot, hot, hot], axis=0).astype(BF16)
    x = (feats_ref[...].astype(F32) + mm(code_w, hot)).astype(BF16)
    inputs_out[0:width, :] = x
    inputs_out[width : width + 16, :] = hot[0:16]
    layers = (
        (first_ref, act_one_out, slope_one_out),
        (second_ref, act_two_out, slope_two_out),
        (third_ref, act_three_out, slope_three_out),
    )
    half = jnp.asarray(0.5, BF16)
    source = inputs_out
    for layer, (weight, act_out, slope_out) in enumerate(layers):
        halved = weight[...] * half
        bias = 0.5 * bias_cols[:, layer : layer + 1]
        for lane in range(0, members, LOW):
            tile = slice(lane, lane + LOW)
            pre = mm(halved, source[0:width, tile]) + bias
            turn = jnp.tanh(pre)
            more = 1.0 + turn
            value = pre * more
            act_out[:, tile] = value.astype(BF16)
            slope_out[:, tile] = more + value * (1.0 - turn)
        source = act_out
    act = act_three_out[...]
    moved = mm(head_w, act)
    for axis in range(3):
        point_out[axis : axis + 1, :] = canon_ref[axis] + moved[axis : axis + 1]
    point_out[3:4, :] = jnp.ones((1, members), F32)

    bone_rows = lax.broadcasted_iota(jnp.int32, (padded, members), 0)
    spread = jnp.zeros((padded, members), F32)
    for member in range(influence):
        chosen = bone_ids_ref[member]
        spread = spread + jnp.where(bone_rows == chosen, skin_ref[member], 0.0)
    bone_out[...] = spread.astype(BF16)

    for tile in range(members // 128):
        lanes = slice(tile * 128, (tile + 1) * 128)
        base = subj_ref[0:1, lanes] * per_subject
        blend = [jnp.zeros((8, 128), F32), jnp.zeros((8, 128), F32)]
        for member in range(influence):
            column = jnp.broadcast_to(base + bone_ids_ref[member, :, lanes], (8, 128))
            within = lax.bitwise_and(column, 127)
            weight = skin_ref[member, :, lanes]
            for part in range(2):
                rows = slice(part * 8, part * 8 + 8)
                matrix = jnp.take_along_axis(table_s[rows, 0:128], within, axis=1, mode="promise_in_bounds")
                for piece in range(1, pieces):
                    other = jnp.take_along_axis(
                        table_s[rows, piece * 128 : (piece + 1) * 128], within, axis=1, mode="promise_in_bounds"
                    )
                    matrix = jnp.where(column >= piece * 128, other, matrix)
                matrix_out[member, rows, lanes] = matrix
                blend[part] = blend[part] + weight * matrix
        blend_out[0:8, lanes] = blend[0]
        blend_out[8:16, lanes] = blend[1]


def forward(feats, code, subj, bone_ids, skin, canon, table, w1, w2, w3, bias, head):
    width, members = feats.shape
    influence = bone_ids.shape[0]
    subjects = code.shape[0]
    table_cols = table.shape[1]
    padded = -(-(table_cols // subjects) // 16) * 16
    act = jax.ShapeDtypeStruct((width, members), BF16)
    slope = jax.ShapeDtypeStruct((width, members), F32)
    return pl.pallas_call(
        forward_kernel,
        out_shape=(
            jax.ShapeDtypeStruct((width + 16, members), BF16),
            act,
            act,
            act,
            slope,
            slope,
            slope,
            jax.ShapeDtypeStruct((4, members), F32),
            jax.ShapeDtypeStruct((influence, 16, members), F32),
            jax.ShapeDtypeStruct((16, members), F32),
            jax.ShapeDtypeStruct((padded, members), BF16),
        ),
        in_specs=[VMEM] * 12,
        out_specs=(VMEM,) * 11,
        scratch_shapes=[
            pltpu.VMEM((16, width), F32),
            pltpu.VMEM((8, width), F32),
            pltpu.VMEM((16, -(-table_cols // 128) * 128), F32),
        ],
        compiler_params=params(16),
    )(feats, code, subj, bone_ids, skin, canon, table, w1, w2, w3, bias, head)


def block_pieces(width):
    piece = width // (2 * FAN)
    return piece, 3 * piece + SMALL


def split_blocks(side, quarter, total_s, mine_out, theirs_out, factor):
    width = mine_out.shape[2]
    piece, rows = block_pieces(width)
    for core, out in ((side, mine_out), (1 - side, theirs_out)):
        for slot in range(FAN):
            place = core * FAN + lax.bitwise_xor(quarter, slot)
            for square in range(3):
                spot = pl.ds(pl.multiple_of(square * width + place * piece, 16), piece)
                out[slot, square * piece : (square + 1) * piece, :] = (total_s[spot, :] * factor).astype(BF16)
            spot = pl.ds(pl.multiple_of(3 * width + place * SMALL, SMALL), SMALL)
            out[slot, 3 * piece : rows, :] = (total_s[spot, :] * factor).astype(BF16)


def lane_sums(value):
    total = value[:, 0:128]
    for lane in range(128, value.shape[1], 128):
        total = total + value[:, lane : lane + 128]
    return jnp.sum(total.T, axis=0, keepdims=True)


def backward_kernel(factor, subjects, per_subject, got, *refs):
    (side_ref, quarter_ref, pos_ref), refs = refs[:3], refs[3:]
    got_refs, refs = refs[:got], refs[got:]
    (
        point_ref,
        blend_ref,
        bone_ref,
        subj_ref,
        inputs_ref,
        act_one_ref,
        act_two_ref,
        act_three_ref,
        slope_one_ref,
        slope_two_ref,
        slope_three_ref,
        first_ref,
        second_ref,
        third_ref,
        head_ref,
        outer_out,
        back_out,
        mine_out,
        theirs_out,
        total_s,
        head_s,
        masked_s,
    ) = refs
    width, members = act_one_ref.shape
    small = 3 * width

    head_s[...] = jnp.zeros_like(head_s)
    head_s[0:3, :] = head_ref[...].astype(F32)
    head_w = head_s[...].astype(BF16)
    total_s[small:, :] = jnp.zeros((total_s.shape[0] - small, width), F32)
    grad = pos_ref[0].astype(F32)
    for ref in got_refs:
        grad = grad + ref[...].astype(F32)
    rows = lax.broadcasted_iota(jnp.int32, (16, members), 0)
    quarter = lax.shift_right_logical(rows, 2)
    place = lax.bitwise_and(rows, 3)
    grad_rows = jnp.where(
        quarter == 0,
        grad[0:1],
        jnp.where(quarter == 1, grad[1:2], jnp.where(quarter == 2, grad[2:3], 0.0)),
    )
    point = point_ref[...]
    point_rows = jnp.where(
        place == 0, point[0:1], jnp.where(place == 1, point[1:2], jnp.where(place == 2, point[2:3], point[3:4]))
    )
    outer = grad_rows * point_rows
    outer_out[...] = outer
    pulled = blend_ref[...] * grad_rows
    shift = pulled[0:4] + pulled[4:8] + pulled[8:12]
    shift = jnp.where(rows[0:4] < 3, shift, 0.0)
    shift = jnp.concatenate([shift, jnp.zeros((12, members), F32)], axis=0).astype(BF16)

    outer = outer.astype(BF16)
    subject = jnp.broadcast_to(subj_ref[...].astype(F32).astype(BF16), (16, members))
    zero = jnp.zeros((), BF16)
    for s in range(subjects):
        masked_s[16 * s : 16 * s + 16, :] = jnp.where(subject == jnp.asarray(s, BF16), outer, zero)
    product = mm(masked_s[...], bone_ref[...], NT)
    for s in range(subjects):
        columns = slice(s * per_subject, (s + 1) * per_subject)
        total_s[small + 8 : small + 24, columns] = product[16 * s : 16 * s + 16, 0:per_subject]

    half = jnp.asarray(0.5, BF16)
    back = mm(head_w * half, shift, TN) * slope_three_ref[...]
    total_s[small + 5 : small + 6, :] = lane_sums(back)
    back = back.astype(BF16)
    total_s[0:width, :] = mm(back, act_two_ref[...], NT)
    total_s[small : small + 3, :] = mm(shift, act_three_ref[...], NT)[0:3]
    back = mm(third_ref[...] * half, back, TN) * slope_two_ref[...]
    total_s[small + 4 : small + 5, :] = lane_sums(back)
    back = back.astype(BF16)
    total_s[width : 2 * width, :] = mm(back, act_one_ref[...], NT)
    back = (mm(second_ref[...] * half, back, TN) * slope_one_ref[...]).astype(BF16)
    back_out[...] = back
    product = mm(inputs_ref[...], back, NT)
    total_s[2 * width : 3 * width, :] = product[0:width].T
    by_subject = product[width : width + subjects]
    total_s[small + 3 : small + 4, :] = jnp.sum(by_subject, axis=0, keepdims=True)
    by_hi, by_rest = two_parts(by_subject)
    by_mid, by_lo = two_parts(by_rest)
    by_parts = jnp.concatenate([by_hi.astype(F32), by_mid.astype(F32), by_lo], axis=0).astype(BF16)
    code = mm(by_parts, first_ref[...])
    total_s[small + 24 : small + 24 + subjects, :] = (
        code[0:subjects] + code[subjects : 2 * subjects] + code[2 * subjects : 3 * subjects]
    )

    split_blocks(side_ref[0], quarter_ref[0], total_s, mine_out, theirs_out, factor)


def backward(side, quarter, pos, got, forwarded, subj, weights, head, factor, subjects, per_subject):
    inputs, act_one, act_two, act_three, *slopes, point, _, blend, bone = forwarded
    width, members = act_one.shape
    piece, rows = block_pieces(width)
    part = jax.ShapeDtypeStruct((FAN, rows, width), BF16)
    return pl.pallas_call(
        functools.partial(backward_kernel, factor, subjects, per_subject, len(got)),
        out_shape=(
            jax.ShapeDtypeStruct((16, members), F32),
            jax.ShapeDtypeStruct((width, members), BF16),
            part,
            part,
        ),
        in_specs=[SMEM] * 2 + [VMEM] * (16 + len(got)),
        out_specs=(VMEM,) * 4,
        scratch_shapes=[
            pltpu.VMEM((3 * width + 2 * FAN * SMALL, width), F32),
            pltpu.VMEM((16, width), F32),
            pltpu.VMEM((16 * subjects, members), BF16),
        ],
        compiler_params=params(24),
    )(
        side,
        quarter,
        pos,
        *got,
        point,
        blend,
        bone,
        subj,
        inputs,
        act_one,
        act_two,
        act_three,
        *slopes,
        *weights,
        head,
    )


def gaussian_kernel(back_ref, first_ref, outer_ref, matrix_ref, feat_out, skin_out):
    feat_out[...] = mm(first_ref[...], back_ref[...], TN).astype(BF16)
    outer = outer_ref[...]
    for member in range(matrix_ref.shape[0]):
        skin_out[member] = jnp.sum(outer * matrix_ref[member], axis=0, keepdims=True)


def gaussian_grads(back, w1, outer, matrix):
    width, members = back.shape
    influence = matrix.shape[0]
    return pl.pallas_call(
        gaussian_kernel,
        out_shape=(
            jax.ShapeDtypeStruct((width, members), BF16),
            jax.ShapeDtypeStruct((influence, 1, members), F32),
        ),
        in_specs=[VMEM] * 4,
        out_specs=(VMEM,) * 2,
        compiler_params=params(16),
    )(back, w1, outer, matrix)


def finish_kernel(side_ref, quarter_ref, *refs):
    mine_refs, refs = refs[:FAN], refs[FAN:]
    theirs_ref, *square_outs, bias_out, head_out, code_out, bone_out, small_s = refs
    piece, rows = block_pieces(theirs_ref.shape[2])
    for core in range(2):
        owner = side_ref[0] if core == 0 else 1 - side_ref[0]
        for slot in range(FAN):
            block = mine_refs[slot] if core == 0 else theirs_ref.at[slot]
            place = owner * FAN + lax.bitwise_xor(quarter_ref[0], slot)
            spot = pl.ds(pl.multiple_of(place * piece, piece), piece)
            for square, out in enumerate(square_outs):
                out[spot, :] = block[square * piece : (square + 1) * piece, :].astype(F32)
            spot = pl.ds(pl.multiple_of(place * SMALL, SMALL), SMALL)
            small_s[spot, :] = block[3 * piece : rows, :].astype(F32)
    small = small_s[...]
    head_out[...] = small[0:3]
    bias_out[...] = small[3:6]
    bone_out[...] = small[8:20, 0 : bone_out.shape[1]]
    code_out[...] = small[24 : 24 + code_out.shape[0]]


def finish(side, quarter, mine, theirs, subjects, table_cols):
    width = mine[0].shape[1]
    square = jax.ShapeDtypeStruct((width, width), F32)
    lines = jax.ShapeDtypeStruct((3, width), F32)
    third, second, first, *small = pl.pallas_call(
        finish_kernel,
        out_shape=(
            square,
            square,
            square,
            lines,
            lines,
            jax.ShapeDtypeStruct((subjects, width), F32),
            jax.ShapeDtypeStruct((12, table_cols), F32),
        ),
        in_specs=[SMEM] * 2 + [VMEM] * (FAN + 1),
        out_specs=(VMEM,) * 7,
        scratch_shapes=[pltpu.VMEM((2 * FAN * SMALL, width), F32)],
        compiler_params=params(16),
    )(side, quarter, *mine, theirs)
    return first, second, third, *small


def attr_kernel(groups, *refs):
    out_ref = refs[-1]
    count = (len(refs) - 1) // groups
    row = 0
    for start in range(0, groups * count, count):
        total = refs[start][0].astype(F32)
        for ref in refs[start + 1 : start + count]:
            total = total + ref[...].astype(F32)
        for place in range(min(total.shape[0], out_ref.shape[0] - row)):
            out_ref[row + place] = total[place : place + 1]
        row += total.shape[0]


def attr_sum(groups, attrs):
    members = groups[0][0].shape[2]
    operands = [value for group in groups for value in group]
    return pl.pallas_call(
        functools.partial(attr_kernel, len(groups)),
        out_shape=jax.ShapeDtypeStruct((attrs, 1, members), F32),
        in_specs=[VMEM] * len(operands),
        out_specs=VMEM,
        compiler_params=params(16),
    )(*operands)


def add(left, right):
    return (left.astype(F32) + right.astype(F32)).astype(BF16)


def swap(value, mask, count):
    return lax.ppermute(value, AXES, [(place, place ^ mask) for place in range(count)])


def tied(values, others):
    held = lax.optimization_barrier((tuple(values), tuple(others)))
    return list(held[0]), list(held[1])


def sum_over_devices(mine, theirs, viewers, shards, between):
    count = viewers * shards
    pair = shards
    rows, width = mine.shape[1:]
    masks = [1 << bit for bit in range(count.bit_length() - 1) if 1 << bit >= FAN and 1 << bit != pair]

    def work(stage, after, got):
        for item in between.get(stage, ()):
            got[0] = item(after, got[0])
        return got

    arrived = swap(theirs, pair, count)
    blocks = [add(mine[slot], arrived[slot]) for slot in range(FAN)]
    got = [swap(blocks[slot], slot, count) for slot in range(1, FAN)]
    got = work("scatter", blocks[0], got)
    total = sum((value.astype(F32) for value in got), blocks[0].astype(F32)).astype(BF16)
    for stage, mask in enumerate(masks):
        got = work(stage, total, [swap(total, mask, count)])
        total = add(total, got[0])
    got = [swap(total, slot, count) for slot in range(1, FAN)]
    got = work("gather", total, got)
    mine = [total, *got]
    theirs = swap(jnp.stack(mine), pair, count)
    return mine, theirs


class Work:
    def __init__(self, call, *operands):
        self.call = call
        self.operands = operands
        self.results = None

    def __call__(self, after, before):
        operands, _ = tied(self.operands, [after])
        results = self.call(*operands)
        self.results, held = tied(results, [before])
        return held[0]


def received(parts, viewers):
    got = []
    for away in range(1, viewers):
        perm = [(place, (place + away) % viewers) for place in range(viewers)]
        got.append(lax.ppermute(parts[away], "view", perm))
    return got


def body(
    entry_grads,
    vis_ids,
    feats,
    code_tab,
    subj_ids,
    bone_ids,
    skin_w,
    canon_pos,
    bone_tf,
    w_first,
    w_second,
    w_third,
    biases,
    w_head,
):
    members = feats.shape[2]
    viewers = lax.axis_size("view")
    shards = lax.axis_size("gauss")
    attrs = entry_grads.shape[1]
    subjects = code_tab.shape[1]
    table_cols = bone_tf.shape[1]
    factor = 1.0 / math.sqrt(members * viewers * shards)
    view = lax.axis_index("view").astype(jnp.int32).reshape(1)
    side = lax.bitwise_and(view, 1)
    quarter = lax.bitwise_and(lax.axis_index("gauss").astype(jnp.int32).reshape(1), FAN - 1)
    position, arrays = entry(
        view,
        (
            vis_ids,
            entry_grads,
            feats[:, 0],
            code_tab.T,
            subj_ids,
            bone_ids,
            skin_w,
            canon_pos,
            bone_tf,
            w_first,
            w_second,
            w_third,
            biases,
            w_head,
        ),
        members,
        viewers,
    )
    vis_ids, entry_grads, *arrays = arrays
    subj_ids, weights, w_head = arrays[2], arrays[7:10], arrays[11]
    position_got = received(position, viewers)
    forwarded = forward(*arrays)
    outer, back_one, mine, theirs = backward(
        side,
        quarter,
        position,
        position_got,
        forwarded,
        subj_ids,
        weights,
        w_head,
        factor,
        subjects,
        table_cols // subjects,
    )

    def scatter_rows(row):
        def call(grads, ids):
            return [scatter(view, grads, ids, row, min(BAND, attrs - row), members, viewers)]

        return Work(call, entry_grads, vis_ids)

    works = [scatter_rows(row) for row in range(0, attrs, BAND)]
    per_gaussian = Work(gaussian_grads, back_one, weights[0], outer, forwarded[8])

    def attributes(_):
        sums = [work.results[0] for work in works]
        return [attr_sum([[value, *received(value, viewers)] for value in sums], attrs)]

    last = Work(attributes, view)
    between = {"scatter": works[:1], 0: works[1:], 1: [per_gaussian], "gather": [last]}
    mine, theirs = sum_over_devices(mine, theirs, viewers, shards, between)
    attr = last.results[0]
    feat_grads, skin_grads = per_gaussian.results
    first, second, third, bias, head, code, bone = finish(side, quarter, mine, theirs, subjects, table_cols)
    return (
        attr,
        feat_grads[:, None, :],
        skin_grads,
        first,
        second,
        third,
        bias,
        head,
        code.T,
        bone,
    )


def solution(mesh):
    placed = (
        P("view", None, "gauss"),
        P("view", "gauss"),
        P(None, "gauss", "view"),
        P(),
        P("gauss", "view"),
        P(None, "gauss", "view"),
        P(None, "gauss", "view"),
        P(None, "gauss", "view"),
        P(),
        P(),
        P(),
        P(),
        P(),
        P(),
    )
    return jax.shard_map(
        body,
        mesh=mesh,
        in_specs=placed,
        out_specs=(
            P(None, "gauss", "view"),
            P(None, "gauss", "view"),
            P(None, "gauss", "view"),
            P(),
            P(),
            P(),
            P(),
            P(),
            P(),
            P(),
        ),
        check_vma=False,
    )
```

```python
import functools
import math

import jax
import jax.numpy as jnp
from jax import lax
from jax.experimental import pallas as pl
from jax.experimental.pallas import tpu as pltpu
from jax.sharding import PartitionSpec as P

F32 = jnp.float32
BF16 = jnp.bfloat16
AXES = ("view", "gauss")
LOW = 256
GROUP = 16
BAND = 32
SMALL = 8
FAN = 4
NT = (((1,), (1,)), ((), ()))
TN = (((0,), (0,)), ((), ()))
HBM = pl.BlockSpec(memory_space=pltpu.HBM)
VMEM = pl.BlockSpec(memory_space=pltpu.VMEM)
SMEM = pl.BlockSpec(memory_space=pltpu.SMEM)


def params(mebibytes):
    return pltpu.CompilerParams(vmem_limit_bytes=mebibytes * 1024 * 1024)


def mm(left, right, dims=(((1,), (0,)), ((), ()))):
    return lax.dot_general(left, right, dims, preferred_element_type=F32)


def divisor(total, choices):
    for choice in choices:
        if total % choice == 0:
            return choice
    return total


def entry_step(entries, rows):
    fitting = [step for step in (2560, 1280, 1024, 512, 256, 128) if rows * step * 2 <= 8 << 20]
    return divisor(entries, fitting)


def scatter_kernel(first_row, rows, viewers, view_ref, grads_ref, ids_ref, out_ref, acc_ref, left_ref):
    entries = ids_ref.shape[1]
    step = left_ref.shape[1]
    height = out_ref.shape[1]
    blocks = acc_ref.shape[0] // height
    groups = height // GROUP
    low_rows = lax.broadcasted_iota(jnp.int32, (LOW, step), 0).astype(F32).astype(BF16)
    one = jnp.ones((), BF16)
    zero = jnp.zeros((), BF16)

    def chunk(index, carry):
        spot = pl.ds(pl.multiple_of(index * step, step), step)
        ids = ids_ref[0:1, spot]
        high = lax.shift_right_logical(ids, 8).astype(F32).astype(BF16)
        low = lax.bitwise_and(ids, LOW - 1).astype(F32).astype(BF16)
        hot = jnp.where(low_rows == low, one, zero)
        high = jnp.broadcast_to(high, (GROUP, step))
        for group in range(groups):
            begin = first_row + group * GROUP
            count = min(GROUP, first_row + rows - begin)
            piece = grads_ref[0, begin : begin + count, spot]
            if count < GROUP:
                piece = jnp.concatenate(
                    [piece.astype(F32), jnp.zeros((GROUP - count, step), F32)], axis=0
                ).astype(BF16)
            for block in range(blocks):
                place = block * height + group * GROUP
                left_ref[place : place + GROUP, :] = jnp.where(high == jnp.asarray(block, BF16), piece, zero)
        product = mm(left_ref[...], hot, NT)

        @pl.when(index == 0)
        def _():
            acc_ref[...] = product

        @pl.when(index != 0)
        def _():
            acc_ref[...] += product

        return carry

    lax.fori_loop(0, entries // step, chunk, 0)
    per = blocks // viewers
    for block in range(blocks):
        slot = lax.rem(block // per - view_ref[0] + viewers, viewers)
        out_ref[slot, :, (block % per) * LOW : (block % per + 1) * LOW] = acc_ref[
            block * height : (block + 1) * height, :
        ].astype(BF16)


def scatter(view, entry_grads, vis_ids, first_row, rows, members, viewers):
    height = -(-rows // GROUP) * GROUP
    blocks = members * viewers // LOW
    step = entry_step(vis_ids.shape[1], blocks * height)
    return pl.pallas_call(
        functools.partial(scatter_kernel, first_row, rows, viewers),
        out_shape=jax.ShapeDtypeStruct((viewers, height, members), BF16),
        in_specs=[SMEM, VMEM, VMEM],
        out_specs=VMEM,
        scratch_shapes=[pltpu.VMEM((blocks * height, LOW), F32), pltpu.VMEM((blocks * height, step), BF16)],
        compiler_params=params(16),
    )(view, entry_grads, vis_ids)


def position_kernel(viewers, view_ref, grads_ref, ids_ref, out_ref, acc_ref, left_ref, rows_ref):
    entries = ids_ref.shape[1]
    step = left_ref.shape[1]
    height = left_ref.shape[0] // 3
    blocks = out_ref.shape[2] * viewers // 128
    per = blocks // viewers
    high_rows = lax.broadcasted_iota(jnp.int32, (height, step), 0).astype(F32).astype(BF16)
    low_rows = lax.broadcasted_iota(jnp.int32, (128, step), 0).astype(F32).astype(BF16)
    one = jnp.ones((), BF16)
    zero = jnp.zeros((), BF16)

    def chunk(index, carry):
        spot = pl.ds(pl.multiple_of(index * step, step), step)
        ids = ids_ref[0:1, spot]
        high = lax.shift_right_logical(ids, 7).astype(F32).astype(BF16)
        low = lax.bitwise_and(ids, 127).astype(F32).astype(BF16)
        hot = jnp.where(low_rows == low, one, zero)
        inside = high_rows == high
        values = grads_ref[0, :, spot].astype(F32)
        for axis in range(3):
            value = jnp.broadcast_to(values[axis : axis + 1], (height, step)).astype(BF16)
            left_ref[axis * height : (axis + 1) * height, :] = jnp.where(inside, value, zero)
        product = mm(left_ref[...], hot, NT)

        @pl.when(index == 0)
        def _():
            acc_ref[...] = product

        @pl.when(index != 0)
        def _():
            acc_ref[...] += product

        return carry

    lax.fori_loop(0, entries // step, chunk, 0)
    rows_ref[...] = jnp.zeros_like(rows_ref)
    for block in range(blocks):
        slot = lax.rem(block // per - view_ref[0] + viewers, viewers)
        lanes = slice(block % per * 128, (block % per + 1) * 128)
        for axis in range(3):
            place = axis * height + block
            rows_ref[slot, axis : axis + 1, lanes] = acc_ref[place : place + 1, :]
    out_ref[...] = rows_ref[...].astype(BF16)


def entry_kernel(viewers, count, view_ref, *refs):
    sources, out_ref, targets = refs[:count], refs[count], refs[count + 1 : 2 * count + 1]
    acc_ref, left_ref, rows_ref, grads_ref, sems = refs[2 * count + 1 :]
    copies = [
        pltpu.make_async_copy(source, target, sems.at[index])
        for index, (source, target) in enumerate(zip(sources, targets))
    ]
    early = pltpu.make_async_copy(sources[1].at[:, 0:GROUP, :], grads_ref, sems.at[count])
    copies[0].start()
    early.start()
    for copy in copies[1:]:
        copy.start()
    copies[0].wait()
    early.wait()
    position_kernel(viewers, view_ref, grads_ref, targets[0], out_ref, acc_ref, left_ref, rows_ref)
    for copy in copies[1:]:
        copy.wait()


def entry(view, arrays, members, viewers):
    height = -(-(members * viewers // 128) // 16) * 16
    step = entry_step(arrays[0].shape[1], 3 * height)
    count = len(arrays)
    results = pl.pallas_call(
        functools.partial(entry_kernel, viewers, count),
        out_shape=(
            jax.ShapeDtypeStruct((viewers, GROUP, members), BF16),
            *(jax.ShapeDtypeStruct(value.shape, value.dtype) for value in arrays),
        ),
        in_specs=[SMEM] + [HBM] * count,
        out_specs=(VMEM,) * (count + 1),
        scratch_shapes=[
            pltpu.VMEM((3 * height, 128), F32),
            pltpu.VMEM((3 * height, step), BF16),
            pltpu.VMEM((viewers, GROUP, members), F32),
            pltpu.VMEM((1, GROUP, arrays[0].shape[1]), BF16),
            pltpu.SemaphoreType.DMA((count + 1,)),
        ],
        compiler_params=params(16),
    )(view, *(pltpu.with_memory_space_constraint(value, pltpu.HBM) for value in arrays))
    return results[0], results[1:]


def two_parts(value):
    top = value.astype(BF16)
    return top, value - top.astype(F32)


def forward_kernel(
    feats_ref,
    code_ref,
    subj_ref,
    bone_ids_ref,
    skin_ref,
    canon_ref,
    table_ref,
    first_ref,
    second_ref,
    third_ref,
    bias_ref,
    head_ref,
    inputs_out,
    act_one_out,
    act_two_out,
    act_three_out,
    slope_one_out,
    slope_two_out,
    slope_three_out,
    point_out,
    matrix_out,
    blend_out,
    bone_out,
    head_s,
    bias_s,
    table_s,
):
    width, members = feats_ref.shape
    subjects = code_ref.shape[0]
    table_cols = table_ref.shape[1]
    per_subject = table_cols // subjects
    influence = bone_ids_ref.shape[0]
    padded = bone_out.shape[0]
    pieces = table_s.shape[1] // 128

    head_s[...] = jnp.zeros_like(head_s)
    head_s[0:3, :] = head_ref[...].astype(F32)
    head_w = head_s[...].astype(BF16)
    bias_s[...] = jnp.zeros_like(bias_s)
    bias_s[0:3, :] = bias_ref[...]
    bias_cols = bias_s[...].T
    table_s[...] = jnp.zeros_like(table_s)
    table_s[0:12, 0:table_cols] = table_ref[...]
    code = code_ref[...]
    code_hi, code_rest = two_parts(code)
    code_mid, code_lo = two_parts(code_rest)
    code_w = jnp.concatenate([code_hi.astype(F32), code_mid.astype(F32), code_lo], axis=0).T.astype(BF16)

    subject = subj_ref[0:1, :]
    hot_rows = lax.broadcasted_iota(jnp.int32, (3 * subjects, members), 0) % subjects
    hot = (hot_rows == subject).astype(F32).astype(BF16)
    x = (feats_ref[...].astype(F32) + mm(code_w, hot)).astype(BF16)
    inputs_out[0:width, :] = x
    inputs_out[width : width + 16, :] = hot[0:16]
    layers = (
        (first_ref, act_one_out, slope_one_out),
        (second_ref, act_two_out, slope_two_out),
        (third_ref, act_three_out, slope_three_out),
    )
    half = jnp.asarray(0.5, BF16)
    source = inputs_out
    for layer, (weight, act_out, slope_out) in enumerate(layers):
        halved = weight[...] * half
        bias = 0.5 * bias_cols[:, layer : layer + 1]
        for lane in range(0, members, LOW):
            tile = slice(lane, lane + LOW)
            pre = mm(halved, source[0:width, tile]) + bias
            turn = jnp.tanh(pre)
            more = 1.0 + turn
            value = pre * more
            act_out[:, tile] = value.astype(BF16)
            slope_out[:, tile] = more + value * (1.0 - turn)
        source = act_out
    act = act_three_out[...]
    moved = mm(head_w, act)
    for axis in range(3):
        point_out[axis : axis + 1, :] = canon_ref[axis] + moved[axis : axis + 1]
    point_out[3:4, :] = jnp.ones((1, members), F32)

    bone_rows = lax.broadcasted_iota(jnp.int32, (padded, members), 0)
    spread = jnp.zeros((padded, members), F32)
    for member in range(influence):
        chosen = bone_ids_ref[member]
        spread = spread + jnp.where(bone_rows == chosen, skin_ref[member], 0.0)
    bone_out[...] = spread.astype(BF16)

    for tile in range(members // 128):
        lanes = slice(tile * 128, (tile + 1) * 128)
        base = subj_ref[0:1, lanes] * per_subject
        blend = [jnp.zeros((8, 128), F32), jnp.zeros((8, 128), F32)]
        for member in range(influence):
            column = jnp.broadcast_to(base + bone_ids_ref[member, :, lanes], (8, 128))
            within = lax.bitwise_and(column, 127)
            weight = skin_ref[member, :, lanes]
            for part in range(2):
                rows = slice(part * 8, part * 8 + 8)
                matrix = jnp.take_along_axis(table_s[rows, 0:128], within, axis=1, mode="promise_in_bounds")
                for piece in range(1, pieces):
                    other = jnp.take_along_axis(
                        table_s[rows, piece * 128 : (piece + 1) * 128], within, axis=1, mode="promise_in_bounds"
                    )
                    matrix = jnp.where(column >= piece * 128, other, matrix)
                matrix_out[member, rows, lanes] = matrix
                blend[part] = blend[part] + weight * matrix
        blend_out[0:8, lanes] = blend[0]
        blend_out[8:16, lanes] = blend[1]


def forward(feats, code, subj, bone_ids, skin, canon, table, w1, w2, w3, bias, head):
    width, members = feats.shape
    influence = bone_ids.shape[0]
    subjects = code.shape[0]
    table_cols = table.shape[1]
    padded = -(-(table_cols // subjects) // 16) * 16
    act = jax.ShapeDtypeStruct((width, members), BF16)
    slope = jax.ShapeDtypeStruct((width, members), F32)
    return pl.pallas_call(
        forward_kernel,
        out_shape=(
            jax.ShapeDtypeStruct((width + 16, members), BF16),
            act,
            act,
            act,
            slope,
            slope,
            slope,
            jax.ShapeDtypeStruct((4, members), F32),
            jax.ShapeDtypeStruct((influence, 16, members), F32),
            jax.ShapeDtypeStruct((16, members), F32),
            jax.ShapeDtypeStruct((padded, members), BF16),
        ),
        in_specs=[VMEM] * 12,
        out_specs=(VMEM,) * 11,
        scratch_shapes=[
            pltpu.VMEM((16, width), F32),
            pltpu.VMEM((8, width), F32),
            pltpu.VMEM((16, -(-table_cols // 128) * 128), F32),
        ],
        compiler_params=params(16),
    )(feats, code, subj, bone_ids, skin, canon, table, w1, w2, w3, bias, head)


def block_pieces(width):
    piece = width // (2 * FAN)
    return piece, 3 * piece + SMALL


def split_blocks(side, quarter, total_s, mine_out, theirs_out, factor):
    width = mine_out.shape[2]
    piece, rows = block_pieces(width)
    for core, out in ((side, mine_out), (1 - side, theirs_out)):
        for slot in range(FAN):
            place = core * FAN + lax.bitwise_xor(quarter, slot)
            for square in range(3):
                spot = pl.ds(pl.multiple_of(square * width + place * piece, 16), piece)
                out[slot, square * piece : (square + 1) * piece, :] = (total_s[spot, :] * factor).astype(BF16)
            spot = pl.ds(pl.multiple_of(3 * width + place * SMALL, SMALL), SMALL)
            out[slot, 3 * piece : rows, :] = (total_s[spot, :] * factor).astype(BF16)


def lane_sums(value):
    total = value[:, 0:128]
    for lane in range(128, value.shape[1], 128):
        total = total + value[:, lane : lane + 128]
    return jnp.sum(total.T, axis=0, keepdims=True)


def backward_kernel(factor, subjects, per_subject, got, *refs):
    (side_ref, quarter_ref, pos_ref), refs = refs[:3], refs[3:]
    got_refs, refs = refs[:got], refs[got:]
    (
        point_ref,
        blend_ref,
        bone_ref,
        subj_ref,
        inputs_ref,
        act_one_ref,
        act_two_ref,
        act_three_ref,
        slope_one_ref,
        slope_two_ref,
        slope_three_ref,
        first_ref,
        second_ref,
        third_ref,
        head_ref,
        outer_out,
        back_out,
        mine_out,
        theirs_out,
        total_s,
        head_s,
        masked_s,
    ) = refs
    width, members = act_one_ref.shape
    small = 3 * width

    head_s[...] = jnp.zeros_like(head_s)
    head_s[0:3, :] = head_ref[...].astype(F32)
    head_w = head_s[...].astype(BF16)
    total_s[small:, :] = jnp.zeros((total_s.shape[0] - small, width), F32)
    grad = pos_ref[0].astype(F32)
    for ref in got_refs:
        grad = grad + ref[...].astype(F32)
    rows = lax.broadcasted_iota(jnp.int32, (16, members), 0)
    quarter = rows // 4
    place = rows % 4
    grad_rows = jnp.where(
        quarter == 0,
        grad[0:1],
        jnp.where(quarter == 1, grad[1:2], jnp.where(quarter == 2, grad[2:3], 0.0)),
    )
    point = point_ref[...]
    point_rows = jnp.where(
        place == 0, point[0:1], jnp.where(place == 1, point[1:2], jnp.where(place == 2, point[2:3], point[3:4]))
    )
    outer = grad_rows * point_rows
    outer_out[...] = outer
    pulled = blend_ref[...] * grad_rows
    shift = pulled[0:4] + pulled[4:8] + pulled[8:12]
    shift = jnp.where(rows[0:4] < 3, shift, 0.0)
    shift = jnp.concatenate([shift, jnp.zeros((12, members), F32)], axis=0).astype(BF16)

    outer = outer.astype(BF16)
    subject = jnp.broadcast_to(subj_ref[...].astype(F32).astype(BF16), (16, members))
    zero = jnp.zeros((), BF16)
    for s in range(subjects):
        masked_s[16 * s : 16 * s + 16, :] = jnp.where(subject == jnp.asarray(s, BF16), outer, zero)
    product = mm(masked_s[...], bone_ref[...], NT)
    for s in range(subjects):
        columns = slice(s * per_subject, (s + 1) * per_subject)
        total_s[small + 8 : small + 24, columns] = product[16 * s : 16 * s + 16, 0:per_subject]

    half = jnp.asarray(0.5, BF16)
    back = mm(head_w * half, shift, TN) * slope_three_ref[...]
    total_s[small + 5 : small + 6, :] = lane_sums(back)
    back = back.astype(BF16)
    total_s[0:width, :] = mm(back, act_two_ref[...], NT)
    total_s[small : small + 3, :] = mm(shift, act_three_ref[...], NT)[0:3]
    back = mm(third_ref[...] * half, back, TN) * slope_two_ref[...]
    total_s[small + 4 : small + 5, :] = lane_sums(back)
    back = back.astype(BF16)
    total_s[width : 2 * width, :] = mm(back, act_one_ref[...], NT)
    back = (mm(second_ref[...] * half, back, TN) * slope_one_ref[...]).astype(BF16)
    back_out[...] = back
    product = mm(inputs_ref[...], back, NT)
    total_s[2 * width : 3 * width, :] = product[0:width].T
    by_subject = product[width : width + subjects]
    total_s[small + 3 : small + 4, :] = jnp.sum(by_subject, axis=0, keepdims=True)
    by_hi, by_rest = two_parts(by_subject)
    by_mid, by_lo = two_parts(by_rest)
    by_parts = jnp.concatenate([by_hi.astype(F32), by_mid.astype(F32), by_lo], axis=0).astype(BF16)
    code = mm(by_parts, first_ref[...])
    total_s[small + 24 : small + 24 + subjects, :] = (
        code[0:subjects] + code[subjects : 2 * subjects] + code[2 * subjects : 3 * subjects]
    )

    split_blocks(side_ref[0], quarter_ref[0], total_s, mine_out, theirs_out, factor)


def backward(side, quarter, pos, got, forwarded, subj, weights, head, factor, subjects, per_subject):
    inputs, act_one, act_two, act_three, *slopes, point, _, blend, bone = forwarded
    width, members = act_one.shape
    piece, rows = block_pieces(width)
    part = jax.ShapeDtypeStruct((FAN, rows, width), BF16)
    return pl.pallas_call(
        functools.partial(backward_kernel, factor, subjects, per_subject, len(got)),
        out_shape=(
            jax.ShapeDtypeStruct((16, members), F32),
            jax.ShapeDtypeStruct((width, members), BF16),
            part,
            part,
        ),
        in_specs=[SMEM] * 2 + [VMEM] * (16 + len(got)),
        out_specs=(VMEM,) * 4,
        scratch_shapes=[
            pltpu.VMEM((3 * width + 2 * FAN * SMALL, width), F32),
            pltpu.VMEM((16, width), F32),
            pltpu.VMEM((16 * subjects, members), BF16),
        ],
        compiler_params=params(24),
    )(
        side,
        quarter,
        pos,
        *got,
        point,
        blend,
        bone,
        subj,
        inputs,
        act_one,
        act_two,
        act_three,
        *slopes,
        *weights,
        head,
    )


def gaussian_kernel(back_ref, first_ref, outer_ref, matrix_ref, feat_out, skin_out):
    feat_out[...] = mm(first_ref[...], back_ref[...], TN).astype(BF16)
    outer = outer_ref[...]
    for member in range(matrix_ref.shape[0]):
        skin_out[member] = jnp.sum(outer * matrix_ref[member], axis=0, keepdims=True)


def gaussian_grads(back, w1, outer, matrix):
    width, members = back.shape
    influence = matrix.shape[0]
    return pl.pallas_call(
        gaussian_kernel,
        out_shape=(
            jax.ShapeDtypeStruct((width, members), BF16),
            jax.ShapeDtypeStruct((influence, 1, members), F32),
        ),
        in_specs=[VMEM] * 4,
        out_specs=(VMEM,) * 2,
        compiler_params=params(16),
    )(back, w1, outer, matrix)


def finish_kernel(side_ref, quarter_ref, *refs):
    mine_refs, refs = refs[:FAN], refs[FAN:]
    theirs_ref, *square_outs, bias_out, head_out, code_out, bone_out, small_s = refs
    piece, rows = block_pieces(theirs_ref.shape[1])
    for core in range(2):
        owner = side_ref[0] if core == 0 else 1 - side_ref[0]
        for slot in range(FAN):
            block = mine_refs[slot] if core == 0 else theirs_ref.at[slot * rows : (slot + 1) * rows]
            place = owner * FAN + lax.bitwise_xor(quarter_ref[0], slot)
            spot = pl.ds(pl.multiple_of(place * piece, piece), piece)
            for square, out in enumerate(square_outs):
                out[spot, :] = block[square * piece : (square + 1) * piece, :].astype(F32)
            spot = pl.ds(pl.multiple_of(place * SMALL, SMALL), SMALL)
            small_s[spot, :] = block[3 * piece : rows, :].astype(F32)
    small = small_s[...]
    head_out[...] = small[0:3]
    bias_out[...] = small[3:6]
    bone_out[...] = small[8:20, 0 : bone_out.shape[1]]
    code_out[...] = small[24 : 24 + code_out.shape[0]]


def finish(side, quarter, mine, theirs, subjects, table_cols):
    width = mine[0].shape[1]
    square = jax.ShapeDtypeStruct((width, width), F32)
    lines = jax.ShapeDtypeStruct((3, width), F32)
    third, second, first, *small = pl.pallas_call(
        finish_kernel,
        out_shape=(
            square,
            square,
            square,
            lines,
            lines,
            jax.ShapeDtypeStruct((subjects, width), F32),
            jax.ShapeDtypeStruct((12, table_cols), F32),
        ),
        in_specs=[SMEM] * 2 + [VMEM] * (FAN + 1),
        out_specs=(VMEM,) * 7,
        scratch_shapes=[pltpu.VMEM((2 * FAN * SMALL, width), F32)],
        compiler_params=params(16),
    )(side, quarter, *mine, theirs)
    return first, second, third, *small


def attr_kernel(groups, *refs):
    out_ref = refs[-1]
    count = (len(refs) - 1) // groups
    row = 0
    for start in range(0, groups * count, count):
        total = refs[start][0].astype(F32)
        for ref in refs[start + 1 : start + count]:
            total = total + ref[...].astype(F32)
        for place in range(min(total.shape[0], out_ref.shape[0] - row)):
            out_ref[row + place] = total[place : place + 1]
        row += total.shape[0]


def attr_sum(groups, attrs):
    members = groups[0][0].shape[2]
    operands = [value for group in groups for value in group]
    return pl.pallas_call(
        functools.partial(attr_kernel, len(groups)),
        out_shape=jax.ShapeDtypeStruct((attrs, 1, members), F32),
        in_specs=[VMEM] * len(operands),
        out_specs=VMEM,
        compiler_params=params(16),
    )(*operands)


def add(left, right):
    return (left.astype(F32) + right.astype(F32)).astype(BF16)


def swap(value, mask, count):
    return lax.ppermute(value, AXES, [(place, place ^ mask) for place in range(count)])


def tied(values, others):
    held = lax.optimization_barrier((tuple(values), tuple(others)))
    return list(held[0]), list(held[1])


def sum_over_devices(mine, theirs, viewers, shards, between):
    count = viewers * shards
    pair = shards
    rows, width = mine.shape[1:]
    masks = [1 << bit for bit in range(count.bit_length() - 1) if 1 << bit >= FAN and 1 << bit != pair]

    def work(stage, after, got):
        for item in between.get(stage, ()):
            got[0] = item(after, got[0])
        return got

    arrived = swap(theirs, pair, count)
    blocks = [add(mine[slot], arrived[slot]) for slot in range(FAN)]
    got = [swap(blocks[slot], slot, count) for slot in range(1, FAN)]
    got = work("scatter", blocks[0], got)
    total = sum((value.astype(F32) for value in got), blocks[0].astype(F32)).astype(BF16)
    for stage, mask in enumerate(masks):
        got = work(stage, total, [swap(total, mask, count)])
        total = add(total, got[0])
    got = [swap(total, slot, count) for slot in range(1, FAN)]
    got = work("gather", total, got)
    mine = [total, *got]
    theirs = swap(jnp.concatenate(mine, axis=0), pair, count)
    return mine, theirs


class Work:
    def __init__(self, call, *operands):
        self.call = call
        self.operands = operands
        self.results = None

    def __call__(self, after, before):
        operands, _ = tied(self.operands, [after])
        results = self.call(*operands)
        self.results, held = tied(results, [before])
        return held[0]


def received(parts, viewers):
    got = []
    for away in range(1, viewers):
        perm = [(place, (place + away) % viewers) for place in range(viewers)]
        got.append(lax.ppermute(parts[away], "view", perm))
    return got


def body(
    entry_grads,
    vis_ids,
    feats,
    code_tab,
    subj_ids,
    bone_ids,
    skin_w,
    canon_pos,
    bone_tf,
    w_first,
    w_second,
    w_third,
    biases,
    w_head,
):
    members = feats.shape[2]
    viewers = lax.axis_size("view")
    shards = lax.axis_size("gauss")
    attrs = entry_grads.shape[1]
    subjects = code_tab.shape[1]
    table_cols = bone_tf.shape[1]
    factor = 1.0 / math.sqrt(members * viewers * shards)
    view = lax.axis_index("view").astype(jnp.int32).reshape(1)
    side = lax.bitwise_and(view, 1)
    quarter = lax.bitwise_and(lax.axis_index("gauss").astype(jnp.int32).reshape(1), FAN - 1)
    position, arrays = entry(
        view,
        (
            vis_ids,
            entry_grads,
            feats[:, 0],
            code_tab.T,
            subj_ids,
            bone_ids,
            skin_w,
            canon_pos,
            bone_tf,
            w_first,
            w_second,
            w_third,
            biases,
            w_head,
        ),
        members,
        viewers,
    )
    vis_ids, entry_grads, *arrays = arrays
    subj_ids, weights, w_head = arrays[2], arrays[7:10], arrays[11]
    position_got = received(position, viewers)
    forwarded = forward(*arrays)
    outer, back_one, mine, theirs = backward(
        side,
        quarter,
        position,
        position_got,
        forwarded,
        subj_ids,
        weights,
        w_head,
        factor,
        subjects,
        table_cols // subjects,
    )

    def scatter_rows(row):
        def call(grads, ids):
            return [scatter(view, grads, ids, row, min(BAND, attrs - row), members, viewers)]

        return Work(call, entry_grads, vis_ids)

    works = [scatter_rows(row) for row in range(0, attrs, BAND)]
    per_gaussian = Work(gaussian_grads, back_one, weights[0], outer, forwarded[8])

    def attributes(_):
        sums = [work.results[0] for work in works]
        return [attr_sum([[value, *received(value, viewers)] for value in sums], attrs)]

    last = Work(attributes, view)
    between = {"scatter": [*works[:1], per_gaussian], 0: works[1:], 1: [last]}
    mine, theirs = sum_over_devices(mine, theirs, viewers, shards, between)
    attr = last.results[0]
    feat_grads, skin_grads = per_gaussian.results
    first, second, third, bias, head, code, bone = finish(side, quarter, mine, theirs, subjects, table_cols)
    return (
        attr,
        feat_grads[:, None, :],
        skin_grads,
        first,
        second,
        third,
        bias,
        head,
        code.T,
        bone,
    )


def solution(mesh):
    placed = (
        P("view", None, "gauss"),
        P("view", "gauss"),
        P(None, "gauss", "view"),
        P(),
        P("gauss", "view"),
        P(None, "gauss", "view"),
        P(None, "gauss", "view"),
        P(None, "gauss", "view"),
        P(),
        P(),
        P(),
        P(),
        P(),
        P(),
    )
    return jax.shard_map(
        body,
        mesh=mesh,
        in_specs=placed,
        out_specs=(
            P(None, "gauss", "view"),
            P(None, "gauss", "view"),
            P(None, "gauss", "view"),
            P(),
            P(),
            P(),
            P(),
            P(),
            P(),
            P(),
        ),
        check_vma=False,
    )
```
